32 devices in a mesh: wide: 8 (over z, y), narrow: 4 (over x, core).
Axes of the slice: x: 2, y: 2, z: 4, core: 2. Of those that a mesh axis runs over, the one named last changes fastest.
Arguments:
- inputs: bfloat16 [3, 8, 196, 1024], P(None, 'wide')
- image_sides: int32 [3, 8], P(None, 'wide'), may hold values from 5 to 7
- tile_cuts: int32 [3, 8, 2], P(None, 'wide'), may hold values from 2 to 4
- cotangent: bfloat16 [3, 8, 49, 2048], P(None, 'wide'), may hold values from -6 to 6
- w_reduce1: bfloat16 [1024, 512], replicated, may hold values from -0.1875 to 0.1875
- w_spatial1: bfloat16 [9, 512, 512], replicated, may hold values from -0.09375 to 0.09375
- w_expand1: bfloat16 [512, 2048], replicated, may hold values from -0.25 to 0.25
- w_project1: bfloat16 [1024, 2048], replicated, may hold values from -0.1875 to 0.1875
- w_reduce2: bfloat16 [2048, 512], replicated, may hold values from -0.125 to 0.125
- w_spatial2: bfloat16 [9, 512, 512], replicated, may hold values from -0.09375 to 0.09375
- w_expand2: bfloat16 [512, 2048], replicated, may hold values from -0.25 to 0.25
- norm_gains: float32 [8192], replicated, may hold values from 0.1 to 1.9
- norm_biases: float32 [8192], replicated, may hold values from -3 to 3
Outputs:
- block_output: bfloat16 [3, 8, 49, 2048], P(None, 'wide', None, 'narrow')
- input_gradient: bfloat16 [3, 8, 196, 1024], P(None, 'wide', None, 'narrow')
- grad_reduce1: float32 [1024, 512], P('wide', 'narrow')
- grad_spatial1: float32 [9, 512, 512], P(None, 'wide', 'narrow')
- grad_expand1: float32 [512, 2048], P('wide', 'narrow')
- grad_project1: float32 [1024, 2048], P('wide', 'narrow')
- grad_reduce2: float32 [2048, 512], P('wide', 'narrow')
- grad_spatial2: float32 [9, 512, 512], P(None, 'wide', 'narrow')
- grad_expand2: float32 [512, 2048], P('wide', 'narrow')
- grad_gains: float32 [8192], P(('wide', 'narrow'))
- grad_biases: float32 [8192], P(('wide', 'narrow'))
- rms_values: float32 [4], replicated
The draws below stay inside these ranges and needn't reach their ends.
Inputs may be any that keep to these rules, and one draw needn't show every extreme that they name: The valid cells of image k are the top left image_sides x image_sides cells of the output grid and the top left 2 * image_sides x 2 * image_sides cells of the input grid.
All inputs are finite; a program needn't handle non-finite values.
Results may differ from the reference program's by a relative error of at most 0.02.
Values may be sent and summed in bfloat16 or wider, within the bound.
A program may use at most 448 MiB of HBM per device.

```python
import math
import jax
import jax.numpy as jnp
from jax import lax

IN = 1024
MID = 512
OUT = 2048
HALF = 7
MICRO = 3
IMAGES = 8
ALLCH = 8192


def draw_inputs(key, part):
    key = jax.random.fold_in(key, 17)
    base_key, pixel_key, channel_key = jax.random.split(key, 3)
    array_shape = (MICRO, IMAGES, 4 * HALF * HALF, IN)
    position = jnp.arange(IMAGES, dtype=jnp.float32) / max(IMAGES - 1, 1)
    image_scale = jnp.exp(math.log(3.0) * position)[None, :, None, None]
    pixel_scale = jnp.exp(jax.random.uniform(pixel_key, (MICRO, IMAGES, 4 * HALF * HALF, 1), jnp.float32, 0.0, math.log(3.4)))
    channel_scale = jnp.exp(jax.random.uniform(channel_key, (1, 1, 1, IN), jnp.float32, 0.0, math.log(2.0)))
    base_values = jax.random.normal(base_key, array_shape, jnp.float32)
    return (base_values * image_scale * pixel_scale * channel_scale).astype(jnp.bfloat16)


def set_ends(values, rng, least, largest):
    spot = [jax.random.randint(jax.random.fold_in(rng, axis), (), 0, length) for axis, length in enumerate(values.shape)]
    main_axis = values.shape.index(max(values.shape))
    neighbour = spot[:main_axis] + [(spot[main_axis] + 1) % values.shape[main_axis]] + spot[main_axis + 1:]
    return values.at[tuple(spot)].set(least).at[tuple(neighbour)].set(largest)


def block_scale(rng, extent, shards, low, top_value):
    factor_of, own = 1.0, jax.random.fold_in(rng, 6)
    for dim, parts in shards:
        steps = jnp.exp(jax.random.uniform(jax.random.fold_in(own, dim), (parts,), jnp.float32, low / len(shards), top_value / len(shards)))
        factor_of = factor_of * jnp.repeat(steps, extent[dim] // parts).reshape([-1 if axis == dim else 1 for axis in range(len(extent))])
    return factor_of


def centred(rng, dims, deviation, most, cuts=(), kind=jnp.bfloat16):
    array = deviation * jax.random.normal(rng, dims, jnp.float32)
    if cuts:
        array = array * block_scale(rng, dims, cuts, -0.22, 0.18)
    return jnp.clip(array, -most, most).astype(kind)


def setup_inputs(seed: int = 0) -> dict:
    keys = jax.random.split(jax.random.key(seed), 14)
    return {
        "inputs": draw_inputs(jax.random.fold_in(keys[13], 71), 0),
        "image_sides": set_ends(jax.random.randint(keys[1], (MICRO, IMAGES), HALF - 2, HALF + 1), jax.random.fold_in(keys[1], 1), HALF - 2, HALF).astype(jnp.int32),
        "tile_cuts": set_ends(jax.random.randint(keys[2], (MICRO, IMAGES, 2), 2, HALF - 2), jax.random.fold_in(keys[2], 1), 2, (HALF - 2) - 1).astype(jnp.int32),
        "cotangent": centred(keys[3], (MICRO, IMAGES, HALF * HALF, OUT), 1.0, 6.0, ((1, 8),)),
        "w_reduce1": centred(keys[4], (IN, MID), IN ** -0.5, 0.1875),
        "w_spatial1": centred(keys[5], (9, MID, MID), (9 * MID) ** -0.5, 0.09375),
        "w_expand1": centred(keys[6], (MID, OUT), MID ** -0.5, 0.25),
        "w_project1": centred(keys[7], (IN, OUT), IN ** -0.5, 0.1875),
        "w_reduce2": centred(keys[8], (OUT, MID), OUT ** -0.5, 0.125),
        "w_spatial2": centred(keys[9], (9, MID, MID), (9 * MID) ** -0.5, 0.09375),
        "w_expand2": centred(keys[10], (MID, OUT), MID ** -0.5, 0.25),
        "norm_gains": jnp.clip(1.0 + 0.18 * jax.random.normal(keys[11], (ALLCH,), jnp.float32), 0.1, 1.9),
        "norm_biases": centred(keys[12], (ALLCH,), 0.5, 3.0, (), jnp.float32),
    }


EPSILON = 1e-05
TAP_STEPS = ((-1, -1), (-1, 0), (-1, 1), (0, -1), (0, 0), (0, 1), (1, -1), (1, 0), (1, 1))

@jax.custom_vjp
def low(v):
    return lax.optimization_barrier(v.astype(jnp.bfloat16)).astype(jnp.float32)

@jax.custom_vjp
def low_back(v):
    return v

def low_keep(v):
    return (low(v), None)

def low_pass(kept, grad):
    return (grad,)

def back_keep(v):
    return (v, None)

def back_low(kept, grad):
    return (low(grad),)
low.defvjp(low_keep, low_pass)
low_back.defvjp(back_keep, back_low)

def smooth(values):
    return jax.nn.gelu(values, approximate=True)

def product(left, right):
    return jnp.einsum('ipc,cd->ipd', left, right, precision=lax.Precision.HIGHEST)

def pixel_masks(side_list):
    full_side = 2 * HALF
    full_cells = jnp.arange(full_side * full_side, dtype=jnp.int32)[None, :]
    full_limit = 2 * side_list[:, None]
    full_valid = ((full_cells // full_side < full_limit) & (full_cells % full_side < full_limit)).astype(jnp.float32)[:, :, None]
    half_cells = jnp.arange(HALF * HALF, dtype=jnp.int32)[None, :]
    half_limit = side_list[:, None]
    half_valid = ((half_cells // HALF < half_limit) & (half_cells % HALF < half_limit)).astype(jnp.float32)[:, :, None]
    return (full_valid, half_valid)

def tile_weights(cut_list):
    position = jnp.arange(HALF, dtype=jnp.int32)[None, :]
    cut_row = cut_list[:, 0:1]
    cut_col = cut_list[:, 1:2]
    tap_masks = []
    for row_step, col_step in TAP_STEPS:
        row_same = (position + row_step >= cut_row) == (position >= cut_row)
        col_same = (position + col_step >= cut_col) == (position >= cut_col)
        tap_masks.append((row_same[:, :, None] & col_same[:, None, :]).reshape(-1, HALF * HALF))
    return jnp.stack(tap_masks, axis=-1).astype(jnp.float32)[..., None]

def strided_columns(feature_grid):
    images = feature_grid.shape[0]
    padded = jnp.pad(feature_grid, ((0, 0), (1, 1), (1, 1), (0, 0)))
    pieces = [padded[:, 1 + row_step:1 + row_step + 2 * HALF:2, 1 + col_step:1 + col_step + 2 * HALF:2, :] for row_step, col_step in TAP_STEPS]
    return jnp.concatenate(pieces, axis=-1).reshape(images, HALF * HALF, -1)

def tile_columns(feature_grid, tap_masks):
    images = feature_grid.shape[0]
    channels = feature_grid.shape[-1]
    padded = jnp.pad(feature_grid, ((0, 0), (1, 1), (1, 1), (0, 0)))
    pieces = [padded[:, 1 + row_step:1 + row_step + HALF, 1 + col_step:1 + col_step + HALF, :] for row_step, col_step in TAP_STEPS]
    stacked = jnp.stack(pieces, axis=3).reshape(images, HALF * HALF, 9, channels)
    return (stacked * tap_masks).reshape(images, HALF * HALF, 9 * channels)

def one_micro(params, inputs_now, sides_now, cuts_now):
    w_reduce1, w_spatial1, w_expand1, w_project1, w_reduce2, w_spatial2, w_expand2, norm_gains, norm_biases = params
    in_width = w_reduce1.shape[0]
    mid_width = w_reduce1.shape[1]
    out_width = w_expand1.shape[1]
    images = inputs_now.shape[0]
    full_valid, half_valid = pixel_masks(sides_now)
    tap_masks = tile_weights(cuts_now)

    def normalize(values, valid_mask, start, width):
        pixel_count = jnp.sum(valid_mask)
        channel_mean = lax.optimization_barrier(jnp.sum(values * valid_mask, axis=(0, 1))) / pixel_count
        variance = lax.optimization_barrier(jnp.sum(values * values * valid_mask, axis=(0, 1))) / pixel_count - channel_mean * channel_mean
        normed = (values - channel_mean) * lax.rsqrt(variance + EPSILON)
        return normed * norm_gains[start:start + width] + norm_biases[start:start + width]
    masked_inputs = inputs_now * full_valid
    first_reduced = low_back(product(masked_inputs, w_reduce1))
    first_active = low(smooth(normalize(first_reduced, full_valid, 0, mid_width)) * full_valid)
    first_columns = strided_columns(first_active.reshape(images, 2 * HALF, 2 * HALF, mid_width))
    first_spatial = low_back(product(first_columns, w_spatial1.reshape(9 * mid_width, mid_width)))
    first_mixed = low_back(low(smooth(normalize(first_spatial, half_valid, mid_width, mid_width)) * half_valid))
    first_expanded = low_back(product(first_mixed, w_expand1))
    picked = masked_inputs.reshape(images, 2 * HALF, 2 * HALF, in_width)[:, ::2, ::2, :].reshape(images, HALF * HALF, in_width)
    first_projected = low_back(product(picked, w_project1))
    normed_both = normalize(jnp.concatenate([first_expanded, first_projected], axis=-1), half_valid, 2 * mid_width, 2 * out_width)
    first_branch = normed_both[..., :out_width]
    first_output = smooth(first_branch + normed_both[..., out_width:]) * half_valid
    first_low = low(first_output)
    second_reduced = low_back(product(first_low, w_reduce2))
    second_active = low_back(low(smooth(normalize(second_reduced, half_valid, 2 * mid_width + 2 * out_width, mid_width)) * half_valid))
    second_columns = tile_columns(second_active.reshape(images, HALF, HALF, mid_width), tap_masks)
    second_spatial = low_back(product(second_columns, w_spatial2.reshape(9 * mid_width, mid_width)))
    second_mixed = low_back(low(smooth(normalize(second_spatial, half_valid, 3 * mid_width + 2 * out_width, mid_width)) * half_valid))
    second_expanded = low_back(product(second_mixed, w_expand2))
    second_branch = normalize(second_expanded, half_valid, 4 * mid_width + 2 * out_width, out_width)
    second_output = smooth(second_branch + low_back(first_low)) * half_valid
    square_sums = jnp.stack([jnp.sum(first_branch * first_branch * half_valid), jnp.sum(first_output * first_output), jnp.sum(second_branch * second_branch * half_valid), jnp.sum(second_output * second_output)])
    return (second_output, square_sums)

def forward(params, inputs_wide, image_sides, tile_cuts):

    def single(operands):
        return jax.checkpoint(one_micro)(params, operands[0], operands[1], operands[2])
    return lax.map(single, (inputs_wide, image_sides, tile_cuts))

def reference(inputs, image_sides, tile_cuts, cotangent, w_reduce1, w_spatial1, w_expand1, w_project1, w_reduce2, w_spatial2, w_expand2, norm_gains, norm_biases):
    weight_list = (w_reduce1, w_spatial1, w_expand1, w_project1, w_reduce2, w_spatial2, w_expand2)
    params = tuple((weight.astype(jnp.float32) for weight in weight_list)) + (norm_gains, norm_biases)
    inputs_wide = inputs.astype(jnp.float32)

    def primal(param_tuple, input_values):
        return forward(param_tuple, input_values, image_sides, tile_cuts)
    (outputs, square_sums), pullback = jax.vjp(primal, params, inputs_wide)
    param_grads, input_grads = pullback((cotangent.astype(jnp.float32), jnp.zeros_like(square_sums)))
    pixel_total = jnp.sum((image_sides * image_sides).astype(jnp.float32))
    rms_values = jnp.sqrt(lax.optimization_barrier(jnp.sum(square_sums, axis=0)) / (pixel_total * OUT))
    return (outputs.astype(jnp.bfloat16), input_grads.astype(jnp.bfloat16), param_grads[0], param_grads[1], param_grads[2], param_grads[3], param_grads[4], param_grads[5], param_grads[6], param_grads[7], param_grads[8], rms_values)
```

```python
import functools
import math
from types import SimpleNamespace

import jax
import jax.numpy as jnp
from jax import lax
from jax.experimental import pallas as pl
from jax.experimental.pallas import tpu as pltpu
from jax.sharding import PartitionSpec as P

MESH = pl.DeviceIdType.MESH
WIDE, NARROW = "wide", "narrow"
BF16 = jnp.bfloat16
F32 = jnp.float32
HALF = 7
FULL = 2 * HALF
EPSILON = 1e-05
C0 = math.sqrt(2.0 / math.pi)
C1 = C0 * 0.044715
HR = 64
FR = 208
TAPS = 9


def dot(a, b):
    return jnp.dot(a, b, preferred_element_type=F32)


def dot_nt(a, b):
    return lax.dot_general(a, b, (((1,), (1,)), ((), ())), preferred_element_type=F32)


def dot_tn(a, b):
    return lax.dot_general(a, b, (((0,), (0,)), ((), ())), preferred_element_type=F32)


def spread(mask, width):
    return jnp.concatenate([mask] * (width // 128), axis=1)


def gelu(v):
    t = jnp.tanh(v * (C0 + C1 * (v * v)))
    h = 0.5 * v
    return h + h * t


def gelu_slope(v):
    v2 = v * v
    t = jnp.tanh(v * (C0 + C1 * v2))
    return 0.5 + 0.5 * t + (0.5 * v) * (1.0 - t * t) * (C0 + (3.0 * C1) * v2)


def column_sum(values):
    return jnp.sum(values, axis=0, keepdims=True)


def half_cell(p):
    i = lax.shift_right_logical(p * 9363, 16)
    return i, p - HALF * i


def full_cell(p):
    i = lax.shift_right_logical(p * 4682, 16)
    return i, p - FULL * i


def tap_of(r):
    t = lax.shift_right_logical(r, 6)
    ta = lax.shift_right_logical(t * 11, 5)
    return ta - 1, t - 3 * ta - 1


def one_zero(condition):
    return jnp.where(condition, 1.0, 0.0)


def strided_pick(rows, cells):
    a, b = tap_of(rows)
    p = lax.bitwise_and(rows, 63)
    i, j = half_cell(p)
    r, c = 2 * i + a, 2 * j + b
    inside = (p < HALF * HALF) & (r >= 0) & (r < FULL) & (c >= 0) & (c < FULL)
    return one_zero(inside & (cells == r * FULL + c)).astype(BF16)


def tile_pick(rows, cells, cut_row, cut_col):
    a, b = tap_of(rows)
    p = lax.bitwise_and(rows, 63)
    i, j = half_cell(p)
    r, c = i + a, j + b
    inside = (p < HALF * HALF) & (r >= 0) & (r < HALF) & (c >= 0) & (c < HALF)
    row_far = one_zero(r >= cut_row) - one_zero(i >= cut_row)
    col_far = one_zero(c >= cut_col) - one_zero(j >= cut_col)
    same = (row_far == 0.0) & (col_far == 0.0)
    return one_zero(inside & same & (cells == r * HALF + c)).astype(BF16)


class Group:
    def __init__(self, sems):
        self.sems = sems
        self.used = 0
        self.items = []

    def sem(self):
        self.used += 1
        return self.sems.at[self.used - 1]

    def remote(self, src, dst, recv_sem, device, when=None):
        copy = pltpu.make_async_remote_copy(
            src_ref=src, dst_ref=dst, send_sem=self.sem(), recv_sem=recv_sem,
            device_id=device, device_id_type=MESH,
        )
        if when is None:
            copy.start()
        else:
            pl.when(when)(copy.start)
        self.items.append((copy, when))

    def finish(self):
        for copy, when in self.items:
            if when is None:
                copy.wait_send()
            else:
                pl.when(when)(copy.wait_send)


def wait_bytes(ref, sem):
    pltpu.make_async_copy(ref, ref, sem).wait()


def kernel(plan, *refs):
    r = SimpleNamespace(**dict(zip(plan.names, refs)))
    r.stat = [getattr(r, "stat%d" % step) for step in range(12)]
    wide, narrow, micros, slots = plan.wide, plan.narrow, plan.micros, plan.slots
    mid, out, inw, allch = plan.mid, plan.out, plan.inw, plan.allch
    pairs = wide // 2
    columns = narrow // 2
    starts, layers = plan.starts, plan.layers
    w = lax.axis_index(WIDE)
    n = lax.axis_index(NARROW)
    x = n // 2
    core = n % 2
    first_micro = x * slots
    fetch = r.fetch

    def micro_of(s):
        return lax.rem(first_micro + s, micros)

    barrier = pltpu.get_barrier_semaphore()

    @pl.loop(1, wide)
    def _(d):
        pl.semaphore_signal(
            barrier, inc=1, device_id=(lax.rem(w + d, wide), n), device_id_type=MESH
        )

    for d in range(1, narrow):
        pl.semaphore_signal(
            barrier, inc=1, device_id=(w, lax.rem(n + d, narrow)), device_id_type=MESH
        )

    def pass_barrier():
        pl.semaphore_wait(barrier, wide - 1 + narrow - 1)

    def build_picks():
        rows = lax.broadcasted_iota(jnp.int32, (TAPS * HR, FR), 0)
        cells = lax.broadcasted_iota(jnp.int32, (TAPS * HR, FR), 1)
        r.pick[...] = strided_pick(rows, cells)

    def build_pick_back():
        rows = lax.broadcasted_iota(jnp.int32, (FR, TAPS * HR), 1)
        cells = lax.broadcasted_iota(jnp.int32, (FR, TAPS * HR), 0)
        r.pick_back[...] = strided_pick(rows, cells)

    def build_tiles(slot, micro):
        rows = lax.broadcasted_iota(jnp.int32, (TAPS * HR, HR), 0)
        cells = lax.broadcasted_iota(jnp.int32, (TAPS * HR, HR), 1)
        r.tiles[slot] = tile_pick(
            rows, cells, r.tile_cuts[0, 0, micro], r.tile_cuts[0, 1, micro]
        )

    def full_mask(micro):
        row, col = full_cell(lax.broadcasted_iota(jnp.int32, (FR, 128), 0))
        limit = 2 * r.image_sides[0, micro]
        return one_zero((row < limit) & (col < limit))

    def half_mask(micro):
        row, col = half_cell(lax.broadcasted_iota(jnp.int32, (HR, 128), 0))
        limit = r.image_sides[0, micro]
        return one_zero((row < limit) & (col < limit))

    def fetch_image(slot, micro):
        return pltpu.make_async_copy(r.inputs.at[micro, 0], r.raw.at[slot], fetch.at[slot])

    def mask_image(slot, micro):
        mask = full_mask(micro)
        raw = jnp.concatenate(
            [r.raw[slot].astype(F32), jnp.zeros((FR - FULL * FULL, inw), F32)], axis=0
        )
        r.image[slot] = (raw * spread(mask, inw)).astype(BF16)

    def chain(*local):
        r.__dict__.update(zip(plan.chain_names, local))
        group = Group(r.chain_sends)
        weights = (
            (r.w_reduce1, r.k_reduce1), (r.w_spatial1, r.k_spatial1), (r.w_project1, r.k_project1),
            (r.w_expand1, r.k_expand1), (r.w_reduce2, r.k_reduce2), (r.w_spatial2, r.k_spatial2),
            (r.w_expand2, r.k_expand2),
        )

        def fetch_weight(index):
            return pltpu.make_async_copy(*weights[index], fetch.at[4 + index])

        fetch_image(0, micro_of(0)).start()
        fetch_weight(0).start()
        for s in range(1, slots):
            fetch_image(s, micro_of(s)).start()
        for index in range(1, 7):
            fetch_weight(index).start()

        def fetch_cotangent(s):
            return pltpu.make_async_copy(
                r.cotangent.at[micro_of(s), 0], r.cot_raw.at[s], fetch.at[11 + s]
            )

        for s in range(slots):
            fetch_cotangent(s).start()
            r.half[s] = half_mask(micro_of(s))
            r.full[s] = full_mask(micro_of(s))

        def send_stats(step):
            stat = r.stat[step]

            @pl.loop(0, wide)
            def _(d):
                p = lax.rem(wide - 1 - w + d, wide)

                @pl.when(p != w)
                def _():
                    pltpu.make_async_remote_copy(
                        src_ref=stat.at[w], dst_ref=stat.at[w],
                        send_sem=r.stat_send.at[step], recv_sem=r.stat_recv.at[step],
                        device_id=(p, n), device_id_type=MESH,
                    ).start()

        def wait_stats(step):
            stat = r.stat[step]
            wait_bytes(stat.at[pl.ds(0, wide - 1)], r.stat_recv.at[step])

        def total(step, row, begin=0, width=None):
            stat = r.stat[step]
            width = stat.shape[2] if width is None else width
            part = stat[0, row : row + 1, begin : begin + width]
            for j in range(1, wide):
                part = part + stat[j, row : row + 1, begin : begin + width]
            return part

        def put(step, row, value, begin=0):
            r.stat[step][w, row : row + 1, begin : begin + value.shape[1]] = value

        def put_pair(step, s, values, begin=0):
            put(step, 2 * s, column_sum(values), begin)
            put(step, 2 * s + 1, column_sum(values * values), begin)

        def inverse_count(s, layer):
            count = r.counts[s : s + 1, 0:1]
            return 1.0 / (count * (4.0 if layer == 0 else 1.0))

        def settle(s, layer, step, begin=0):
            start, width = layers[layer]
            inv_n = inverse_count(s, layer)
            mean = total(step, 2 * s, begin, width) * inv_n
            square = total(step, 2 * s + 1, begin, width) * inv_n
            inv = lax.rsqrt(square - mean * mean + EPSILON)
            scale = r.gains[:, start : start + width] * inv
            r.norms[2 * s : 2 * s + 1, start : start + width] = inv
            r.norms[2 * s + 1 : 2 * s + 2, start : start + width] = -mean * inv
            return scale, r.biases[:, start : start + width] - mean * scale

        def kept(s, layer):
            start, width = layers[layer]
            gain = r.gains[:, start : start + width]
            inv = r.norms[2 * s : 2 * s + 1, start : start + width]
            offset = r.norms[2 * s + 1 : 2 * s + 2, start : start + width]
            return inv, offset, gain * inv, r.biases[:, start : start + width] + gain * offset

        def normed(s, layer, z):
            inv, offset, _, _ = kept(s, layer)
            return z * inv + offset

        def activation(s, layer, z):
            _, _, scale, shift = kept(s, layer)
            return z * scale + shift

        def settle_back(s, layer, step, sum_row, gain_row, begin=0):
            start, width = layers[layer]
            sum_u = total(step, sum_row, begin, width)
            sum_g = total(step, gain_row, begin, width)
            live = jnp.where(first_micro + s < micros, 1.0, 0.0)
            for row, value in ((0, sum_g), (1, sum_u)):
                if s == 0:
                    r.norm_sums[row : row + 1, start : start + width] = value
                else:
                    r.norm_sums[row : row + 1, start : start + width] += live * value
            inv_n = inverse_count(s, layer)
            inv, offset, k0, _ = kept(s, layer)
            k2 = -k0 * (sum_g * inv_n)
            return k0, -k0 * (sum_u * inv_n) + k2 * offset, k2 * inv

        def live_row(s, row):
            if s == 0:
                return row
            return row * jnp.where(first_micro + s < micros, 1.0, 0.0)

        def fold_row(row):
            parts = [row[:, c : c + mid] for c in range(0, row.shape[1], mid)]
            return functools.reduce(lambda a, b: a + b, parts)

        def add_squares(s, index, values):
            row = live_row(s, fold_row(column_sum(values)))
            if s == 0:
                r.squares[index : index + 1, :] = row
            else:
                r.squares[index : index + 1, :] += row

        def share(src, dst, recv_sem, cut=None):
            for c in range(columns):
                amount = min(slots, micros - c * slots)
                if amount <= 0:
                    continue
                for h in range(columns):
                    part = src.at[0:amount]
                    if cut is not None:
                        part = src.at[0:amount, :, h * cut : (h + 1) * cut]
                    group.remote(
                        part, dst.at[c * slots : c * slots + amount], recv_sem,
                        (w, 2 * h), x == c,
                    )

        def rows2(ref):
            value = ref[...]
            return value.reshape(value.shape[0] * value.shape[1], value.shape[2])

        def set_rows(ref, value):
            ref[...] = value.reshape(ref.shape)

        def rows_of(value, s, count=HR):
            return value[s * count : (s + 1) * count]

        def gather_tiles(s, value, select):
            picked = dot(select, value).astype(BF16)
            for t in range(TAPS):
                r.cols[s * HR : (s + 1) * HR, t * mid : (t + 1) * mid] = picked[
                    t * HR : (t + 1) * HR
                ]

        def half_wide(s, width):
            return spread(r.half[s], width)

        for s in range(slots):
            fetch_image(s, micro_of(s)).wait()
            mask_image(s, micro_of(s))
        fetch_weight(0).wait()
        for s in range(slots):
            z = dot(r.image[s], r.k_reduce1[...])
            r.z0[s] = z
            put_pair(0, s, z)
            side = r.image_sides[0, micro_of(s)]
            area = jnp.full((1, mid), side * side, jnp.int32).astype(F32)
            put(0, 2 * slots + s, area)
        pass_barrier()
        send_stats(0)
        build_picks()
        for s in range(slots):
            build_tiles(s, micro_of(s))
        centre = r.pick[4 * HR : 5 * HR, :]
        for s in range(slots):
            r.picked[s * HR : (s + 1) * HR, :] = dot(centre, r.image[s]).astype(BF16)
        fetch_weight(2).wait()
        set_rows(r.z_short, dot(r.picked[...], r.k_project1[...]))
        for s in range(slots):
            put_pair(2, s, r.z_short[s], out)
        fetch_weight(1).wait()
        wait_stats(0)
        for s in range(slots):
            r.counts[s : s + 1, :] = total(0, 2 * slots + s, 0, 128)

        for s in range(slots):
            scale, shift = settle(s, 0, 0)
            act = gelu(r.z0[s] * scale + shift) * spread(r.full[s], mid)
            act = act.astype(BF16)
            r.act1[s] = act
            gather_tiles(s, act, r.pick[...])
        z = dot(r.cols[...], r.k_spatial1[...])
        for s in range(slots):
            r.z1[s] = rows_of(z, s)
            put_pair(1, s, rows_of(z, s) * half_wide(s, mid))
        send_stats(1)
        share(r.act1, r.h_act1, r.h_recv.at[0])
        for s in range(slots):
            r.slope0[s] = gelu_slope(activation(s, 0, r.z0[s])) * spread(r.full[s], mid)
        fetch_weight(3).wait()
        wait_stats(1)

        for s in range(slots):
            scale, shift = settle(s, 1, 1)
            mixed = gelu(r.z1[s] * scale + shift) * half_wide(s, mid)
            r.mix1[s] = mixed.astype(BF16)
        z = dot(rows2(r.mix1), r.k_expand1[...])
        for s in range(slots):
            r.z_branch[s] = rows_of(z, s)
            put_pair(2, s, rows_of(z, s))
        send_stats(2)
        share(r.mix1, r.h_mix1, r.h_recv.at[1])
        for s in range(slots):
            r.slope1[s] = gelu_slope(activation(s, 1, r.z1[s])) * half_wide(s, mid)
        fetch_weight(4).wait()
        wait_stats(2)

        for s in range(slots):
            scale, shift = settle(s, 2, 2, 0)
            scale_short, shift_short = settle(s, 3, 2, out)
            joined = (r.z_branch[s] * scale + shift) + (
                r.z_short[s] * scale_short + shift_short
            )
            r.slope2[s] = joined
            block = gelu(joined) * half_wide(s, out)
            r.low1[s] = block.astype(BF16)
        z = dot(rows2(r.low1), r.k_reduce2[...])
        for s in range(slots):
            r.z3[s] = rows_of(z, s)
            put_pair(3, s, rows_of(z, s))
        send_stats(3)
        share(r.low1, r.h_low1, r.h_recv.at[2])
        for s in range(slots):
            mask = half_wide(s, out)
            branch = activation(s, 2, r.z_branch[s])
            joined = r.slope2[s]
            add_squares(s, 0, branch * branch * mask)
            block = gelu(joined) * mask
            add_squares(s, 1, block * block)
            r.slope2[s] = gelu_slope(joined) * mask
        fetch_weight(5).wait()
        wait_stats(3)

        for s in range(slots):
            scale, shift = settle(s, 4, 3)
            act = gelu(r.z3[s] * scale + shift) * half_wide(s, mid)
            act = act.astype(BF16)
            r.act2[s] = act
            gather_tiles(s, act, r.tiles[s])
        z = dot(r.cols[...], r.k_spatial2[...])
        for s in range(slots):
            r.z4[s] = rows_of(z, s)
            put_pair(4, s, rows_of(z, s) * half_wide(s, mid))
        send_stats(4)
        share(r.act2, r.h_act2, r.h_recv.at[3])
        for s in range(slots):
            r.slope3[s] = gelu_slope(activation(s, 4, r.z3[s])) * half_wide(s, mid)
        fetch_weight(6).wait()
        wait_stats(4)

        for s in range(slots):
            scale, shift = settle(s, 5, 4)
            mixed = gelu(r.z4[s] * scale + shift) * half_wide(s, mid)
            r.mix2[s] = mixed.astype(BF16)
        z = dot(rows2(r.mix2), r.k_expand2[...])
        for s in range(slots):
            r.z5[s] = rows_of(z, s)
            put_pair(5, s, rows_of(z, s))
        send_stats(5)
        share(r.mix2, r.h_mix2, r.h_recv.at[4])
        for s in range(slots):
            r.slope4[s] = gelu_slope(activation(s, 5, r.z4[s])) * half_wide(s, mid)
            fetch_cotangent(s).wait()
        wait_stats(5)

        for s in range(slots):
            scale, shift = settle(s, 6, 5)
            joined = (r.z5[s] * scale + shift) + r.low1[s].astype(F32)
            cot = jnp.concatenate(
                [r.cot_raw[s].astype(F32), jnp.zeros((HR - HALF * HALF, out), F32)], axis=0
            )
            u = gelu_slope(joined) * cot * half_wide(s, out)
            r.u_out[s] = u
            put(6, 2 * s, column_sum(u))
            put(6, 2 * s + 1, column_sum(u * normed(s, 6, r.z5[s])))
        send_stats(6)
        for s in range(slots):
            mask = half_wide(s, out)
            branch = activation(s, 6, r.z5[s])
            add_squares(s, 2, branch * branch * mask)
            block = gelu(branch + r.low1[s].astype(F32)) * mask
            add_squares(s, 3, block * block)
            r.final[s] = block.astype(BF16)
        part = out // narrow
        for s in range(slots):
            for target in range(narrow):
                src = r.final.at[s, :, target * part : (target + 1) * part]
                dst = r.o_final.at[first_micro + s]
                group.remote(
                    src, dst, r.o_recv.at[0], (w, target),
                    (first_micro + s < micros) & (n != target),
                )
        for index in range(4):
            put(7, 2 * slots + index, r.squares[index : index + 1, :])
        wait_stats(6)

        for s in range(slots):
            k0, k1, k2 = settle_back(s, 6, 6, 2 * s, 2 * s + 1)
            grad = (k0 * r.u_out[s] + k1 + k2 * r.z5[s]) * half_wide(s, out)
            r.g_e2[s] = grad.astype(BF16)
        back = dot_nt(rows2(r.g_e2), r.k_expand2[...]).astype(BF16).astype(F32)
        for s in range(slots):
            u = rows_of(back, s) * r.slope4[s]
            r.u_mid[s] = u
            put(7, 2 * s, column_sum(u))
            put(7, 2 * s + 1, column_sum(u * normed(s, 5, r.z4[s])))
        send_stats(7)
        share(r.g_e2, r.h_g_e2, r.h_recv.at[5], out // columns)
        wait_stats(7)
        for index in range(4):
            r.rms_part[index : index + 1, :] = total(7, 2 * slots + index)
        count = r.counts[0:1, :]
        for s in range(1, slots):
            count = count + live_row(s, r.counts[s : s + 1, :])
        r.rms_part[4:5, :] = spread(count, mid)

        for s in range(slots):
            k0, k1, k2 = settle_back(s, 5, 7, 2 * s, 2 * s + 1)
            grad = (k0 * r.u_mid[s] + k1 + k2 * r.z4[s]) * half_wide(s, mid)
            r.g_s2[s] = grad.astype(BF16)
            gather_tiles(s, r.g_s2[s], r.tiles[s])
        back = None
        for t in range(TAPS):
            back_tap = dot_nt(
                r.cols[:, t * mid : (t + 1) * mid],
                r.k_spatial2[(8 - t) * mid : (9 - t) * mid, :],
            )
            back = back_tap if back is None else back + back_tap
        back = back.astype(BF16).astype(F32)
        for s in range(slots):
            u = rows_of(back, s) * r.slope3[s]
            r.u_mid[s] = u
            put(8, 2 * s, column_sum(u))
            put(8, 2 * s + 1, column_sum(u * normed(s, 4, r.z3[s])))
        send_stats(8)
        share(r.g_s2, r.h_g_s2, r.h_recv.at[6], mid // columns)
        wait_stats(8)

        for s in range(slots):
            k0, k1, k2 = settle_back(s, 4, 8, 2 * s, 2 * s + 1)
            grad = (k0 * r.u_mid[s] + k1 + k2 * r.z3[s]) * half_wide(s, mid)
            r.g_r2[s] = grad.astype(BF16)
        back = dot_nt(rows2(r.g_r2), r.k_reduce2[...])
        for s in range(slots):
            u = (rows_of(back, s) + r.u_out[s].astype(BF16).astype(F32)) * r.slope2[s]
            r.u_out[s] = u
            put(9, 3 * s, column_sum(u))
            put(9, 3 * s + 1, column_sum(u * normed(s, 2, r.z_branch[s])))
            put(9, 3 * s + 2, column_sum(u * normed(s, 3, r.z_short[s])))
        send_stats(9)
        share(r.g_r2, r.h_g_r2, r.h_recv.at[7], mid // columns)
        wait_stats(9)

        for s in range(slots):
            k0, k1, k2 = settle_back(s, 2, 9, 3 * s, 3 * s + 1)
            grad = (k0 * r.u_out[s] + k1 + k2 * r.z_branch[s]) * half_wide(s, out)
            r.g_e1[s] = grad.astype(BF16)
        back = dot_nt(rows2(r.g_e1), r.k_expand1[...]).astype(BF16).astype(F32)
        for s in range(slots):
            u = rows_of(back, s) * r.slope1[s]
            r.u_mid[s] = u
            put(10, 2 * s, column_sum(u))
            put(10, 2 * s + 1, column_sum(u * normed(s, 1, r.z1[s])))
        send_stats(10)
        share(r.g_e1, r.h_g_e1, r.h_recv.at[8], out // columns)
        for s in range(slots):
            k0, k1, k2 = settle_back(s, 3, 9, 3 * s, 3 * s + 2)
            grad = (k0 * r.u_out[s] + k1 + k2 * r.z_short[s]) * half_wide(s, out)
            r.g_p1[s] = grad.astype(BF16)
        share(r.g_p1, r.h_g_p1, r.h_recv.at[9], out // columns)
        build_pick_back()
        r.picked[...] = dot_nt(rows2(r.g_p1), r.k_project1[...]).astype(
            BF16
        )
        wait_stats(10)

        for s in range(slots):
            k0, k1, k2 = settle_back(s, 1, 10, 2 * s, 2 * s + 1)
            grad = (k0 * r.u_mid[s] + k1 + k2 * r.z1[s]) * half_wide(s, mid)
            r.g_s1[s] = grad.astype(BF16)
        g_rows = rows2(r.g_s1)
        for t in range(TAPS):
            r.cols[:, t * mid : (t + 1) * mid] = dot_nt(
                g_rows, r.k_spatial1[t * mid : (t + 1) * mid, :]
            ).astype(BF16)
        for s in range(slots):
            back = jnp.concatenate(
                [r.cols[s * HR : (s + 1) * HR, t * mid : (t + 1) * mid] for t in range(TAPS)],
                axis=0,
            )
            u = dot(r.pick_back[...], back) * r.slope0[s]
            r.slope0[s] = u
            put(11, 2 * s, column_sum(u))
            put(11, 2 * s + 1, column_sum(u * normed(s, 0, r.z0[s])))
        send_stats(11)
        share(r.g_s1, r.h_g_s1, r.h_recv.at[10], mid // columns)
        wait_stats(11)

        for s in range(slots):
            k0, k1, k2 = settle_back(s, 0, 11, 2 * s, 2 * s + 1)
            grad = (k0 * r.slope0[s] + k1 + k2 * r.z0[s]) * spread(r.full[s], mid)
            r.g_r1[s] = grad.astype(BF16)
        share(r.g_r1, r.h_g_r1, r.h_recv.at[11], mid // columns)
        section = allch // wide
        own = pl.ds(pl.multiple_of(w * section, 128), section)
        for target in range(narrow):
            group.remote(
                r.norm_sums.at[:, own], r.o_norms.at[x], r.o_recv.at[2], (w, target),
                n != target,
            )
            group.remote(
                r.rms_part, r.o_rms.at[x], r.o_recv.at[3], (w, target), n != target
            )
        r.o_norms[x] = r.norm_sums[:, own]
        r.o_rms[x] = r.rms_part[...]
        for s in range(slots):
            grad = dot_nt(r.g_r1[s], r.k_reduce1[...])
            grad = grad + dot(
                r.pick_back[:, 4 * HR : 5 * HR], r.picked[s * HR : (s + 1) * HR, :]
            )
            r.image[s] = grad.astype(BF16)
        part = inw // narrow
        for s in range(slots):
            for target in range(narrow):
                group.remote(
                    r.image.at[s, :, target * part : (target + 1) * part],
                    r.o_input.at[first_micro + s], r.o_recv.at[1], (w, target),
                    (first_micro + s < micros) & (n != target),
                )
        for s in range(slots):
            for target in range(narrow):

                @pl.when((n == target) & (first_micro + s < micros))
                def _(s=s, target=target):
                    wide_part = out // narrow
                    r.o_final[first_micro + s] = r.final[
                        s, :, target * wide_part : (target + 1) * wide_part
                    ]
                    r.o_input[first_micro + s] = r.image[
                        s, :, target * part : (target + 1) * part
                    ]

        for c in range(columns):
            amount = min(slots, micros - c * slots)
            others = micros - max(amount, 0)

            @pl.when(x == c)
            def _(others=others):
                wait_bytes(r.o_final.at[0:others], r.o_recv.at[0])
                wait_bytes(r.o_input.at[0:others], r.o_recv.at[1])

        wait_bytes(r.o_norms.at[0 : columns - 1], r.o_recv.at[2])
        wait_bytes(r.o_rms.at[0 : columns - 1], r.o_recv.at[3])
        for index, spec in enumerate(plan.products):
            wait_bytes(getattr(r, "out_" + spec.name), r.w_recv.at[index])
        group.finish()
        for step in range(12):
            wait_bytes(r.stat[step].at[pl.ds(0, wide - 1)], r.stat_send.at[step])

    def helper(*local):
        r.__dict__.update(zip(plan.helper_names, local))
        group = Group(r.helper_sends)
        parity = w % 2
        place = w // 2
        partner = w + 1 - 2 * parity

        for m in range(micros):
            fetch_image(m, m).start()
        build_picks()
        for m in range(micros):
            build_tiles(m, m)
        for m in range(micros):
            fetch_image(m, m).wait()
            mask_image(m, m)
        centre = r.pick[4 * HR : 5 * HR, :]
        for m in range(micros):
            r.picked[m * HR : (m + 1) * HR, :] = dot(centre, r.image[m]).astype(BF16)
        pass_barrier()

        def tall(ref):
            value = ref[...]
            return value.reshape(value.shape[0] * value.shape[1], value.shape[2])

        def multiply(spec):
            name, rows = spec.name, spec.rows
            grad = tall(getattr(r, "h_g_" + name))
            product = getattr(r, "p_" + name)
            if spec.taps == 1:
                left = r.picked if name == "p1" else None
                chunk = min(256, spec.depth)
                for begin in range(0, spec.depth, chunk):
                    if name == "p1":
                        piece = left[:, begin : begin + chunk]
                    else:
                        source = getattr(r, spec.left)
                        piece = source[:, :, begin : begin + chunk]
                        piece = piece.reshape(piece.shape[0] * piece.shape[1], chunk)
                    value = dot_tn(piece, grad).astype(BF16)
                    for b in range(chunk // rows):
                        block = begin // rows + b
                        product[block // 2, block % 2, 0] = value[b * rows : (b + 1) * rows]
            else:
                for m in range(micros):
                    select = r.pick[...] if name == "s1" else r.tiles[m]
                    columns_now = dot(select, getattr(r, spec.left)[m]).astype(BF16)
                    for t in range(TAPS):
                        r.h_cols[t, m * HR : (m + 1) * HR, :] = columns_now[
                            t * HR : (t + 1) * HR
                        ]

                @pl.loop(0, TAPS)
                def _(t):
                    value = dot_tn(r.h_cols[t], grad).astype(BF16)
                    for block in range(wide):
                        product[block // 2, block % 2, t] = value[
                            block * rows : (block + 1) * rows
                        ]

        def start_first(index):
            name = plan.products[index].name
            group.remote(
                getattr(r, "p_" + name).at[:, 1 - parity], getattr(r, "one_" + name), r.one_recv.at[index],
                (partner, n),
            )

        def start_second(index):
            name = plan.products[index].name
            product, one, two = getattr(r, "p_" + name), getattr(r, "one_" + name), getattr(r, "two_" + name)
            wait_bytes(one, r.one_recv.at[index])
            for q in range(pairs):
                value = product[q, parity].astype(F32) + one[q].astype(F32)
                value = value.astype(BF16)
                product[q, parity] = value
                group.remote(
                    product.at[q, parity], two.at[place], r.two_recv.at[index],
                    (2 * q + parity, n), place != q,
                )
            two[place] = product[place, parity]

        def finish(index):
            spec = plan.products[index]
            name = spec.name
            two, last = getattr(r, "two_" + name), getattr(r, "last_" + name)
            if pairs > 1:
                wait_bytes(two.at[0 : pairs - 1], r.two_recv.at[index])
            value = two[0].astype(F32)
            for q in range(1, pairs):
                value = value + two[q].astype(F32)
            width = spec.width // 2
            result = getattr(r, "out_" + name)
            shape = result.shape
            result[...] = value[..., :width].reshape(shape)
            last[...] = value[..., width:].reshape(shape)
            group.remote(last, result, r.w_recv.at[index], (w, n + 1))

        count = len(plan.products)
        for index in range(count + 2):
            if index < count:
                spec = plan.products[index]
                name = spec.name
                if spec.left_sem is not None:
                    wait_bytes(getattr(r, spec.left), r.h_recv.at[spec.left_sem])
                wait_bytes(getattr(r, "h_g_" + name), r.h_recv.at[spec.grad_sem])
                multiply(spec)
                start_first(index)
            if 0 <= index - 1 < count:
                start_second(index - 1)
            if 0 <= index - 2 < count:
                finish(index - 2)

        wait_bytes(r.o_final, r.o_recv.at[0])
        wait_bytes(r.o_input, r.o_recv.at[1])
        wait_bytes(r.o_norms, r.o_recv.at[2])
        wait_bytes(r.o_rms, r.o_recv.at[3])
        group.finish()

    @pl.when(core == 1)
    def _():
        pl.run_scoped(chain, *plan.chain_local)

    @pl.when(core == 0)
    def _():
        pl.run_scoped(helper, *plan.helper_local)

    for m in range(micros):
        r.out_block[m, 0] = r.o_final[m, 0 : HALF * HALF, :]
        r.out_input[m, 0] = r.o_input[m, 0 : FULL * FULL, :]
    norms = r.o_norms[0]
    sums = r.o_rms[0]
    for c in range(1, columns):
        norms = norms + r.o_norms[c]
        sums = sums + r.o_rms[c]
    share_width = allch // (wide * narrow)
    for target in range(narrow):

        @pl.when(n == target)
        def _(target=target):
            piece = norms[:, target * share_width : (target + 1) * share_width]
            r.out_gains[...] = piece[0]
            r.out_biases[...] = piece[1]

    square = jnp.sum(sums[0:4], axis=1, keepdims=True)
    rms = jnp.sqrt(square / (sums[4:5, 0:1] * out))
    for index in range(4):
        r.out_rms[index] = rms[index, 0]


def hand_out(results):
    count = len(results)

    def copies(*refs):
        for i in range(count - 1):
            refs[count + i][...] = refs[i][...]
        for index in range(4):
            refs[2 * count - 1][index] = refs[count - 1][index]

    in_vmem = pl.BlockSpec(memory_space=pltpu.VMEM)
    in_smem = pl.BlockSpec(memory_space=pltpu.SMEM)
    places = (in_vmem,) * (count - 1) + (in_smem,)
    return pl.pallas_call(
        copies,
        out_shape=tuple(jax.ShapeDtypeStruct(v.shape, v.dtype) for v in results),
        in_specs=places,
        out_specs=places,
        name="hand_out",
    )(*results)


def shards(
    inputs, image_sides, tile_cuts, cotangent, w_reduce1, w_spatial1, w_expand1, w_project1,
    w_reduce2, w_spatial2, w_expand2, norm_gains, norm_biases,
):
    wide = lax.axis_size(WIDE)
    narrow = lax.axis_size(NARROW)
    columns = narrow // 2
    micros = inputs.shape[0]
    slots = -(-micros // columns)
    inw, mid = w_reduce1.shape
    out = w_expand1.shape[1]
    allch = norm_gains.shape[0]
    pairs = wide // 2
    starts = (0, mid, 2 * mid, 2 * mid + out, 2 * mid + 2 * out, 3 * mid + 2 * out,
              4 * mid + 2 * out)
    widths = (mid, mid, out, out, mid, mid, out)

    def product(name, taps, depth, width, left, left_sem, grad_sem, rows):
        return SimpleNamespace(
            name=name, taps=taps, depth=depth, width=width // columns, rows=depth // wide,
            left=left, left_sem=left_sem, grad_sem=grad_sem, cells=rows,
        )

    products = (
        product("e2", 1, mid, out, "h_mix2", 4, 5, HR),
        product("s2", TAPS, mid, mid, "h_act2", 3, 6, HR),
        product("r2", 1, out, mid, "h_low1", 2, 7, HR),
        product("e1", 1, mid, out, "h_mix1", 1, 8, HR),
        product("p1", 1, inw, out, "picked", None, 9, HR),
        product("s1", TAPS, mid, mid, "h_act1", 0, 10, HR),
        product("r1", 1, inw, mid, "image", None, 11, FR),
    )
    vmem = pltpu.VMEM
    hbm = pl.BlockSpec(memory_space=pl.ANY)
    in_vmem = pl.BlockSpec(memory_space=pltpu.VMEM)
    in_smem = pl.BlockSpec(memory_space=pltpu.SMEM)

    args = dict(
        inputs=(inputs, hbm),
        image_sides=(image_sides.T, in_smem),
        tile_cuts=(tile_cuts.transpose(1, 2, 0), in_smem),
        cotangent=(cotangent, hbm),
        w_reduce1=(w_reduce1, hbm),
        w_spatial1=(w_spatial1.reshape(TAPS * mid, mid), hbm),
        w_expand1=(w_expand1, hbm),
        w_project1=(w_project1, hbm),
        w_reduce2=(w_reduce2, hbm),
        w_spatial2=(w_spatial2.reshape(TAPS * mid, mid), hbm),
        w_expand2=(w_expand2, hbm),
        gains=(norm_gains.reshape(1, allch), in_vmem),
        biases=(norm_biases.reshape(1, allch), in_vmem),
    )
    share = allch // (wide * narrow)
    outputs = dict(
        out_block=((micros, 1, HALF * HALF, out // narrow), BF16),
        out_input=((micros, 1, FULL * FULL, inw // narrow), BF16),
    )
    for spec in (products[6], products[5], products[3], products[4], products[2], products[1],
                 products[0]):
        shape = (spec.rows, spec.width // 2)
        if spec.taps > 1:
            shape = (spec.taps,) + shape
        outputs["out_" + spec.name] = (shape, F32)
    outputs["out_gains"] = ((share,), F32)
    outputs["out_biases"] = ((share,), F32)
    outputs["out_rms"] = ((4,), F32)

    scratch = dict(
        pick_back=vmem((FR, TAPS * HR), BF16),
        k_reduce1=vmem(w_reduce1.shape, BF16),
        k_spatial1=vmem((TAPS * mid, mid), BF16),
        k_expand1=vmem(w_expand1.shape, BF16),
        k_project1=vmem(w_project1.shape, BF16),
        k_reduce2=vmem(w_reduce2.shape, BF16),
        k_spatial2=vmem((TAPS * mid, mid), BF16),
        k_expand2=vmem(w_expand2.shape, BF16),
        cot_raw=vmem((slots, HALF * HALF, out), BF16),
        half=vmem((slots, HR, 128), F32),
        full=vmem((slots, FR, 128), F32),
        counts=vmem((slots, 128), F32),
        norms=vmem((2 * slots, allch), F32),
        norm_sums=vmem((2, allch), F32),
        squares=vmem((4, mid), F32),
        rms_part=vmem((8, mid), F32),
        z0=vmem((slots, FR, mid), F32),
        slope0=vmem((slots, FR, mid), F32),
        act1=vmem((slots, FR, mid), BF16),
        cols=vmem((slots * HR, TAPS * mid), BF16),
        z1=vmem((slots, HR, mid), F32),
        slope1=vmem((slots, HR, mid), F32),
        mix1=vmem((slots, HR, mid), BF16),
        z_branch=vmem((slots, HR, out), F32),
        z_short=vmem((slots, HR, out), F32),
        slope2=vmem((slots, HR, out), F32),
        low1=vmem((slots, HR, out), BF16),
        z3=vmem((slots, HR, mid), F32),
        slope3=vmem((slots, HR, mid), F32),
        act2=vmem((slots, HR, mid), BF16),
        z4=vmem((slots, HR, mid), F32),
        slope4=vmem((slots, HR, mid), F32),
        mix2=vmem((slots, HR, mid), BF16),
        z5=vmem((slots, HR, out), F32),
        u_out=vmem((slots, HR, out), F32),
        u_mid=vmem((slots, HR, mid), F32),
        final=vmem((slots, HR, out), BF16),
        g_e2=vmem((slots, HR, out), BF16),
        g_s2=vmem((slots, HR, mid), BF16),
        g_r2=vmem((slots, HR, mid), BF16),
        g_e1=vmem((slots, HR, out), BF16),
        g_p1=vmem((slots, HR, out), BF16),
        g_s1=vmem((slots, HR, mid), BF16),
        g_r1=vmem((slots, FR, mid), BF16),
        h_act1=vmem((micros, FR, mid), BF16),
        h_mix1=vmem((micros, HR, mid), BF16),
        h_low1=vmem((micros, HR, out), BF16),
        h_act2=vmem((micros, HR, mid), BF16),
        h_mix2=vmem((micros, HR, mid), BF16),
        h_cols=vmem((TAPS, micros * HR, mid), BF16),
        o_final=vmem((micros, HR, out // narrow), BF16),
        o_input=vmem((micros, FR, inw // narrow), BF16),
        o_norms=vmem((columns, 2, allch // wide), F32),
        o_rms=vmem((columns, 8, mid), F32),
    )
    stat_rows = (3, 2, 2, 2, 2, 2, 2, 2, 2, 3, 2, 2)
    stat_widths = (mid, mid, 2 * out, mid, mid, out, out, mid, mid, out, mid, mid)
    for step in range(12):
        rows = stat_rows[step] * slots + (4 if step == 7 else 0)
        scratch["stat%d" % step] = vmem((wide, rows, stat_widths[step]), F32)
    for spec in products:
        name, taps, rows, width = spec.name, spec.taps, spec.rows, spec.width
        scratch["h_g_" + name] = vmem((micros, spec.cells, width), BF16)
        scratch["p_" + name] = vmem((pairs, 2, taps, rows, width), BF16)
        scratch["one_" + name] = vmem((pairs, taps, rows, width), BF16)
        scratch["two_" + name] = vmem((pairs, taps, rows, width), BF16)
        last = (rows, width // 2) if taps == 1 else (taps, rows, width // 2)
        scratch["last_" + name] = vmem(last, F32)
    semaphores = dict(
        fetch=(16,),
        stat_send=(12,),
        stat_recv=(12,),
        chain_sends=(12 * columns * columns + 2 * slots * narrow + 2 * narrow,),
        helper_sends=(len(products) * (2 + pairs),),
        h_recv=(12,),
        o_recv=(4,),
        w_recv=(len(products),),
        one_recv=(len(products),),
        two_recv=(len(products),),
    )
    for name, shape in semaphores.items():
        scratch[name] = pltpu.SemaphoreType.DMA(shape)
    helper_local = {name: scratch.pop(name) for name in tuple(scratch) if name in ("h_cols",)
                    or name[:2] == "p_" or name[:5] == "last_"}

    def image_buffers(count):
        return dict(
            raw=vmem((count, FULL * FULL, inw), BF16),
            image=vmem((count, FR, inw), BF16),
            picked=vmem((count * HR, inw), BF16),
            pick=vmem((TAPS * HR, FR), BF16),
            tiles=vmem((count, TAPS * HR, HR), BF16),
        )

    chain_local = {name: scratch.pop(name) for name in tuple(scratch)
                   if name not in semaphores and name[:2] not in ("h_", "o_") and name[:4] not in ("one_", "two_", "stat")}
    helper_local.update(image_buffers(micros))
    chain_local.update(image_buffers(slots))
    plan = SimpleNamespace(
        chain_names=tuple(chain_local), chain_local=tuple(chain_local.values()),
        helper_names=tuple(helper_local), helper_local=tuple(helper_local.values()),
        names=tuple(args) + tuple(outputs) + tuple(scratch),
        wide=wide, narrow=narrow, micros=micros, slots=slots,
        mid=mid, out=out, inw=inw, allch=allch,
        starts=starts, layers=tuple(zip(starts, widths)), products=products,
    )
    results = pl.pallas_call(
        functools.partial(kernel, plan),
        out_shape=tuple(jax.ShapeDtypeStruct(s, d) for s, d in outputs.values()),
        in_specs=[spec for _, spec in args.values()],
        out_specs=(in_vmem,) * (len(outputs) - 1) + (in_smem,),
        scratch_shapes=list(scratch.values()),
        compiler_params=pltpu.CompilerParams(
            collective_id=0, has_side_effects=True, vmem_limit_bytes=63 * 2**20 + 2**19
        ),
        name="bottleneck_pair",
    )(*[value for value, _ in args.values()])
    return hand_out(results)


def solution(mesh):
    return jax.shard_map(
        shards,
        mesh=mesh,
        in_specs=(
            P(None, WIDE, None, None),
            P(None, WIDE),
            P(None, WIDE, None),
            P(None, WIDE, None, None),
            P(), P(), P(), P(), P(), P(), P(), P(), P(),
        ),
        out_specs=(
            P(None, WIDE, None, NARROW),
            P(None, WIDE, None, NARROW),
            P(WIDE, NARROW),
            P(None, WIDE, NARROW),
            P(WIDE, NARROW),
            P(WIDE, NARROW),
            P(WIDE, NARROW),
            P(None, WIDE, NARROW),
            P(WIDE, NARROW),
            P((WIDE, NARROW)),
            P((WIDE, NARROW)),
            P(),
        ),
        check_vma=False,
    )
```

```python
import functools
import math
from types import SimpleNamespace

import jax
import jax.numpy as jnp
from jax import lax
from jax.experimental import pallas as pl
from jax.experimental.pallas import tpu as pltpu
from jax.sharding import PartitionSpec as P

MESH = pl.DeviceIdType.MESH
WIDE, NARROW = "wide", "narrow"
BF16 = jnp.bfloat16
F32 = jnp.float32
HALF = 7
FULL = 2 * HALF
EPSILON = 1e-05
C0 = math.sqrt(2.0 / math.pi)
C1 = C0 * 0.044715
HR = 64
FR = 208
TAPS = 9
STEPS = 15
LOW_STEPS = (6, 7, 8, 9, 10, 11, 13)
HALVING = ("e2", "r2", "e1", "p1")


def dot(a, b):
    return jnp.dot(a, b, preferred_element_type=F32)


def dot_nt(a, b):
    return lax.dot_general(a, b, (((1,), (1,)), ((), ())), preferred_element_type=F32)


def dot_tn(a, b):
    return lax.dot_general(a, b, (((0,), (0,)), ((), ())), preferred_element_type=F32)


def spread(mask, width):
    return jnp.concatenate([mask] * (width // 128), axis=1)


def gelu(v):
    t = jnp.tanh(v * (C0 + C1 * (v * v)))
    h = 0.5 * v
    return h + h * t


def gelu_slope(v):
    v2 = v * v
    t = jnp.tanh(v * (C0 + C1 * v2))
    return 0.5 + 0.5 * t + (0.5 * v) * (1.0 - t * t) * (C0 + (3.0 * C1) * v2)


def column_sum(values):
    return jnp.sum(values, axis=0, keepdims=True)


def half_cell(p):
    i = lax.shift_right_logical(p * 9363, 16)
    return i, p - HALF * i


def full_cell(p):
    i = lax.shift_right_logical(p * 4682, 16)
    return i, p - FULL * i


def tap_of(r):
    t = lax.shift_right_logical(r, 6)
    ta = lax.shift_right_logical(t * 11, 5)
    return ta - 1, t - 3 * ta - 1


def one_zero(condition):
    return jnp.where(condition, 1.0, 0.0)


def strided_pick(rows, cells):
    a, b = tap_of(rows)
    p = lax.bitwise_and(rows, 63)
    i, j = half_cell(p)
    r, c = 2 * i + a, 2 * j + b
    inside = (p < HALF * HALF) & (r >= 0) & (r < FULL) & (c >= 0) & (c < FULL)
    return one_zero(inside & (cells == r * FULL + c)).astype(BF16)


def tile_pick(rows, cells, cut_row, cut_col):
    a, b = tap_of(rows)
    p = lax.bitwise_and(rows, 63)
    i, j = half_cell(p)
    r, c = i + a, j + b
    inside = (p < HALF * HALF) & (r >= 0) & (r < HALF) & (c >= 0) & (c < HALF)
    row_far = one_zero(r >= cut_row) - one_zero(i >= cut_row)
    col_far = one_zero(c >= cut_col) - one_zero(j >= cut_col)
    same = (row_far == 0.0) & (col_far == 0.0)
    return one_zero(inside & same & (cells == r * HALF + c)).astype(BF16)


class Group:
    def __init__(self, sems):
        self.sems = sems
        self.used = 0
        self.items = []

    def sem(self):
        self.used += 1
        return self.sems.at[self.used - 1]

    def remote(self, src, dst, recv_sem, device, when=None):
        copy = pltpu.make_async_remote_copy(
            src_ref=src, dst_ref=dst, send_sem=self.sem(), recv_sem=recv_sem,
            device_id=device, device_id_type=MESH,
        )
        if when is None:
            copy.start()
        else:
            pl.when(when)(copy.start)
        self.items.append((copy, when))

    def finish(self):
        for copy, when in self.items:
            if when is None:
                copy.wait_send()
            else:
                pl.when(when)(copy.wait_send)


def wait_bytes(ref, sem):
    pltpu.make_async_copy(ref, ref, sem).wait()


def kernel(plan, *refs):
    r = SimpleNamespace(**dict(zip(plan.names, refs)))
    r.stat = [getattr(r, "stat%d" % step) for step in range(STEPS)]
    wide, narrow, micros, slots = plan.wide, plan.narrow, plan.micros, plan.slots
    mid, out, inw, allch = plan.mid, plan.out, plan.inw, plan.allch
    places = wide // 2
    columns = narrow // 2
    layers = plan.layers
    w = lax.axis_index(WIDE)
    n = lax.axis_index(NARROW)
    x = n // 2
    core = n % 2
    first_micro = x * slots
    fetch = r.fetch
    parity = w % 2
    place = w // 2
    partner = w + 1 - 2 * parity
    own_act = 0 if plan.gather else parity

    def micro_of(s):
        return lax.rem(first_micro + s, micros)

    barrier = pltpu.get_barrier_semaphore()

    @pl.loop(1, wide)
    def _(d):
        pl.semaphore_signal(
            barrier, inc=1, device_id=(lax.rem(w + d, wide), n), device_id_type=MESH
        )

    for d in range(1, narrow):
        pl.semaphore_signal(
            barrier, inc=1, device_id=(w, lax.rem(n + d, narrow)), device_id_type=MESH
        )

        pl.semaphore_signal(
            barrier, inc=1, device_id=(partner, lax.rem(n + d, narrow)), device_id_type=MESH
        )

    def pass_barrier():
        pl.semaphore_wait(barrier, wide - 1 + 2 * (narrow - 1))

    def build_picks():
        rows = lax.broadcasted_iota(jnp.int32, (TAPS * HR, FR), 0)
        cells = lax.broadcasted_iota(jnp.int32, (TAPS * HR, FR), 1)
        r.pick[...] = strided_pick(rows, cells)

    def build_pick_back():
        rows = lax.broadcasted_iota(jnp.int32, (FR, TAPS * HR), 1)
        cells = lax.broadcasted_iota(jnp.int32, (FR, TAPS * HR), 0)
        r.pick_back[...] = strided_pick(rows, cells)

    def build_tiles(slot, micro):
        rows = lax.broadcasted_iota(jnp.int32, (TAPS * HR, HR), 0)
        cells = lax.broadcasted_iota(jnp.int32, (TAPS * HR, HR), 1)
        r.tiles[slot] = tile_pick(
            rows, cells, r.tile_cuts[0, 0, micro], r.tile_cuts[0, 1, micro]
        )

    def full_mask(micro):
        row, col = full_cell(lax.broadcasted_iota(jnp.int32, (FR, 128), 0))
        limit = 2 * r.image_sides[0, micro]
        return one_zero((row < limit) & (col < limit))

    def half_mask(micro):
        row, col = half_cell(lax.broadcasted_iota(jnp.int32, (HR, 128), 0))
        limit = r.image_sides[0, micro]
        return one_zero((row < limit) & (col < limit))

    def fetch_image(slot, micro):
        return pltpu.make_async_copy(r.inputs.at[micro, 0], r.raw.at[slot], fetch.at[slot])

    def mask_image(target, slot, micro):
        mask = full_mask(micro)
        raw = jnp.concatenate(
            [r.raw[slot].astype(F32), jnp.zeros((FR - FULL * FULL, inw), F32)], axis=0
        )
        target[...] = (raw * spread(mask, inw)).astype(BF16)

    def chain(*local):
        r.__dict__.update(zip(plan.chain_names, local))
        group = Group(r.chain_sends)
        weights = (
            (r.w_reduce1, r.k_reduce1), (r.w_spatial1, r.k_spatial1), (r.w_project1, r.k_project1),
            (r.w_expand1, r.k_expand1), (r.w_reduce2, r.k_reduce2), (r.w_spatial2, r.k_spatial2),
            (r.w_expand2, r.k_expand2),
        )

        def fetch_weight(index):
            return pltpu.make_async_copy(*weights[index], fetch.at[4 + index])

        fetch_image(0, micro_of(0)).start()
        fetch_weight(0).start()
        for s in range(1, slots):
            fetch_image(s, micro_of(s)).start()
        for index in range(1, 7):
            fetch_weight(index).start()

        def fetch_cotangent(s):
            return pltpu.make_async_copy(
                r.cotangent.at[micro_of(s), 0], r.cot_raw.at[s], fetch.at[11 + s]
            )

        for s in range(slots):
            fetch_cotangent(s).start()
            r.half[s] = half_mask(micro_of(s))
            r.full[s] = full_mask(micro_of(s))

        def send_stats(step):
            stat = r.stat[step]

            @pl.loop(0, wide)
            def _(d):
                p = lax.rem(wide - 1 - w + d, wide)

                @pl.when(p != w)
                def _():
                    pltpu.make_async_remote_copy(
                        src_ref=stat.at[w], dst_ref=stat.at[w],
                        send_sem=r.stat_send.at[step], recv_sem=r.stat_recv.at[step],
                        device_id=(p, n), device_id_type=MESH,
                    ).start()

        def wait_stats(step):
            stat = r.stat[step]
            wait_bytes(stat.at[pl.ds(0, wide - 1)], r.stat_recv.at[step])

        def total(step, row, begin=0, width=None):
            stat = r.stat[step]
            width = stat.shape[2] if width is None else width
            part = stat[0, row : row + 1, begin : begin + width]
            for j in range(1, wide):
                part = part + stat[j, row : row + 1, begin : begin + width]
            return part

        def put(step, row, value, begin=0):
            r.stat[step][w, row : row + 1, begin : begin + value.shape[1]] = value

        def put_pair(step, s, values, begin=0):
            put(step, 2 * s, column_sum(values), begin)
            put(step, 2 * s + 1, column_sum(values * values), begin)

        def put_low(row, rows, value):
            folds = 16 // rows
            part = value.shape[1] // folds
            for k in range(folds):
                at = row * folds + k
                r.stage[at : at + 1, 0:part] = value[:, k * part : (k + 1) * part]

        def send_low(step):
            width = r.stat[step].shape[2]
            r.stat[step][w] = r.stage[:, 0:width].astype(BF16)
            send_stats(step)

        def wait_low(step):
            wait_stats(step)
            width = r.stat[step].shape[2]
            part = r.stat[step][0].astype(F32)
            for j in range(1, wide):
                part = part + r.stat[step][j].astype(F32)
            r.sums[:, 0:width] = part

        def low_total(step, row, rows):
            folds = 16 // rows
            width = r.stat[step].shape[2]
            first = row * folds
            return jnp.concatenate(
                [r.sums[first + k : first + k + 1, 0:width] for k in range(folds)], axis=1
            )

        def inverse_count(s, layer):
            count = r.counts[s : s + 1, 0:1]
            return 1.0 / (count * (4.0 if layer == 0 else 1.0))

        def settle(s, layer, step, begin=0):
            start, width = layers[layer]
            inv_n = inverse_count(s, layer)
            mean = total(step, 2 * s, begin, width) * inv_n
            square = total(step, 2 * s + 1, begin, width) * inv_n
            inv = lax.rsqrt(square - mean * mean + EPSILON)
            scale = r.gains[:, start : start + width] * inv
            r.norms[2 * s : 2 * s + 1, start : start + width] = inv
            r.norms[2 * s + 1 : 2 * s + 2, start : start + width] = -mean * inv
            return scale, r.biases[:, start : start + width] - mean * scale

        def kept(s, layer):
            start, width = layers[layer]
            gain = r.gains[:, start : start + width]
            inv = r.norms[2 * s : 2 * s + 1, start : start + width]
            offset = r.norms[2 * s + 1 : 2 * s + 2, start : start + width]
            return inv, offset, gain * inv, r.biases[:, start : start + width] + gain * offset

        def normed(s, layer, z):
            inv, offset, _, _ = kept(s, layer)
            return z * inv + offset

        def activation(s, layer, z):
            _, _, scale, shift = kept(s, layer)
            return z * scale + shift

        def settle_back(s, layer, step, sum_u=None, sum_g=None):
            start, width = layers[layer]
            sum_u = low_total(step, 2 * s, 2 * slots) if sum_u is None else sum_u
            sum_g = low_total(step, 2 * s + 1, 2 * slots) if sum_g is None else sum_g
            live = jnp.where(first_micro + s < micros, 1.0, 0.0)
            for row, value in ((0, sum_g), (1, sum_u)):
                if s == 0:
                    r.norm_sums[row : row + 1, start : start + width] = value
                else:
                    r.norm_sums[row : row + 1, start : start + width] += live * value
            inv_n = inverse_count(s, layer)
            inv, offset, k0, _ = kept(s, layer)
            k2 = -k0 * (sum_g * inv_n)
            return k0, -k0 * (sum_u * inv_n) + k2 * offset, k2 * inv

        def live_row(s, row):
            if s == 0:
                return row
            return row * jnp.where(first_micro + s < micros, 1.0, 0.0)

        def fold_row(row):
            parts = [row[:, c : c + mid] for c in range(0, row.shape[1], mid)]
            return functools.reduce(lambda a, b: a + b, parts)

        def add_squares(s, index, values):
            row = live_row(s, fold_row(column_sum(values)))
            if s == 0:
                r.squares[index : index + 1, :] = row
            else:
                r.squares[index : index + 1, :] += row

        def share(src, dst, recv_sem):
            for c in range(columns):
                amount = min(slots, micros - c * slots)
                for h in range(columns if amount > 0 else 0):
                    group.remote(
                        src.at[0:amount], dst.at[c * slots : c * slots + amount], recv_sem,
                        (w, 2 * h), x == c,
                    )

        def share_grad(src, index):
            spec = plan.products[index]
            dst = getattr(r, "h_g_" + spec.name)
            for c in range(columns):
                amount = min(slots, micros - c * slots)
                for quarter in range(narrow if amount > 0 else 0):
                    h, v = quarter // 2, quarter % 2
                    group.remote(
                        src.at[0:amount, :, quarter * spec.width : (quarter + 1) * spec.width],
                        dst.at[parity, c * slots : c * slots + amount], r.g_recv.at[index],
                        (w - parity + v, 2 * h), x == c,
                    )

        def rows2(ref):
            value = ref[...]
            return value.reshape(value.shape[0] * value.shape[1], value.shape[2])

        def set_rows(ref, value):
            ref[...] = value.reshape(ref.shape)

        def rows_of(value, s, count=HR):
            return value[s * count : (s + 1) * count]

        def gather_tiles(s, value, select):
            picked = dot(select, value).astype(BF16)
            for t in range(TAPS):
                r.cols[s * HR : (s + 1) * HR, t * mid : (t + 1) * mid] = picked[
                    t * HR : (t + 1) * HR
                ]

        def half_wide(s, width):
            return spread(r.half[s], width)

        for s in range(slots):
            fetch_image(s, micro_of(s)).wait()
            mask_image(r.image.at[s], s, micro_of(s))
        fetch_weight(0).wait()
        for s in range(slots):
            z = dot(r.image[s], r.k_reduce1[...])
            r.z0[s] = z
            put_pair(0, s, z)
            side = r.image_sides[0, micro_of(s)]
            area = jnp.full((1, mid), side * side, jnp.int32).astype(F32)
            put(0, 2 * slots + s, area)
        pass_barrier()
        send_stats(0)
        build_picks()
        for s in range(slots):
            build_tiles(s, micro_of(s))
        centre = r.pick[4 * HR : 5 * HR, :]
        for s in range(slots):
            r.picked[s * HR : (s + 1) * HR, :] = dot(centre, r.image[s]).astype(BF16)
        fetch_weight(2).wait()
        set_rows(r.z_short, dot(r.picked[...], r.k_project1[...]))
        for s in range(slots):
            put_pair(12, s, r.z_short[s])
        send_stats(12)
        fetch_weight(1).wait()
        wait_stats(0)
        for s in range(slots):
            r.counts[s : s + 1, :] = total(0, 2 * slots + s, 0, 128)

        for s in range(slots):
            scale, shift = settle(s, 0, 0)
            act = gelu(r.z0[s] * scale + shift) * spread(r.full[s], mid)
            act = act.astype(BF16)
            r.act1[s] = act
            gather_tiles(s, act, r.pick[...])
        z = dot(r.cols[...], r.k_spatial1[...])
        for s in range(slots):
            r.z1[s] = rows_of(z, s)
            put_pair(1, s, rows_of(z, s) * half_wide(s, mid))
        send_stats(1)
        share(r.act1, r.h_act1.at[own_act], r.h_recv.at[0])
        for s in range(slots):
            r.slope0[s] = gelu_slope(activation(s, 0, r.z0[s])) * spread(r.full[s], mid)
        fetch_weight(3).wait()
        wait_stats(1)

        for s in range(slots):
            scale, shift = settle(s, 1, 1)
            mixed = gelu(r.z1[s] * scale + shift) * half_wide(s, mid)
            r.mix1[s] = mixed.astype(BF16)
        z = dot(rows2(r.mix1), r.k_expand1[...])
        for s in range(slots):
            r.z_branch[s] = rows_of(z, s)
            put_pair(2, s, rows_of(z, s))
        send_stats(2)
        share(r.mix1, r.h_mix1.at[parity], r.h_recv.at[1])
        for s in range(slots):
            r.slope1[s] = gelu_slope(activation(s, 1, r.z1[s])) * half_wide(s, mid)
        fetch_weight(4).wait()
        wait_stats(12)
        wait_stats(2)

        for s in range(slots):
            scale, shift = settle(s, 2, 2)
            scale_short, shift_short = settle(s, 3, 12)
            joined = (r.z_branch[s] * scale + shift) + (
                r.z_short[s] * scale_short + shift_short
            )
            r.slope2[s] = joined
            block = gelu(joined) * half_wide(s, out)
            r.low1[s] = block.astype(BF16)
        z = dot(rows2(r.low1), r.k_reduce2[...])
        for s in range(slots):
            r.z3[s] = rows_of(z, s)
            put_pair(3, s, rows_of(z, s))
        send_stats(3)
        share(r.low1, r.h_low1.at[parity], r.h_recv.at[2])
        for s in range(slots):
            mask = half_wide(s, out)
            branch = activation(s, 2, r.z_branch[s])
            joined = r.slope2[s]
            add_squares(s, 0, branch * branch * mask)
            block = gelu(joined) * mask
            add_squares(s, 1, block * block)
            r.slope2[s] = gelu_slope(joined) * mask
        fetch_weight(5).wait()
        wait_stats(3)

        for s in range(slots):
            scale, shift = settle(s, 4, 3)
            act = gelu(r.z3[s] * scale + shift) * half_wide(s, mid)
            act = act.astype(BF16)
            r.act2[s] = act
            gather_tiles(s, act, r.tiles[s])
        z = dot(r.cols[...], r.k_spatial2[...])
        for s in range(slots):
            r.z4[s] = rows_of(z, s)
            put_pair(4, s, rows_of(z, s) * half_wide(s, mid))
        send_stats(4)
        share(r.act2, r.h_act2.at[own_act], r.h_recv.at[3])
        for s in range(slots):
            r.slope3[s] = gelu_slope(activation(s, 4, r.z3[s])) * half_wide(s, mid)
        fetch_weight(6).wait()
        wait_stats(4)

        for s in range(slots):
            scale, shift = settle(s, 5, 4)
            mixed = gelu(r.z4[s] * scale + shift) * half_wide(s, mid)
            r.mix2[s] = mixed.astype(BF16)
        z = dot(rows2(r.mix2), r.k_expand2[...])
        for s in range(slots):
            r.z5[s] = rows_of(z, s)
            put_pair(5, s, rows_of(z, s))
        send_stats(5)
        share(r.mix2, r.h_mix2.at[parity], r.h_recv.at[4])
        for s in range(slots):
            r.slope4[s] = gelu_slope(activation(s, 5, r.z4[s])) * half_wide(s, mid)
            fetch_cotangent(s).wait()
        wait_stats(5)

        for s in range(slots):
            scale, shift = settle(s, 6, 5)
            joined = (r.z5[s] * scale + shift) + r.low1[s].astype(F32)
            cot = jnp.concatenate(
                [r.cot_raw[s].astype(F32), jnp.zeros((HR - HALF * HALF, out), F32)], axis=0
            )
            u = gelu_slope(joined) * cot * half_wide(s, out)
            r.u_out[s] = u
            put_low(2 * s, 2 * slots, column_sum(u))
            put_low(2 * s + 1, 2 * slots, column_sum(u * normed(s, 6, r.z5[s])))
        send_low(6)
        for s in range(slots):
            mask = half_wide(s, out)
            branch = activation(s, 6, r.z5[s])
            add_squares(s, 2, branch * branch * mask)
            block = gelu(branch + r.low1[s].astype(F32)) * mask
            add_squares(s, 3, block * block)
            r.final[s] = block.astype(BF16)
        part = out // narrow
        for s in range(slots):
            for target in range(narrow):
                src = r.final.at[s, :, target * part : (target + 1) * part]
                dst = r.o_final.at[first_micro + s]
                group.remote(
                    src, dst, r.o_recv.at[0], (w, target),
                    (first_micro + s < micros) & (n != target),
                )
        r.stat[14][w] = r.squares[...]
        send_stats(14)
        wait_low(6)

        for s in range(slots):
            k0, k1, k2 = settle_back(s, 6, 6)
            grad = (k0 * r.u_out[s] + k1 + k2 * r.z5[s]) * half_wide(s, out)
            r.g_e2[s] = grad.astype(BF16)
        back = dot_nt(rows2(r.g_e2), r.k_expand2[...]).astype(BF16).astype(F32)
        for s in range(slots):
            u = rows_of(back, s) * r.slope4[s]
            r.u_mid[s] = u
            put_low(2 * s, 2 * slots, column_sum(u))
            put_low(2 * s + 1, 2 * slots, column_sum(u * normed(s, 5, r.z4[s])))
        send_low(7)
        share_grad(r.g_e2, 0)
        wait_low(7)
        wait_stats(14)
        for index in range(4):
            r.rms_part[index : index + 1, :] = total(14, index)
        count = r.counts[0:1, :]
        for s in range(1, slots):
            count = count + live_row(s, r.counts[s : s + 1, :])
        r.rms_part[4:5, :] = spread(count, mid)

        for s in range(slots):
            k0, k1, k2 = settle_back(s, 5, 7)
            grad = (k0 * r.u_mid[s] + k1 + k2 * r.z4[s]) * half_wide(s, mid)
            r.g_s2[s] = grad.astype(BF16)
            gather_tiles(s, r.g_s2[s], r.tiles[s])
        back = None
        for t in range(TAPS):
            back_tap = dot_nt(
                r.cols[:, t * mid : (t + 1) * mid],
                r.k_spatial2[(8 - t) * mid : (9 - t) * mid, :],
            )
            back = back_tap if back is None else back + back_tap
        back = back.astype(BF16).astype(F32)
        for s in range(slots):
            u = rows_of(back, s) * r.slope3[s]
            r.u_mid[s] = u
            put_low(2 * s, 2 * slots, column_sum(u))
            put_low(2 * s + 1, 2 * slots, column_sum(u * normed(s, 4, r.z3[s])))
        send_low(8)
        share_grad(r.g_s2, 1)
        wait_low(8)

        for s in range(slots):
            k0, k1, k2 = settle_back(s, 4, 8)
            grad = (k0 * r.u_mid[s] + k1 + k2 * r.z3[s]) * half_wide(s, mid)
            r.g_r2[s] = grad.astype(BF16)
        back = dot_nt(rows2(r.g_r2), r.k_reduce2[...])
        for s in range(slots):
            u = (rows_of(back, s) + r.u_out[s].astype(BF16).astype(F32)) * r.slope2[s]
            r.u_out[s] = u
            put_low(2 * s, 2 * slots, column_sum(u))
            put_low(2 * s + 1, 2 * slots, column_sum(u * normed(s, 2, r.z_branch[s])))
        send_low(9)
        for s in range(slots):
            put_low(s, slots, column_sum(r.u_out[s] * normed(s, 3, r.z_short[s])))
        send_low(13)
        share_grad(r.g_r2, 2)
        wait_low(9)

        for s in range(slots):
            k0, k1, k2 = settle_back(s, 2, 9)
            grad = (k0 * r.u_out[s] + k1 + k2 * r.z_branch[s]) * half_wide(s, out)
            r.g_e1[s] = grad.astype(BF16)
        back = dot_nt(rows2(r.g_e1), r.k_expand1[...]).astype(BF16).astype(F32)
        for s in range(slots):
            u = rows_of(back, s) * r.slope1[s]
            r.u_mid[s] = u
            put_low(2 * s, 2 * slots, column_sum(u))
            put_low(2 * s + 1, 2 * slots, column_sum(u * normed(s, 1, r.z1[s])))
        send_low(10)
        sums_u = [low_total(9, 2 * s, 2 * slots) for s in range(slots)]
        wait_low(13)
        for s in range(slots):
            k0, k1, k2 = settle_back(s, 3, 13, sums_u[s], low_total(13, s, slots))
            grad = (k0 * r.u_out[s] + k1 + k2 * r.z_short[s]) * half_wide(s, out)
            r.g_p1[s] = grad.astype(BF16)
        share_grad(r.g_p1, 4)
        share_grad(r.g_e1, 3)
        build_pick_back()
        r.picked[...] = dot_nt(rows2(r.g_p1), r.k_project1[...]).astype(
            BF16
        )
        wait_low(10)

        for s in range(slots):
            k0, k1, k2 = settle_back(s, 1, 10)
            grad = (k0 * r.u_mid[s] + k1 + k2 * r.z1[s]) * half_wide(s, mid)
            r.g_s1[s] = grad.astype(BF16)
        g_rows = rows2(r.g_s1)
        for t in range(TAPS):
            r.cols[:, t * mid : (t + 1) * mid] = dot_nt(
                g_rows, r.k_spatial1[t * mid : (t + 1) * mid, :]
            ).astype(BF16)
        for s in range(slots):
            back = jnp.concatenate(
                [r.cols[s * HR : (s + 1) * HR, t * mid : (t + 1) * mid] for t in range(TAPS)],
                axis=0,
            )
            u = dot(r.pick_back[...], back) * r.slope0[s]
            r.slope0[s] = u
            put_low(2 * s, 2 * slots, column_sum(u))
            put_low(2 * s + 1, 2 * slots, column_sum(u * normed(s, 0, r.z0[s])))
        send_low(11)
        share_grad(r.g_s1, 5)
        wait_low(11)

        for s in range(slots):
            k0, k1, k2 = settle_back(s, 0, 11)
            grad = (k0 * r.slope0[s] + k1 + k2 * r.z0[s]) * spread(r.full[s], mid)
            r.g_r1[s] = grad.astype(BF16)
        share_grad(r.g_r1, 6)
        section = allch // wide
        own = pl.ds(pl.multiple_of(w * section, 128), section)
        for target in range(narrow):
            group.remote(
                r.norm_sums.at[:, own], r.o_norms.at[x], r.o_recv.at[2], (w, target),
                n != target,
            )
            group.remote(
                r.rms_part, r.o_rms.at[x], r.o_recv.at[3], (w, target), n != target
            )
        r.o_norms[x] = r.norm_sums[:, own]
        r.o_rms[x] = r.rms_part[...]
        for s in range(slots):
            grad = dot_nt(r.g_r1[s], r.k_reduce1[...])
            grad = grad + dot(
                r.pick_back[:, 4 * HR : 5 * HR], r.picked[s * HR : (s + 1) * HR, :]
            )
            r.image[s] = grad.astype(BF16)
        part = inw // narrow
        for s in range(slots):
            for target in range(narrow):
                group.remote(
                    r.image.at[s, :, target * part : (target + 1) * part],
                    r.o_input.at[first_micro + s], r.o_recv.at[1], (w, target),
                    (first_micro + s < micros) & (n != target),
                )
        for s in range(slots):
            for target in range(narrow):

                @pl.when((n == target) & (first_micro + s < micros))
                def _(s=s, target=target):
                    wide_part = out // narrow
                    r.o_final[first_micro + s] = r.final[
                        s, :, target * wide_part : (target + 1) * wide_part
                    ]
                    r.o_input[first_micro + s] = r.image[
                        s, :, target * part : (target + 1) * part
                    ]

        for c in range(columns):
            amount = min(slots, micros - c * slots)
            others = micros - max(amount, 0)

            @pl.when(x == c)
            def _(others=others):
                wait_bytes(r.o_final.at[0:others], r.o_recv.at[0])
                wait_bytes(r.o_input.at[0:others], r.o_recv.at[1])

        wait_bytes(r.o_norms.at[0 : columns - 1], r.o_recv.at[2])
        wait_bytes(r.o_rms.at[0 : columns - 1], r.o_recv.at[3])
        wait_products()
        group.finish()
        for step in range(STEPS):
            wait_bytes(r.stat[step].at[pl.ds(0, wide - 1)], r.stat_send.at[step])

    def wait_products():
        for index, spec in enumerate(plan.products):
            wait_bytes(getattr(r, "out_" + spec.name), r.w_recv.at[index])

    def helper(*local):
        r.__dict__.update(zip(plan.helper_names, local))
        group = Group(r.helper_sends)
        low, high = place % 2, place // 2

        def relay(ref, sem):
            group.remote(ref.at[parity], ref.at[parity], r.y_recv.at[sem], (partner, n))

        def arrived(ref, sem):
            wait_bytes(ref.at[0], r.y_recv.at[sem])

        def scatter(src, dst, sem):
            for q in range(places):
                part = src.at[:, :, q * 128 : (q + 1) * 128]
                group.remote(
                    part, dst.at[place, parity], r.z_recv.at[sem], (2 * q + parity, n), place != q
                )

                @pl.when(place == q)
                def _(q=q):
                    dst[q, parity] = src[:, :, q * 128 : (q + 1) * 128]

        def forward(ref, sem):
            if places > 1:
                wait_bytes(ref.at[0 : places - 1, 0], r.z_recv.at[sem])
            group.remote(
                ref.at[:, parity], ref.at[:, parity], r.y_recv.at[sem], (partner, n)
            )

        def forwarded(ref, sem):
            wait_bytes(ref.at[:, 0], r.y_recv.at[sem])

        def tile_base():
            rows = lax.broadcasted_iota(jnp.int32, (TAPS * HR, HR), 0)
            cells = lax.broadcasted_iota(jnp.int32, (TAPS * HR, HR), 1)
            a, b = tap_of(rows)
            p = lax.bitwise_and(rows, 63)
            i, j = half_cell(p)
            ti, tj = i + a, j + b
            inside = (p < HALF * HALF) & (ti >= 0) & (ti < HALF) & (tj >= 0) & (tj < HALF)
            r.t_base[...] = one_zero(inside & (cells == ti * HALF + tj))
            r.t_row[...] = jnp.where(a != 0, jnp.maximum(i, ti), -1).astype(F32)
            r.t_col[...] = jnp.where(b != 0, jnp.maximum(j, tj), -1).astype(F32)

        def tiles_at(q, v, m):
            keep = (r.t_row[...] != r.cuts[q, v, 2 * m : 2 * m + 1, 0:HR]) & (
                r.t_col[...] != r.cuts[q, v, 2 * m + 1 : 2 * m + 2, 0:HR]
            )
            return jnp.where(keep, r.t_base[...], 0.0).astype(BF16)

        def strided_columns(cols, source):
            @pl.loop(0, places)
            def _(q):
                for v in range(2):
                    grids = jnp.concatenate([source[q, v, m] for m in range(micros)], axis=1)
                    picked = dot(r.pick[...], grids).astype(BF16)
                    for m in range(micros):
                        row = pl.multiple_of(((q * 2 + v) * micros + m) * HR, HR)
                        for t in range(TAPS):
                            cols[pl.ds(row, HR), t * 128 : (t + 1) * 128] = picked[
                                t * HR : (t + 1) * HR, m * 128 : (m + 1) * 128
                            ]

        def tile_columns(cols, source):
            @pl.loop(0, places)
            def _(q):
                for v in range(2):
                    for m in range(micros):
                        row = pl.multiple_of(((q * 2 + v) * micros + m) * HR, HR)
                        picked = dot(tiles_at(q, v, m), source[q, v, m]).astype(BF16)
                        for t in range(TAPS):
                            cols[pl.ds(row, HR), t * 128 : (t + 1) * 128] = picked[
                                t * HR : (t + 1) * HR
                            ]

        def pair_columns(name, source):
            for v in range(2):
                for m in range(micros):
                    select = r.pick[...] if name == "s1" else tiles_at(place, v, m)
                    picked = dot(select, source[v, m]).astype(BF16)
                    for t in range(TAPS):
                        r.h_cols[t, v, m] = picked[t * HR : (t + 1) * HR]

        def flat(value):
            return value.reshape(math.prod(value.shape[:-1]), value.shape[-1])

        def store_blocks(product, tap, begin, value, deep, halving):
            step = min(deep, value.shape[0])
            for b in range(0, value.shape[0], step):
                row = begin + b
                at = pl.ds(row % deep, step)
                block = row // deep
                if halving:
                    product[block // 2, block % 2, tap, at, :] = value[b : b + step]
                else:
                    product[block, tap, at, :] = value[b : b + step]

        def multiply(spec):
            grad = flat(getattr(r, "h_g_" + spec.name)[...])
            product = getattr(r, "p_" + spec.name)
            deep = spec.depth // places
            chunk = min(256, spec.depth)
            if spec.taps == 1:
                left = getattr(r, spec.left)
                for begin in range(0, spec.depth, chunk):
                    value = dot_tn(flat(left[..., begin : begin + chunk]), grad).astype(BF16)
                    store_blocks(product, 0, begin, value, deep, spec.halving)
            else:
                pair_columns(spec.name, getattr(r, spec.left))

                @pl.loop(0, TAPS)
                def _(t):
                    for begin in range(0, spec.depth, chunk):
                        value = dot_tn(
                            flat(r.h_cols[t, :, :, :, begin : begin + chunk]), grad
                        ).astype(BF16)
                        store_blocks(product, t, begin, value, deep, spec.halving)

        def start(index):
            spec = plan.products[index]
            grad = getattr(r, "h_g_" + spec.name)
            wait_bytes(grad, r.g_recv.at[index])
            if spec.gathered:
                source, target = grad, getattr(r, "ga_" + spec.name)
            else:
                multiply(spec)
                source, target = getattr(r, "p_" + spec.name), getattr(r, "two_" + spec.name)
            if spec.halving:
                group.remote(
                    source.at[:, 1 - low], getattr(r, "one_" + spec.name),
                    r.one_recv.at[index], (2 * (place + 1 - 2 * low) + parity, n),
                )
                return
            for q in range(places):
                group.remote(
                    source if spec.gathered else source.at[q], target.at[place],
                    r.two_recv.at[index], (2 * q + parity, n), place != q,
                )
            target[place] = source[...] if spec.gathered else source[place]

        def middle(index):
            spec = plan.products[index]
            if not spec.halving:
                return
            source, one = getattr(r, "p_" + spec.name), getattr(r, "one_" + spec.name)
            wait_bytes(one, r.one_recv.at[index])
            far = source[1 - high, low].astype(F32) + one[1 - high].astype(F32)
            source[1 - high, low] = far.astype(BF16)
            group.remote(
                source.at[1 - high, low], getattr(r, "two_" + spec.name), r.two_recv.at[index],
                (2 * (place + 2 - 4 * high) + parity, n),
            )

        def finish(index):
            spec = plan.products[index]
            rows = spec.rows
            last = getattr(r, "last_" + spec.name)
            target = getattr(r, ("ga_" if spec.gathered else "two_") + spec.name)
            if spec.halving:
                wait_bytes(target, r.two_recv.at[index])
            elif places > 1:
                wait_bytes(target.at[0 : places - 1], r.two_recv.at[index])
            if spec.gathered:
                cols = getattr(r, "cols_" + spec.name)
                value = dot_tn(flat(target[...]), cols[...])
                for t in range(TAPS):
                    tap = value[:, t * 128 : (t + 1) * 128].T
                    for half in range(2):
                        last[half, t] = tap[half * rows : (half + 1) * rows]
            else:
                if spec.halving:
                    value = getattr(r, "p_" + spec.name)[high, low].astype(F32)
                    value = value + getattr(r, "one_" + spec.name)[high].astype(F32)
                    value = value + target[...].astype(F32)
                else:
                    value = target[0].astype(F32)
                    for q in range(1, places):
                        value = value + target[q].astype(F32)
                for half in range(2):
                    part = value[:, half * rows : (half + 1) * rows]
                    last[half] = part if spec.taps > 1 else part[0]
            result = getattr(r, "out_" + spec.name)

            @pl.when(parity == 0)
            def _():
                result[...] = last[0]

            sem = r.w_recv.at[index]
            group.remote(last.at[1], result, sem, (partner, n), parity == 0)
            group.remote(last.at[0], result, sem, (partner, n + 1), parity == 1)
            group.remote(last.at[1], result, sem, (w, n + 1), parity == 1)

        for m in range(micros):
            fetch_image(m, m).start()
        build_picks()
        tile_base()
        for m in range(micros):
            for k in range(2):
                cut = jnp.full((1, 128), r.tile_cuts[0, k, m], jnp.int32).astype(F32)
                r.cuts[place, parity, 2 * m + k : 2 * m + k + 1, :] = cut
        for m in range(micros):
            fetch_image(m, m).wait()
            mask_image(r.h_image.at[parity, m], m, m)
        pass_barrier()
        relay(r.h_image, 0)
        if plan.gather:
            for q in range(places):
                group.remote(
                    r.cuts.at[place, parity], r.cuts.at[place, parity], r.z_recv.at[1],
                    (2 * q + parity, n), place != q,
                )
        else:
            relay(r.cuts.at[place], 1)
        wait_bytes(r.h_act1.at[0], r.h_recv.at[0])
        if plan.gather:
            scatter(r.h_act1.at[0], r.sp_act1, 2)
            forward(r.cuts, 1)
        else:
            relay(r.h_act1, 2)
        wait_bytes(r.h_mix1.at[0], r.h_recv.at[1])
        relay(r.h_mix1, 3)
        if plan.gather:
            forward(r.sp_act1, 2)
        wait_bytes(r.h_low1.at[0], r.h_recv.at[2])
        relay(r.h_low1, 4)
        if plan.gather:
            forwarded(r.sp_act1, 2)
            strided_columns(r.cols_s1, r.sp_act1)
        arrived(r.h_image, 0)
        centre = r.pick[4 * HR : 5 * HR, :]
        for v in range(2):
            for m in range(micros):
                r.h_picked[v, m] = dot(centre, r.h_image[v, m]).astype(BF16)
        wait_bytes(r.h_act2.at[0], r.h_recv.at[3])
        if plan.gather:
            scatter(r.h_act2.at[0], r.sp_act2, 5)
        else:
            relay(r.h_act2, 5)
        wait_bytes(r.h_mix2.at[0], r.h_recv.at[4])
        relay(r.h_mix2, 6)
        if plan.gather:
            forward(r.sp_act2, 5)
            forwarded(r.cuts, 1)
            forwarded(r.sp_act2, 5)
            tile_columns(r.cols_s2, r.sp_act2)
        else:
            arrived(r.cuts.at[0], 1)
            arrived(r.h_act1, 2)
            arrived(r.h_act2, 5)
        arrived(r.h_mix1, 3)
        arrived(r.h_low1, 4)
        arrived(r.h_mix2, 6)

        start(0)
        middle(0)
        start(1)
        start(2)
        middle(2)
        start(4)
        start(3)
        middle(4)
        middle(3)
        start(5)
        start(6)
        finish(0)
        finish(1)
        finish(2)
        finish(4)
        finish(3)
        finish(5)
        finish(6)

        wait_bytes(r.o_final, r.o_recv.at[0])
        wait_bytes(r.o_input, r.o_recv.at[1])
        wait_bytes(r.o_norms, r.o_recv.at[2])
        wait_bytes(r.o_rms, r.o_recv.at[3])
        pl.when(parity == 1)(wait_products)
        group.finish()

    @pl.when(core == 1)
    def _():
        pl.run_scoped(chain, *plan.chain_local)

    @pl.when(core == 0)
    def _():
        pl.run_scoped(helper, *plan.helper_local)

    for m in range(micros):
        r.out_block[m, 0] = r.o_final[m, 0 : HALF * HALF, :]
        r.out_input[m, 0] = r.o_input[m, 0 : FULL * FULL, :]
    norms = r.o_norms[0]
    sums = r.o_rms[0]
    for c in range(1, columns):
        norms = norms + r.o_norms[c]
        sums = sums + r.o_rms[c]
    share_width = allch // (wide * narrow)
    for target in range(narrow):

        @pl.when(n == target)
        def _(target=target):
            piece = norms[:, target * share_width : (target + 1) * share_width]
            r.out_gains[...] = piece[0]
            r.out_biases[...] = piece[1]

    square = jnp.sum(sums[0:4], axis=1, keepdims=True)
    rms = jnp.sqrt(square / (sums[4:5, 0:1] * out))
    for index in range(4):
        r.out_rms[index] = rms[index, 0]


def hand_out(results):
    count = len(results)

    def copies(*refs):
        for i in range(count - 1):
            refs[count + i][...] = refs[i][...]
        for index in range(4):
            refs[2 * count - 1][index] = refs[count - 1][index]

    in_vmem = pl.BlockSpec(memory_space=pltpu.VMEM)
    in_smem = pl.BlockSpec(memory_space=pltpu.SMEM)
    places = (in_vmem,) * (count - 1) + (in_smem,)
    return pl.pallas_call(
        copies,
        out_shape=tuple(jax.ShapeDtypeStruct(v.shape, v.dtype) for v in results),
        in_specs=places,
        out_specs=places,
        name="hand_out",
    )(*results)


def shards(
    inputs, image_sides, tile_cuts, cotangent, w_reduce1, w_spatial1, w_expand1, w_project1,
    w_reduce2, w_spatial2, w_expand2, norm_gains, norm_biases,
):
    wide = lax.axis_size(WIDE)
    narrow = lax.axis_size(NARROW)
    columns = narrow // 2
    micros = inputs.shape[0]
    slots = -(-micros // columns)
    inw, mid = w_reduce1.shape
    out = w_expand1.shape[1]
    allch = norm_gains.shape[0]
    places = wide // 2
    gather = mid // places == 128
    starts = (0, mid, 2 * mid, 2 * mid + out, 2 * mid + 2 * out, 3 * mid + 2 * out,
              4 * mid + 2 * out)
    widths = (mid, mid, out, out, mid, mid, out)

    def product(name, taps, depth, width, left, rows):
        return SimpleNamespace(
            name=name, taps=taps, depth=depth, width=width // narrow, rows=depth // wide,
            left=left, cells=rows, gathered=gather and taps > 1,
            halving=places == 4 and name in HALVING,
        )

    products = (
        product("e2", 1, mid, out, "h_mix2", HR),
        product("s2", TAPS, mid, mid, "h_act2", HR),
        product("r2", 1, out, mid, "h_low1", HR),
        product("e1", 1, mid, out, "h_mix1", HR),
        product("p1", 1, inw, out, "h_picked", HR),
        product("s1", TAPS, mid, mid, "h_act1", HR),
        product("r1", 1, inw, mid, "h_image", FR),
    )
    vmem = pltpu.VMEM
    hbm = pl.BlockSpec(memory_space=pl.ANY)
    in_vmem = pl.BlockSpec(memory_space=pltpu.VMEM)
    in_smem = pl.BlockSpec(memory_space=pltpu.SMEM)

    args = dict(
        inputs=(inputs, hbm),
        image_sides=(image_sides.T, in_smem),
        tile_cuts=(tile_cuts.transpose(1, 2, 0), in_smem),
        cotangent=(cotangent, hbm),
        w_reduce1=(w_reduce1, hbm),
        w_spatial1=(w_spatial1.reshape(TAPS * mid, mid), hbm),
        w_expand1=(w_expand1, hbm),
        w_project1=(w_project1, hbm),
        w_reduce2=(w_reduce2, hbm),
        w_spatial2=(w_spatial2.reshape(TAPS * mid, mid), hbm),
        w_expand2=(w_expand2, hbm),
        gains=(norm_gains.reshape(1, allch), in_vmem),
        biases=(norm_biases.reshape(1, allch), in_vmem),
    )
    share = allch // (wide * narrow)
    outputs = dict(
        out_block=((micros, 1, HALF * HALF, out // narrow), BF16),
        out_input=((micros, 1, FULL * FULL, inw // narrow), BF16),
    )
    for spec in (products[6], products[5], products[3], products[4], products[2], products[1],
                 products[0]):
        shape = (spec.rows, spec.width)
        if spec.taps > 1:
            shape = (spec.taps,) + shape
        outputs["out_" + spec.name] = (shape, F32)
    outputs["out_gains"] = ((share,), F32)
    outputs["out_biases"] = ((share,), F32)
    outputs["out_rms"] = ((4,), F32)

    scratch = dict(
        pick_back=vmem((FR, TAPS * HR), BF16),
        k_reduce1=vmem(w_reduce1.shape, BF16),
        k_spatial1=vmem((TAPS * mid, mid), BF16),
        k_expand1=vmem(w_expand1.shape, BF16),
        k_project1=vmem(w_project1.shape, BF16),
        k_reduce2=vmem(w_reduce2.shape, BF16),
        k_spatial2=vmem((TAPS * mid, mid), BF16),
        k_expand2=vmem(w_expand2.shape, BF16),
        cot_raw=vmem((slots, HALF * HALF, out), BF16),
        half=vmem((slots, HR, 128), F32),
        full=vmem((slots, FR, 128), F32),
        counts=vmem((slots, 128), F32),
        norms=vmem((2 * slots, allch), F32),
        norm_sums=vmem((2, allch), F32),
        squares=vmem((4, mid), F32),
        stage=vmem((16, out // 4), F32),
        sums=vmem((16, out // 4), F32),
        rms_part=vmem((8, mid), F32),
        z0=vmem((slots, FR, mid), F32),
        slope0=vmem((slots, FR, mid), F32),
        act1=vmem((slots, FR, mid), BF16),
        cols=vmem((slots * HR, TAPS * mid), BF16),
        z1=vmem((slots, HR, mid), F32),
        slope1=vmem((slots, HR, mid), F32),
        mix1=vmem((slots, HR, mid), BF16),
        z_branch=vmem((slots, HR, out), F32),
        z_short=vmem((slots, HR, out), F32),
        slope2=vmem((slots, HR, out), F32),
        low1=vmem((slots, HR, out), BF16),
        z3=vmem((slots, HR, mid), F32),
        slope3=vmem((slots, HR, mid), F32),
        act2=vmem((slots, HR, mid), BF16),
        z4=vmem((slots, HR, mid), F32),
        slope4=vmem((slots, HR, mid), F32),
        mix2=vmem((slots, HR, mid), BF16),
        z5=vmem((slots, HR, out), F32),
        u_out=vmem((slots, HR, out), F32),
        u_mid=vmem((slots, HR, mid), F32),
        final=vmem((slots, HR, out), BF16),
        g_e2=vmem((slots, HR, out), BF16),
        g_s2=vmem((slots, HR, mid), BF16),
        g_r2=vmem((slots, HR, mid), BF16),
        g_e1=vmem((slots, HR, out), BF16),
        g_p1=vmem((slots, HR, out), BF16),
        g_s1=vmem((slots, HR, mid), BF16),
        g_r1=vmem((slots, FR, mid), BF16),
        h_act1=vmem((1 if gather else 2, micros, FR, mid), BF16),
        h_mix1=vmem((2, micros, HR, mid), BF16),
        h_low1=vmem((2, micros, HR, out), BF16),
        h_act2=vmem((1 if gather else 2, micros, HR, mid), BF16),
        h_mix2=vmem((2, micros, HR, mid), BF16),
        h_image=vmem((2, micros, FR, inw), BF16),
        cuts=vmem((places, 2, 8, 128), F32),
        o_final=vmem((micros, HR, out // narrow), BF16),
        o_input=vmem((micros, FR, inw // narrow), BF16),
        o_norms=vmem((columns, 2, allch // wide), F32),
        o_rms=vmem((columns, 8, mid), F32),
    )
    stat_rows = (3, 2, 2, 2, 2, 2, 2, 2, 2, 2, 2, 2, 2, 1, 2)
    stat_widths = (mid, mid, out, mid, mid, out, out, mid, mid, out, mid, mid, out, out, mid)
    for step in range(STEPS):
        rows, width = stat_rows[step] * slots, stat_widths[step]
        if step in LOW_STEPS:
            scratch["stat%d" % step] = vmem((wide, 16, rows * width // 16), BF16)
        else:
            scratch["stat%d" % step] = vmem((wide, rows, width), F32)
    helper_local = dict(
        raw=vmem((micros, FULL * FULL, inw), BF16),
        pick=vmem((TAPS * HR, FR), BF16),
        h_picked=vmem((2, micros, HR, inw), BF16),
        t_base=vmem((TAPS * HR, HR), F32),
        t_row=vmem((TAPS * HR, HR), F32),
        t_col=vmem((TAPS * HR, HR), F32),
    )
    if gather:
        scratch["sp_act1"] = vmem((places, 2, micros, FR, 128), BF16)
        scratch["sp_act2"] = vmem((places, 2, micros, HR, 128), BF16)
    else:
        helper_local["h_cols"] = vmem((TAPS, 2, micros, HR, mid), BF16)
    for spec in products:
        name, taps, rows, width = spec.name, spec.taps, spec.rows, spec.width
        scratch["h_g_" + name] = vmem((2, micros, spec.cells, width), BF16)
        if spec.gathered:
            scratch["ga_" + name] = vmem((places, 2, micros, HR, width), BF16)
            helper_local["cols_" + name] = vmem((places * 2 * micros * HR, TAPS * 128), BF16)
        else:
            block = (taps, 2 * rows, width)
            if spec.halving:
                scratch["one_" + name] = vmem((2,) + block, BF16)
                scratch["two_" + name] = vmem(block, BF16)
                helper_local["p_" + name] = vmem((2, 2) + block, BF16)
            else:
                scratch["two_" + name] = vmem((places,) + block, BF16)
                helper_local["p_" + name] = vmem((places,) + block, BF16)
        last = (2, rows, width) if taps == 1 else (2, taps, rows, width)
        helper_local["last_" + name] = vmem(last, F32)
    semaphores = dict(
        fetch=(16,),
        stat_send=(STEPS,),
        stat_recv=(STEPS,),
        chain_sends=(7 * columns * narrow + 5 * columns * columns + 2 * slots * narrow + 2 * narrow,),
        helper_sends=(7 * (places + 3) + 3 * places + 16,),
        h_recv=(5,),
        g_recv=(7,),
        y_recv=(7,),
        z_recv=(7,),
        o_recv=(4,),
        w_recv=(7,),
        one_recv=(7,),
        two_recv=(7,),
    )
    for name, shape in semaphores.items():
        scratch[name] = pltpu.SemaphoreType.DMA(shape)
    shared = ("h_", "o_", "sp", "ga", "cu", "on", "tw")
    chain_local = {name: scratch.pop(name) for name in tuple(scratch)
                   if name not in semaphores and name[:2] not in shared and name[:4] != "stat"}
    chain_local.update(
        raw=vmem((slots, FULL * FULL, inw), BF16),
        image=vmem((slots, FR, inw), BF16),
        picked=vmem((slots * HR, inw), BF16),
        pick=vmem((TAPS * HR, FR), BF16),
        tiles=vmem((slots, TAPS * HR, HR), BF16),
    )
    plan = SimpleNamespace(
        chain_names=tuple(chain_local), chain_local=tuple(chain_local.values()),
        helper_names=tuple(helper_local), helper_local=tuple(helper_local.values()),
        names=tuple(args) + tuple(outputs) + tuple(scratch),
        wide=wide, narrow=narrow, micros=micros, slots=slots,
        mid=mid, out=out, inw=inw, allch=allch,
        gather=gather, layers=tuple(zip(starts, widths)), products=products,
    )
    results = pl.pallas_call(
        functools.partial(kernel, plan),
        out_shape=tuple(jax.ShapeDtypeStruct(s, d) for s, d in outputs.values()),
        in_specs=[spec for _, spec in args.values()],
        out_specs=(in_vmem,) * (len(outputs) - 1) + (in_smem,),
        scratch_shapes=list(scratch.values()),
        compiler_params=pltpu.CompilerParams(
            collective_id=0, has_side_effects=True, vmem_limit_bytes=63 * 2**20 + 2**19
        ),
        name="bottleneck_pair",
    )(*[value for value, _ in args.values()])
    return hand_out(results)


def solution(mesh):
    return jax.shard_map(
        shards,
        mesh=mesh,
        in_specs=(
            P(None, WIDE, None, None),
            P(None, WIDE),
            P(None, WIDE, None),
            P(None, WIDE, None, None),
            P(), P(), P(), P(), P(), P(), P(), P(), P(),
        ),
        out_specs=(
            P(None, WIDE, None, NARROW),
            P(None, WIDE, None, NARROW),
            P(WIDE, NARROW),
            P(None, WIDE, NARROW),
            P(WIDE, NARROW),
            P(WIDE, NARROW),
            P(WIDE, NARROW),
            P(None, WIDE, NARROW),
            P(WIDE, NARROW),
            P((WIDE, NARROW)),
            P((WIDE, NARROW)),
            P(),
        ),
        check_vma=False,
    )
```

```python
import functools
import math
from types import SimpleNamespace

import jax
import jax.numpy as jnp
from jax import lax
from jax.experimental import pallas as pl
from jax.experimental.pallas import tpu as pltpu
from jax.sharding import PartitionSpec as P

MESH = pl.DeviceIdType.MESH
WIDE, NARROW = "wide", "narrow"
BF16 = jnp.bfloat16
F32 = jnp.float32
HALF = 7
FULL = 2 * HALF
EPSILON = 1e-05
C0 = math.sqrt(2.0 / math.pi)
C1 = C0 * 0.044715
HR = 64
FR = 208
TAPS = 9
STEPS = 15
LOW_STEPS = (6, 7, 8, 9, 10, 11, 13)
HALVING = ("p1",)


def dot(a, b):
    return jnp.dot(a, b, preferred_element_type=F32)


def dot_nt(a, b):
    return lax.dot_general(a, b, (((1,), (1,)), ((), ())), preferred_element_type=F32)


def dot_tn(a, b):
    return lax.dot_general(a, b, (((0,), (0,)), ((), ())), preferred_element_type=F32)


def spread(mask, width):
    return jnp.concatenate([mask] * (width // 128), axis=1)


def gelu(v):
    t = jnp.tanh(v * (C0 + C1 * (v * v)))
    h = 0.5 * v
    return h + h * t


def gelu_slope(v):
    v2 = v * v
    t = jnp.tanh(v * (C0 + C1 * v2))
    return 0.5 + 0.5 * t + (0.5 * v) * (1.0 - t * t) * (C0 + (3.0 * C1) * v2)


def column_sum(values):
    return jnp.sum(values, axis=0, keepdims=True)


def half_cell(p):
    i = lax.shift_right_logical(p * 9363, 16)
    return i, p - HALF * i


def full_cell(p):
    i = lax.shift_right_logical(p * 4682, 16)
    return i, p - FULL * i


def tap_of(r):
    t = lax.shift_right_logical(r, 6)
    ta = lax.shift_right_logical(t * 11, 5)
    return ta - 1, t - 3 * ta - 1


def one_zero(condition):
    return jnp.where(condition, 1.0, 0.0)


def strided_pick(rows, cells):
    a, b = tap_of(rows)
    p = lax.bitwise_and(rows, 63)
    i, j = half_cell(p)
    r, c = 2 * i + a, 2 * j + b
    inside = (p < HALF * HALF) & (r >= 0) & (r < FULL) & (c >= 0) & (c < FULL)
    return one_zero(inside & (cells == r * FULL + c)).astype(BF16)


def tile_pick(rows, cells, cut_row, cut_col):
    a, b = tap_of(rows)
    p = lax.bitwise_and(rows, 63)
    i, j = half_cell(p)
    r, c = i + a, j + b
    inside = (p < HALF * HALF) & (r >= 0) & (r < HALF) & (c >= 0) & (c < HALF)
    row_far = one_zero(r >= cut_row) - one_zero(i >= cut_row)
    col_far = one_zero(c >= cut_col) - one_zero(j >= cut_col)
    same = (row_far == 0.0) & (col_far == 0.0)
    return one_zero(inside & same & (cells == r * HALF + c)).astype(BF16)


class Group:
    def __init__(self, sems):
        self.sems = sems
        self.used = 0
        self.items = []

    def sem(self):
        self.used += 1
        return self.sems.at[self.used - 1]

    def remote(self, src, dst, recv_sem, device, when=None):
        copy = pltpu.make_async_remote_copy(
            src_ref=src, dst_ref=dst, send_sem=self.sem(), recv_sem=recv_sem,
            device_id=device, device_id_type=MESH,
        )
        if when is None:
            copy.start()
        else:
            pl.when(when)(copy.start)
        self.items.append((copy, when))

    def finish(self):
        for copy, when in self.items:
            if when is None:
                copy.wait_send()
            else:
                pl.when(when)(copy.wait_send)


def wait_bytes(ref, sem):
    pltpu.make_async_copy(ref, ref, sem).wait()


def kernel(plan, *refs):
    r = SimpleNamespace(**dict(zip(plan.names, refs)))
    r.stat = [getattr(r, "stat%d" % step) for step in range(STEPS)]
    wide, narrow, micros, slots = plan.wide, plan.narrow, plan.micros, plan.slots
    mid, out, inw, allch = plan.mid, plan.out, plan.inw, plan.allch
    places = wide // 2
    columns = narrow // 2
    layers = plan.layers
    w = lax.axis_index(WIDE)
    n = lax.axis_index(NARROW)
    x = n // 2
    core = n % 2
    first_micro = x * slots
    fetch = r.fetch
    parity = w % 2
    place = w // 2
    partner = w + 1 - 2 * parity
    own_act = 0 if plan.gather else parity

    def micro_of(s):
        return lax.rem(first_micro + s, micros)

    barrier = pltpu.get_barrier_semaphore()

    @pl.loop(1, wide)
    def _(d):
        pl.semaphore_signal(
            barrier, inc=1, device_id=(lax.rem(w + d, wide), n), device_id_type=MESH
        )

    for d in range(1, narrow):
        pl.semaphore_signal(
            barrier, inc=1, device_id=(w, lax.rem(n + d, narrow)), device_id_type=MESH
        )

        pl.semaphore_signal(
            barrier, inc=1, device_id=(partner, lax.rem(n + d, narrow)), device_id_type=MESH
        )

    def pass_barrier():
        pl.semaphore_wait(barrier, wide - 1 + 2 * (narrow - 1))

    def build_picks():
        rows = lax.broadcasted_iota(jnp.int32, (TAPS * HR, FR), 0)
        cells = lax.broadcasted_iota(jnp.int32, (TAPS * HR, FR), 1)
        r.pick[...] = strided_pick(rows, cells)

    def build_pick_back():
        rows = lax.broadcasted_iota(jnp.int32, (FR, TAPS * HR), 1)
        cells = lax.broadcasted_iota(jnp.int32, (FR, TAPS * HR), 0)
        r.pick_back[...] = strided_pick(rows, cells)

    def build_tiles(slot, micro):
        rows = lax.broadcasted_iota(jnp.int32, (TAPS * HR, HR), 0)
        cells = lax.broadcasted_iota(jnp.int32, (TAPS * HR, HR), 1)
        r.tiles[slot] = tile_pick(
            rows, cells, r.tile_cuts[0, 0, micro], r.tile_cuts[0, 1, micro]
        )

    def full_mask(micro):
        row, col = full_cell(lax.broadcasted_iota(jnp.int32, (FR, 128), 0))
        limit = 2 * r.image_sides[0, micro]
        return one_zero((row < limit) & (col < limit))

    def half_mask(micro):
        row, col = half_cell(lax.broadcasted_iota(jnp.int32, (HR, 128), 0))
        limit = r.image_sides[0, micro]
        return one_zero((row < limit) & (col < limit))

    def fetch_image(slot, micro):
        return pltpu.make_async_copy(r.inputs.at[micro, 0], r.raw.at[slot], fetch.at[slot])

    def mask_image(target, slot, micro):
        mask = full_mask(micro)
        raw = jnp.concatenate(
            [r.raw[slot].astype(F32), jnp.zeros((FR - FULL * FULL, inw), F32)], axis=0
        )
        target[...] = (raw * spread(mask, inw)).astype(BF16)

    def chain(*local):
        r.__dict__.update(zip(plan.chain_names, local))
        group = Group(r.chain_sends)
        weights = (
            (r.w_reduce1, r.k_reduce1), (r.w_spatial1, r.k_spatial1), (r.w_project1, r.k_project1),
            (r.w_expand1, r.k_expand1), (r.w_reduce2, r.k_reduce2), (r.w_spatial2, r.k_spatial2),
            (r.w_expand2, r.k_expand2),
        )

        def fetch_weight(index):
            return pltpu.make_async_copy(*weights[index], fetch.at[4 + index])

        fetch_image(0, micro_of(0)).start()
        fetch_weight(0).start()
        for s in range(1, slots):
            fetch_image(s, micro_of(s)).start()
        for index in range(1, 7):
            fetch_weight(index).start()

        def fetch_cotangent(s):
            return pltpu.make_async_copy(
                r.cotangent.at[micro_of(s), 0], r.cot_raw.at[s], fetch.at[11 + s]
            )

        for s in range(slots):
            fetch_cotangent(s).start()
            r.half[s] = half_mask(micro_of(s))
            r.full[s] = full_mask(micro_of(s))

        def send_stats(step):
            stat = r.stat[step]

            @pl.loop(0, wide)
            def _(d):
                p = lax.rem(wide - 1 - w + d, wide)

                @pl.when(p != w)
                def _():
                    pltpu.make_async_remote_copy(
                        src_ref=stat.at[w], dst_ref=stat.at[w],
                        send_sem=r.stat_send.at[step], recv_sem=r.stat_recv.at[step],
                        device_id=(p, n), device_id_type=MESH,
                    ).start()

        def wait_stats(step):
            stat = r.stat[step]
            wait_bytes(stat.at[pl.ds(0, wide - 1)], r.stat_recv.at[step])

        def total(step, row, begin=0, width=None):
            stat = r.stat[step]
            width = stat.shape[2] if width is None else width
            part = stat[0, row : row + 1, begin : begin + width]
            for j in range(1, wide):
                part = part + stat[j, row : row + 1, begin : begin + width]
            return part

        def put(step, row, value, begin=0):
            r.stat[step][w, row : row + 1, begin : begin + value.shape[1]] = value

        def put_pair(step, s, values, begin=0):
            put(step, 2 * s, column_sum(values), begin)
            put(step, 2 * s + 1, column_sum(values * values), begin)

        def put_low(row, rows, value):
            folds = 16 // rows
            part = value.shape[1] // folds
            for k in range(folds):
                at = row * folds + k
                r.stage[at : at + 1, 0:part] = value[:, k * part : (k + 1) * part]

        def send_low(step):
            width = r.stat[step].shape[2]
            r.stat[step][w] = r.stage[:, 0:width].astype(BF16)
            send_stats(step)

        def wait_low(step):
            wait_stats(step)
            width = r.stat[step].shape[2]
            part = r.stat[step][0].astype(F32)
            for j in range(1, wide):
                part = part + r.stat[step][j].astype(F32)
            r.sums[:, 0:width] = part

        def low_total(step, row, rows):
            folds = 16 // rows
            width = r.stat[step].shape[2]
            first = row * folds
            return jnp.concatenate(
                [r.sums[first + k : first + k + 1, 0:width] for k in range(folds)], axis=1
            )

        def inverse_count(s, layer):
            count = r.counts[s : s + 1, 0:1]
            return 1.0 / (count * (4.0 if layer == 0 else 1.0))

        def settle(s, layer, step, begin=0):
            start, width = layers[layer]
            inv_n = inverse_count(s, layer)
            mean = total(step, 2 * s, begin, width) * inv_n
            square = total(step, 2 * s + 1, begin, width) * inv_n
            inv = lax.rsqrt(square - mean * mean + EPSILON)
            scale = r.gains[:, start : start + width] * inv
            r.norms[2 * s : 2 * s + 1, start : start + width] = inv
            r.norms[2 * s + 1 : 2 * s + 2, start : start + width] = -mean * inv
            return scale, r.biases[:, start : start + width] - mean * scale

        def kept(s, layer):
            start, width = layers[layer]
            gain = r.gains[:, start : start + width]
            inv = r.norms[2 * s : 2 * s + 1, start : start + width]
            offset = r.norms[2 * s + 1 : 2 * s + 2, start : start + width]
            return inv, offset, gain * inv, r.biases[:, start : start + width] + gain * offset

        def normed(s, layer, z):
            inv, offset, _, _ = kept(s, layer)
            return z * inv + offset

        def activation(s, layer, z):
            _, _, scale, shift = kept(s, layer)
            return z * scale + shift

        def settle_back(s, layer, step, sum_u=None, sum_g=None):
            start, width = layers[layer]
            sum_u = low_total(step, 2 * s, 2 * slots) if sum_u is None else sum_u
            sum_g = low_total(step, 2 * s + 1, 2 * slots) if sum_g is None else sum_g
            live = jnp.where(first_micro + s < micros, 1.0, 0.0)
            for row, value in ((0, sum_g), (1, sum_u)):
                if s == 0:
                    r.norm_sums[row : row + 1, start : start + width] = value
                else:
                    r.norm_sums[row : row + 1, start : start + width] += live * value
            inv_n = inverse_count(s, layer)
            inv, offset, k0, _ = kept(s, layer)
            k2 = -k0 * (sum_g * inv_n)
            return k0, -k0 * (sum_u * inv_n) + k2 * offset, k2 * inv

        def live_row(s, row):
            if s == 0:
                return row
            return row * jnp.where(first_micro + s < micros, 1.0, 0.0)

        def fold_row(row):
            parts = [row[:, c : c + mid] for c in range(0, row.shape[1], mid)]
            return functools.reduce(lambda a, b: a + b, parts)

        def add_squares(s, index, values):
            row = live_row(s, fold_row(column_sum(values)))
            if s == 0:
                r.squares[index : index + 1, :] = row
            else:
                r.squares[index : index + 1, :] += row

        def share(src, dst, recv_sem):
            for c in range(columns):
                amount = min(slots, micros - c * slots)
                for h in range(columns if amount > 0 else 0):
                    group.remote(
                        src.at[0:amount], dst.at[c * slots : c * slots + amount], recv_sem,
                        (w, 2 * h), x == c,
                    )

        def share_grad(src, index):
            spec = plan.products[index]
            dst = getattr(r, "h_g_" + spec.name)
            for c in range(columns):
                amount = min(slots, micros - c * slots)
                for quarter in range(narrow if amount > 0 else 0):
                    h, v = quarter // 2, quarter % 2
                    group.remote(
                        src.at[0:amount, :, quarter * spec.width : (quarter + 1) * spec.width],
                        dst.at[parity, c * slots : c * slots + amount], r.g_recv.at[index],
                        (w - parity + v, 2 * h), x == c,
                    )

        def rows2(ref):
            value = ref[...]
            return value.reshape(value.shape[0] * value.shape[1], value.shape[2])

        def set_rows(ref, value):
            ref[...] = value.reshape(ref.shape)

        def rows_of(value, s, count=HR):
            return value[s * count : (s + 1) * count]

        def gather_tiles(s, value, select):
            picked = dot(select, value).astype(BF16)
            for t in range(TAPS):
                r.cols[s * HR : (s + 1) * HR, t * mid : (t + 1) * mid] = picked[
                    t * HR : (t + 1) * HR
                ]

        def half_wide(s, width):
            return spread(r.half[s], width)

        for s in range(slots):
            fetch_image(s, micro_of(s)).wait()
            mask_image(r.image.at[s], s, micro_of(s))
        fetch_weight(0).wait()
        for s in range(slots):
            z = dot(r.image[s], r.k_reduce1[...])
            r.z0[s] = z
            put_pair(0, s, z)
            side = r.image_sides[0, micro_of(s)]
            area = jnp.full((1, mid), side * side, jnp.int32).astype(F32)
            put(0, 2 * slots + s, area)
        build_picks()
        pass_barrier()
        send_stats(0)
        for s in range(slots):
            build_tiles(s, micro_of(s))
        centre = r.pick[4 * HR : 5 * HR, :]
        for s in range(slots):
            r.picked[s * HR : (s + 1) * HR, :] = dot(centre, r.image[s]).astype(BF16)
        fetch_weight(1).wait()
        wait_stats(0)
        for s in range(slots):
            r.counts[s : s + 1, :] = total(0, 2 * slots + s, 0, 128)

        for s in range(slots):
            scale, shift = settle(s, 0, 0)
            act = gelu(r.z0[s] * scale + shift) * spread(r.full[s], mid)
            act = act.astype(BF16)
            r.act1[s] = act
            gather_tiles(s, act, r.pick[...])
        z = dot(r.cols[...], r.k_spatial1[...])
        for s in range(slots):
            r.z1[s] = rows_of(z, s)
            put_pair(1, s, rows_of(z, s) * half_wide(s, mid))
        send_stats(1)
        share(r.act1, r.h_act1.at[own_act], r.h_recv.at[0])
        fetch_weight(2).wait()
        set_rows(r.z_short, dot(r.picked[...], r.k_project1[...]))
        for s in range(slots):
            put_pair(12, s, r.z_short[s])
        send_stats(12)
        for s in range(slots):
            r.slope0[s] = gelu_slope(activation(s, 0, r.z0[s])) * spread(r.full[s], mid)
        fetch_weight(3).wait()
        wait_stats(1)

        for s in range(slots):
            scale, shift = settle(s, 1, 1)
            mixed = gelu(r.z1[s] * scale + shift) * half_wide(s, mid)
            r.mix1[s] = mixed.astype(BF16)
        z = dot(rows2(r.mix1), r.k_expand1[...])
        for s in range(slots):
            r.z_branch[s] = rows_of(z, s)
            put_pair(2, s, rows_of(z, s))
        send_stats(2)
        share(r.mix1, r.h_mix1.at[parity], r.h_recv.at[1])
        for s in range(slots):
            r.slope1[s] = gelu_slope(activation(s, 1, r.z1[s])) * half_wide(s, mid)
        fetch_weight(4).wait()
        wait_stats(12)
        wait_stats(2)

        for s in range(slots):
            scale, shift = settle(s, 2, 2)
            scale_short, shift_short = settle(s, 3, 12)
            joined = (r.z_branch[s] * scale + shift) + (
                r.z_short[s] * scale_short + shift_short
            )
            r.slope2[s] = joined
            block = gelu(joined) * half_wide(s, out)
            r.low1[s] = block.astype(BF16)
        z = dot(rows2(r.low1), r.k_reduce2[...])
        for s in range(slots):
            r.z3[s] = rows_of(z, s)
            put_pair(3, s, rows_of(z, s))
        send_stats(3)
        share(r.low1, r.h_low1.at[parity], r.h_recv.at[2])
        for s in range(slots):
            mask = half_wide(s, out)
            branch = activation(s, 2, r.z_branch[s])
            joined = r.slope2[s]
            add_squares(s, 0, branch * branch * mask)
            block = gelu(joined) * mask
            add_squares(s, 1, block * block)
            r.slope2[s] = gelu_slope(joined) * mask
        fetch_weight(5).wait()
        wait_stats(3)

        for s in range(slots):
            scale, shift = settle(s, 4, 3)
            act = gelu(r.z3[s] * scale + shift) * half_wide(s, mid)
            act = act.astype(BF16)
            r.act2[s] = act
            gather_tiles(s, act, r.tiles[s])
        z = dot(r.cols[...], r.k_spatial2[...])
        for s in range(slots):
            r.z4[s] = rows_of(z, s)
            put_pair(4, s, rows_of(z, s) * half_wide(s, mid))
        send_stats(4)
        share(r.act2, r.h_act2.at[own_act], r.h_recv.at[3])
        for s in range(slots):
            r.slope3[s] = gelu_slope(activation(s, 4, r.z3[s])) * half_wide(s, mid)
        fetch_weight(6).wait()
        wait_stats(4)

        for s in range(slots):
            scale, shift = settle(s, 5, 4)
            mixed = gelu(r.z4[s] * scale + shift) * half_wide(s, mid)
            r.mix2[s] = mixed.astype(BF16)
        z = dot(rows2(r.mix2), r.k_expand2[...])
        for s in range(slots):
            r.z5[s] = rows_of(z, s)
            put_pair(5, s, rows_of(z, s))
        send_stats(5)
        share(r.mix2, r.h_mix2.at[parity], r.h_recv.at[4])
        for s in range(slots):
            r.slope4[s] = gelu_slope(activation(s, 5, r.z4[s])) * half_wide(s, mid)
            fetch_cotangent(s).wait()
        wait_stats(5)

        for s in range(slots):
            scale, shift = settle(s, 6, 5)
            joined = (r.z5[s] * scale + shift) + r.low1[s].astype(F32)
            cot = jnp.concatenate(
                [r.cot_raw[s].astype(F32), jnp.zeros((HR - HALF * HALF, out), F32)], axis=0
            )
            u = gelu_slope(joined) * cot * half_wide(s, out)
            r.u_out[s] = u
            put_low(2 * s, 2 * slots, column_sum(u))
            put_low(2 * s + 1, 2 * slots, column_sum(u * normed(s, 6, r.z5[s])))
        send_low(6)
        for s in range(slots):
            mask = half_wide(s, out)
            branch = activation(s, 6, r.z5[s])
            add_squares(s, 2, branch * branch * mask)
            block = gelu(branch + r.low1[s].astype(F32)) * mask
            add_squares(s, 3, block * block)
            r.final[s] = block.astype(BF16)
        part = out // narrow
        for s in range(slots):
            for target in range(narrow):
                src = r.final.at[s, :, target * part : (target + 1) * part]
                dst = r.o_final.at[first_micro + s]
                group.remote(
                    src, dst, r.o_recv.at[0], (w, target),
                    (first_micro + s < micros) & (n != target),
                )
        r.stat[14][w] = r.squares[...]
        send_stats(14)
        wait_low(6)

        for s in range(slots):
            k0, k1, k2 = settle_back(s, 6, 6)
            grad = (k0 * r.u_out[s] + k1 + k2 * r.z5[s]) * half_wide(s, out)
            r.g_e2[s] = grad.astype(BF16)
        back = dot_nt(rows2(r.g_e2), r.k_expand2[...]).astype(BF16).astype(F32)
        for s in range(slots):
            u = rows_of(back, s) * r.slope4[s]
            r.u_mid[s] = u
            put_low(2 * s, 2 * slots, column_sum(u))
            put_low(2 * s + 1, 2 * slots, column_sum(u * normed(s, 5, r.z4[s])))
        send_low(7)
        share_grad(r.g_e2, 0)
        wait_low(7)
        wait_stats(14)
        for index in range(4):
            r.rms_part[index : index + 1, :] = total(14, index)
        count = r.counts[0:1, :]
        for s in range(1, slots):
            count = count + live_row(s, r.counts[s : s + 1, :])
        r.rms_part[4:5, :] = spread(count, mid)

        for s in range(slots):
            k0, k1, k2 = settle_back(s, 5, 7)
            grad = (k0 * r.u_mid[s] + k1 + k2 * r.z4[s]) * half_wide(s, mid)
            r.g_s2[s] = grad.astype(BF16)
            gather_tiles(s, r.g_s2[s], r.tiles[s])
        back = None
        for t in range(TAPS):
            back_tap = dot_nt(
                r.cols[:, t * mid : (t + 1) * mid],
                r.k_spatial2[(8 - t) * mid : (9 - t) * mid, :],
            )
            back = back_tap if back is None else back + back_tap
        back = back.astype(BF16).astype(F32)
        for s in range(slots):
            u = rows_of(back, s) * r.slope3[s]
            r.u_mid[s] = u
            put_low(2 * s, 2 * slots, column_sum(u))
            put_low(2 * s + 1, 2 * slots, column_sum(u * normed(s, 4, r.z3[s])))
        send_low(8)
        share_grad(r.g_s2, 1)
        wait_low(8)

        for s in range(slots):
            k0, k1, k2 = settle_back(s, 4, 8)
            grad = (k0 * r.u_mid[s] + k1 + k2 * r.z3[s]) * half_wide(s, mid)
            r.g_r2[s] = grad.astype(BF16)
        back = dot_nt(rows2(r.g_r2), r.k_reduce2[...])
        for s in range(slots):
            u = (rows_of(back, s) + r.u_out[s].astype(BF16).astype(F32)) * r.slope2[s]
            r.u_out[s] = u
            put_low(2 * s, 2 * slots, column_sum(u))
            put_low(2 * s + 1, 2 * slots, column_sum(u * normed(s, 2, r.z_branch[s])))
        send_low(9)
        for s in range(slots):
            put_low(s, slots, column_sum(r.u_out[s] * normed(s, 3, r.z_short[s])))
        send_low(13)
        share_grad(r.g_r2, 2)
        wait_low(9)

        for s in range(slots):
            k0, k1, k2 = settle_back(s, 2, 9)
            grad = (k0 * r.u_out[s] + k1 + k2 * r.z_branch[s]) * half_wide(s, out)
            r.g_e1[s] = grad.astype(BF16)
        back = dot_nt(rows2(r.g_e1), r.k_expand1[...]).astype(BF16).astype(F32)
        for s in range(slots):
            u = rows_of(back, s) * r.slope1[s]
            r.u_mid[s] = u
            put_low(2 * s, 2 * slots, column_sum(u))
            put_low(2 * s + 1, 2 * slots, column_sum(u * normed(s, 1, r.z1[s])))
        send_low(10)
        sums_u = [low_total(9, 2 * s, 2 * slots) for s in range(slots)]
        wait_low(13)
        for s in range(slots):
            k0, k1, k2 = settle_back(s, 3, 13, sums_u[s], low_total(13, s, slots))
            grad = (k0 * r.u_out[s] + k1 + k2 * r.z_short[s]) * half_wide(s, out)
            r.g_p1[s] = grad.astype(BF16)
        share_grad(r.g_p1, 4)
        share_grad(r.g_e1, 3)
        build_pick_back()
        r.picked[...] = dot_nt(rows2(r.g_p1), r.k_project1[...]).astype(
            BF16
        )
        wait_low(10)

        for s in range(slots):
            k0, k1, k2 = settle_back(s, 1, 10)
            grad = (k0 * r.u_mid[s] + k1 + k2 * r.z1[s]) * half_wide(s, mid)
            r.g_s1[s] = grad.astype(BF16)
        g_rows = rows2(r.g_s1)
        for t in range(TAPS):
            r.cols[:, t * mid : (t + 1) * mid] = dot_nt(
                g_rows, r.k_spatial1[t * mid : (t + 1) * mid, :]
            ).astype(BF16)
        for s in range(slots):
            back = jnp.concatenate(
                [r.cols[s * HR : (s + 1) * HR, t * mid : (t + 1) * mid] for t in range(TAPS)],
                axis=0,
            )
            u = dot(r.pick_back[...], back) * r.slope0[s]
            r.slope0[s] = u
            put_low(2 * s, 2 * slots, column_sum(u))
            put_low(2 * s + 1, 2 * slots, column_sum(u * normed(s, 0, r.z0[s])))
        send_low(11)
        share_grad(r.g_s1, 5)
        wait_low(11)

        for s in range(slots):
            k0, k1, k2 = settle_back(s, 0, 11)
            grad = (k0 * r.slope0[s] + k1 + k2 * r.z0[s]) * spread(r.full[s], mid)
            r.g_r1[s] = grad.astype(BF16)
        share_grad(r.g_r1, 6)
        section = allch // wide
        own = pl.ds(pl.multiple_of(w * section, 128), section)
        for target in range(narrow):
            group.remote(
                r.norm_sums.at[:, own], r.o_norms.at[x], r.o_recv.at[2], (w, target),
                n != target,
            )
            group.remote(
                r.rms_part, r.o_rms.at[x], r.o_recv.at[3], (w, target), n != target
            )
        r.o_norms[x] = r.norm_sums[:, own]
        r.o_rms[x] = r.rms_part[...]
        for s in range(slots):
            grad = dot_nt(r.g_r1[s], r.k_reduce1[...])
            grad = grad + dot(
                r.pick_back[:, 4 * HR : 5 * HR], r.picked[s * HR : (s + 1) * HR, :]
            )
            r.image[s] = grad.astype(BF16)
        part = inw // narrow
        for s in range(slots):
            for target in range(narrow):
                group.remote(
                    r.image.at[s, :, target * part : (target + 1) * part],
                    r.o_input.at[first_micro + s], r.o_recv.at[1], (w, target),
                    (first_micro + s < micros) & (n != target),
                )
        for s in range(slots):
            for target in range(narrow):

                @pl.when((n == target) & (first_micro + s < micros))
                def _(s=s, target=target):
                    wide_part = out // narrow
                    r.o_final[first_micro + s] = r.final[
                        s, :, target * wide_part : (target + 1) * wide_part
                    ]
                    r.o_input[first_micro + s] = r.image[
                        s, :, target * part : (target + 1) * part
                    ]

        for c in range(columns):
            amount = min(slots, micros - c * slots)
            others = micros - max(amount, 0)

            @pl.when(x == c)
            def _(others=others):
                wait_bytes(r.o_final.at[0:others], r.o_recv.at[0])
                wait_bytes(r.o_input.at[0:others], r.o_recv.at[1])

        wait_bytes(r.o_norms.at[0 : columns - 1], r.o_recv.at[2])
        wait_bytes(r.o_rms.at[0 : columns - 1], r.o_recv.at[3])
        wait_products()
        group.finish()
        for step in range(STEPS):
            wait_bytes(r.stat[step].at[pl.ds(0, wide - 1)], r.stat_send.at[step])

    def wait_products():
        for index, spec in enumerate(plan.products):
            landing = getattr(r, "d_" + spec.name)
            wait_bytes(landing, r.w_recv.at[index])
            getattr(r, "out_" + spec.name)[...] = landing[...].astype(F32)

    def helper(*local):
        r.__dict__.update(zip(plan.helper_names, local))
        group = Group(r.helper_sends)
        low, high = place % 2, place // 2

        def relay(ref, sem):
            group.remote(ref.at[parity], ref.at[parity], r.y_recv.at[sem], (partner, n))

        def arrived(ref, sem):
            wait_bytes(ref.at[0], r.y_recv.at[sem])

        def scatter(src, dst, sem):
            for q in range(places):
                part = src.at[:, :, q * 128 : (q + 1) * 128]
                group.remote(
                    part, dst.at[place, parity], r.z_recv.at[sem], (2 * q + parity, n), place != q
                )

                @pl.when(place == q)
                def _(q=q):
                    dst[q, parity] = src[:, :, q * 128 : (q + 1) * 128]

        def forward(ref, sem):
            if places > 1:
                wait_bytes(ref.at[0 : places - 1, 0], r.z_recv.at[sem])
            group.remote(
                ref.at[:, parity], ref.at[:, parity], r.y_recv.at[sem], (partner, n)
            )

        def forwarded(ref, sem):
            wait_bytes(ref.at[:, 0], r.y_recv.at[sem])

        def tile_base():
            rows = lax.broadcasted_iota(jnp.int32, (TAPS * HR, HR), 0)
            cells = lax.broadcasted_iota(jnp.int32, (TAPS * HR, HR), 1)
            a, b = tap_of(rows)
            p = lax.bitwise_and(rows, 63)
            i, j = half_cell(p)
            ti, tj = i + a, j + b
            inside = (p < HALF * HALF) & (ti >= 0) & (ti < HALF) & (tj >= 0) & (tj < HALF)
            r.t_base[...] = one_zero(inside & (cells == ti * HALF + tj))
            r.t_row[...] = jnp.where(a != 0, jnp.maximum(i, ti), -1).astype(F32)
            r.t_col[...] = jnp.where(b != 0, jnp.maximum(j, tj), -1).astype(F32)

        def tiles_at(q, v, m):
            keep = (r.t_row[...] != r.cuts[q, v, 2 * m : 2 * m + 1, 0:HR]) & (
                r.t_col[...] != r.cuts[q, v, 2 * m + 1 : 2 * m + 2, 0:HR]
            )
            return jnp.where(keep, r.t_base[...], 0.0).astype(BF16)

        def strided_columns(cols, source):
            @pl.loop(0, places)
            def _(q):
                for v in range(2):
                    grids = jnp.concatenate([source[q, v, m] for m in range(micros)], axis=1)
                    picked = dot(r.pick[...], grids).astype(BF16)
                    for m in range(micros):
                        row = pl.multiple_of(((q * 2 + v) * micros + m) * HR, HR)
                        for t in range(TAPS):
                            cols[pl.ds(row, HR), t * 128 : (t + 1) * 128] = picked[
                                t * HR : (t + 1) * HR, m * 128 : (m + 1) * 128
                            ]

        def tile_columns(cols, source):
            @pl.loop(0, places)
            def _(q):
                for v in range(2):
                    for m in range(micros):
                        row = pl.multiple_of(((q * 2 + v) * micros + m) * HR, HR)
                        picked = dot(tiles_at(q, v, m), source[q, v, m]).astype(BF16)
                        for t in range(TAPS):
                            cols[pl.ds(row, HR), t * 128 : (t + 1) * 128] = picked[
                                t * HR : (t + 1) * HR
                            ]

        def pair_columns(name, source):
            for v in range(2):
                for m in range(micros):
                    select = r.pick[...] if name == "s1" else tiles_at(place, v, m)
                    picked = dot(select, source[v, m]).astype(BF16)
                    for t in range(TAPS):
                        r.h_cols[t, v, m] = picked[t * HR : (t + 1) * HR]

        def flat(value):
            return value.reshape(math.prod(value.shape[:-1]), value.shape[-1])

        def store_blocks(product, tap, begin, value, deep, halving):
            step = min(deep, value.shape[0])
            for b in range(0, value.shape[0], step):
                row = begin + b
                at = pl.ds(row % deep, step)
                block = row // deep
                if halving:
                    product[block // 2, block % 2, tap, at, :] = value[b : b + step]
                else:
                    product[block, tap, at, :] = value[b : b + step]

        def multiply(spec):
            grad = flat(getattr(r, "h_g_" + spec.name)[...])
            product = getattr(r, "p_" + spec.name)
            deep = spec.depth // places
            chunk = min(256, spec.depth)
            if spec.taps == 1:
                left = getattr(r, spec.left)
                for begin in range(0, spec.depth, chunk):
                    value = dot_tn(flat(left[..., begin : begin + chunk]), grad).astype(BF16)
                    store_blocks(product, 0, begin, value, deep, spec.halving)
            else:
                pair_columns(spec.name, getattr(r, spec.left))

                @pl.loop(0, TAPS)
                def _(t):
                    for begin in range(0, spec.depth, chunk):
                        value = dot_tn(
                            flat(r.h_cols[t, :, :, :, begin : begin + chunk]), grad
                        ).astype(BF16)
                        store_blocks(product, t, begin, value, deep, spec.halving)

        def start(index):
            spec = plan.products[index]
            grad = getattr(r, "h_g_" + spec.name)
            wait_bytes(grad, r.g_recv.at[index])
            if spec.gathered:
                source, target = grad, getattr(r, "ga_" + spec.name)
            else:
                multiply(spec)
                source, target = getattr(r, "p_" + spec.name), getattr(r, "two_" + spec.name)
            if spec.halving:
                group.remote(
                    source.at[:, 1 - low], getattr(r, "one_" + spec.name),
                    r.one_recv.at[index], (2 * (place + 1 - 2 * low) + parity, n),
                )
                return
            for q in range(places):
                group.remote(
                    source if spec.gathered else source.at[q], target.at[place],
                    r.two_recv.at[index], (2 * q + parity, n), place != q,
                )
            target[place] = source[...] if spec.gathered else source[place]

        def middle(index):
            spec = plan.products[index]
            if not spec.halving:
                return
            source, one = getattr(r, "p_" + spec.name), getattr(r, "one_" + spec.name)
            wait_bytes(one, r.one_recv.at[index])
            far = source[1 - high, low].astype(F32) + one[1 - high].astype(F32)
            source[1 - high, low] = far.astype(BF16)
            group.remote(
                source.at[1 - high, low], getattr(r, "two_" + spec.name), r.two_recv.at[index],
                (2 * (place + 2 - 4 * high) + parity, n),
            )

        def finish(index):
            spec = plan.products[index]
            rows = spec.rows
            last = getattr(r, "last_" + spec.name)
            target = getattr(r, ("ga_" if spec.gathered else "two_") + spec.name)
            if spec.halving:
                wait_bytes(target, r.two_recv.at[index])
            elif places > 1:
                wait_bytes(target.at[0 : places - 1], r.two_recv.at[index])
            result = getattr(r, "out_" + spec.name)
            landing = getattr(r, "d_" + spec.name)

            def keep(half, part, at=Ellipsis):
                last[(half,) if at is Ellipsis else (half, at)] = part.astype(BF16)
                if half == 0:

                    @pl.when(parity == 0)
                    def _():
                        result[at] = part

            if spec.gathered:
                cols = getattr(r, "cols_" + spec.name)
                value = dot_tn(flat(target[...]), cols[...])
                for t in range(TAPS):
                    tap = value[:, t * 128 : (t + 1) * 128].T
                    for half in range(2):
                        keep(half, tap[half * rows : (half + 1) * rows], t)
            else:
                if spec.halving:
                    value = getattr(r, "p_" + spec.name)[high, low].astype(F32)
                    value = value + getattr(r, "one_" + spec.name)[high].astype(F32)
                    value = value + target[...].astype(F32)
                else:
                    value = target[0].astype(F32)
                    for q in range(1, places):
                        value = value + target[q].astype(F32)
                for half in range(2):
                    part = value[:, half * rows : (half + 1) * rows]
                    keep(half, part if spec.taps > 1 else part[0])

            sem = r.w_recv.at[index]
            group.remote(last.at[1], landing, sem, (partner, n), parity == 0)
            group.remote(last.at[0], landing, sem, (partner, n + 1), parity == 1)
            group.remote(last.at[1], landing, sem, (w, n + 1), parity == 1)

        for m in range(micros):
            fetch_image(m, m).start()
        build_picks()
        tile_base()
        for m in range(micros):
            for k in range(2):
                cut = jnp.full((1, 128), r.tile_cuts[0, k, m], jnp.int32).astype(F32)
                r.cuts[place, parity, 2 * m + k : 2 * m + k + 1, :] = cut
        for m in range(micros):
            fetch_image(m, m).wait()
            mask_image(r.h_image.at[parity, m], m, m)
        pass_barrier()
        relay(r.h_image, 0)
        if plan.gather:
            for q in range(places):
                group.remote(
                    r.cuts.at[place, parity], r.cuts.at[place, parity], r.z_recv.at[1],
                    (2 * q + parity, n), place != q,
                )
        else:
            relay(r.cuts.at[place], 1)
        wait_bytes(r.h_act1.at[0], r.h_recv.at[0])
        if plan.gather:
            scatter(r.h_act1.at[0], r.sp_act1, 2)
            forward(r.cuts, 1)
        else:
            relay(r.h_act1, 2)
        wait_bytes(r.h_mix1.at[0], r.h_recv.at[1])
        relay(r.h_mix1, 3)
        if plan.gather:
            forward(r.sp_act1, 2)
        wait_bytes(r.h_low1.at[0], r.h_recv.at[2])
        relay(r.h_low1, 4)
        if plan.gather:
            forwarded(r.sp_act1, 2)
            strided_columns(r.cols_s1, r.sp_act1)
        arrived(r.h_image, 0)
        centre = r.pick[4 * HR : 5 * HR, :]
        for v in range(2):
            for m in range(micros):
                r.h_picked[v, m] = dot(centre, r.h_image[v, m]).astype(BF16)
        wait_bytes(r.h_act2.at[0], r.h_recv.at[3])
        if plan.gather:
            scatter(r.h_act2.at[0], r.sp_act2, 5)
        else:
            relay(r.h_act2, 5)
        wait_bytes(r.h_mix2.at[0], r.h_recv.at[4])
        relay(r.h_mix2, 6)
        if plan.gather:
            forward(r.sp_act2, 5)
            forwarded(r.cuts, 1)
            forwarded(r.sp_act2, 5)
            tile_columns(r.cols_s2, r.sp_act2)
        else:
            arrived(r.cuts.at[0], 1)
            arrived(r.h_act1, 2)
            arrived(r.h_act2, 5)
        arrived(r.h_mix1, 3)
        arrived(r.h_low1, 4)
        arrived(r.h_mix2, 6)

        start(0)
        start(1)
        start(2)
        start(4)
        start(3)
        middle(4)
        start(5)
        finish(0)
        finish(1)
        finish(2)
        start(6)
        finish(3)
        finish(4)
        finish(5)
        finish(6)

        wait_bytes(r.o_final, r.o_recv.at[0])
        wait_bytes(r.o_input, r.o_recv.at[1])
        wait_bytes(r.o_norms, r.o_recv.at[2])
        wait_bytes(r.o_rms, r.o_recv.at[3])
        pl.when(parity == 1)(wait_products)
        group.finish()

    @pl.when(core == 1)
    def _():
        pl.run_scoped(chain, *plan.chain_local)

    @pl.when(core == 0)
    def _():
        pl.run_scoped(helper, *plan.helper_local)

    for m in range(micros):
        r.out_block[m, 0] = r.o_final[m, 0 : HALF * HALF, :]
        r.out_input[m, 0] = r.o_input[m, 0 : FULL * FULL, :]
    norms = r.o_norms[0]
    sums = r.o_rms[0]
    for c in range(1, columns):
        norms = norms + r.o_norms[c]
        sums = sums + r.o_rms[c]
    share_width = allch // (wide * narrow)
    for target in range(narrow):

        @pl.when(n == target)
        def _(target=target):
            piece = norms[:, target * share_width : (target + 1) * share_width]
            r.out_gains[...] = piece[0]
            r.out_biases[...] = piece[1]

    square = jnp.sum(sums[0:4], axis=1, keepdims=True)
    rms = jnp.sqrt(square / (sums[4:5, 0:1] * out))
    for index in range(4):
        r.out_rms[index] = rms[index, 0]


def hand_out(results):
    count = len(results)

    def copies(*refs):
        for i in range(count - 1):
            refs[count + i][...] = refs[i][...]
        for index in range(4):
            refs[2 * count - 1][index] = refs[count - 1][index]

    in_vmem = pl.BlockSpec(memory_space=pltpu.VMEM)
    in_smem = pl.BlockSpec(memory_space=pltpu.SMEM)
    places = (in_vmem,) * (count - 1) + (in_smem,)
    return pl.pallas_call(
        copies,
        out_shape=tuple(jax.ShapeDtypeStruct(v.shape, v.dtype) for v in results),
        in_specs=places,
        out_specs=places,
        name="hand_out",
    )(*results)


def shards(
    inputs, image_sides, tile_cuts, cotangent, w_reduce1, w_spatial1, w_expand1, w_project1,
    w_reduce2, w_spatial2, w_expand2, norm_gains, norm_biases,
):
    wide = lax.axis_size(WIDE)
    narrow = lax.axis_size(NARROW)
    columns = narrow // 2
    micros = inputs.shape[0]
    slots = -(-micros // columns)
    inw, mid = w_reduce1.shape
    out = w_expand1.shape[1]
    allch = norm_gains.shape[0]
    places = wide // 2
    gather = mid // places == 128
    starts = (0, mid, 2 * mid, 2 * mid + out, 2 * mid + 2 * out, 3 * mid + 2 * out,
              4 * mid + 2 * out)
    widths = (mid, mid, out, out, mid, mid, out)

    def product(name, taps, depth, width, left, rows):
        return SimpleNamespace(
            name=name, taps=taps, depth=depth, width=width // narrow, rows=depth // wide,
            left=left, cells=rows, gathered=gather and taps > 1,
            halving=places == 4 and name in HALVING,
        )

    products = (
        product("e2", 1, mid, out, "h_mix2", HR),
        product("s2", TAPS, mid, mid, "h_act2", HR),
        product("r2", 1, out, mid, "h_low1", HR),
        product("e1", 1, mid, out, "h_mix1", HR),
        product("p1", 1, inw, out, "h_picked", HR),
        product("s1", TAPS, mid, mid, "h_act1", HR),
        product("r1", 1, inw, mid, "h_image", FR),
    )
    vmem = pltpu.VMEM
    hbm = pl.BlockSpec(memory_space=pl.ANY)
    in_vmem = pl.BlockSpec(memory_space=pltpu.VMEM)
    in_smem = pl.BlockSpec(memory_space=pltpu.SMEM)

    args = dict(
        inputs=(inputs, hbm),
        image_sides=(image_sides.T, in_smem),
        tile_cuts=(tile_cuts.transpose(1, 2, 0), in_smem),
        cotangent=(cotangent, hbm),
        w_reduce1=(w_reduce1, hbm),
        w_spatial1=(w_spatial1.reshape(TAPS * mid, mid), hbm),
        w_expand1=(w_expand1, hbm),
        w_project1=(w_project1, hbm),
        w_reduce2=(w_reduce2, hbm),
        w_spatial2=(w_spatial2.reshape(TAPS * mid, mid), hbm),
        w_expand2=(w_expand2, hbm),
        gains=(norm_gains.reshape(1, allch), in_vmem),
        biases=(norm_biases.reshape(1, allch), in_vmem),
    )
    share = allch // (wide * narrow)
    outputs = dict(
        out_block=((micros, 1, HALF * HALF, out // narrow), BF16),
        out_input=((micros, 1, FULL * FULL, inw // narrow), BF16),
    )
    for spec in (products[6], products[5], products[3], products[4], products[2], products[1],
                 products[0]):
        shape = (spec.rows, spec.width)
        if spec.taps > 1:
            shape = (spec.taps,) + shape
        outputs["out_" + spec.name] = (shape, F32)
    outputs["out_gains"] = ((share,), F32)
    outputs["out_biases"] = ((share,), F32)
    outputs["out_rms"] = ((4,), F32)

    scratch = dict(
        pick_back=vmem((FR, TAPS * HR), BF16),
        k_reduce1=vmem(w_reduce1.shape, BF16),
        k_spatial1=vmem((TAPS * mid, mid), BF16),
        k_expand1=vmem(w_expand1.shape, BF16),
        k_project1=vmem(w_project1.shape, BF16),
        k_reduce2=vmem(w_reduce2.shape, BF16),
        k_spatial2=vmem((TAPS * mid, mid), BF16),
        k_expand2=vmem(w_expand2.shape, BF16),
        cot_raw=vmem((slots, HALF * HALF, out), BF16),
        half=vmem((slots, HR, 128), F32),
        full=vmem((slots, FR, 128), F32),
        counts=vmem((slots, 128), F32),
        norms=vmem((2 * slots, allch), F32),
        norm_sums=vmem((2, allch), F32),
        squares=vmem((4, mid), F32),
        stage=vmem((16, out // 4), F32),
        sums=vmem((16, out // 4), F32),
        rms_part=vmem((8, mid), F32),
        z0=vmem((slots, FR, mid), F32),
        slope0=vmem((slots, FR, mid), F32),
        act1=vmem((slots, FR, mid), BF16),
        cols=vmem((slots * HR, TAPS * mid), BF16),
        z1=vmem((slots, HR, mid), F32),
        slope1=vmem((slots, HR, mid), F32),
        mix1=vmem((slots, HR, mid), BF16),
        z_branch=vmem((slots, HR, out), F32),
        z_short=vmem((slots, HR, out), F32),
        slope2=vmem((slots, HR, out), F32),
        low1=vmem((slots, HR, out), BF16),
        z3=vmem((slots, HR, mid), F32),
        slope3=vmem((slots, HR, mid), F32),
        act2=vmem((slots, HR, mid), BF16),
        z4=vmem((slots, HR, mid), F32),
        slope4=vmem((slots, HR, mid), F32),
        mix2=vmem((slots, HR, mid), BF16),
        z5=vmem((slots, HR, out), F32),
        u_out=vmem((slots, HR, out), F32),
        u_mid=vmem((slots, HR, mid), F32),
        final=vmem((slots, HR, out), BF16),
        g_e2=vmem((slots, HR, out), BF16),
        g_s2=vmem((slots, HR, mid), BF16),
        g_r2=vmem((slots, HR, mid), BF16),
        g_e1=vmem((slots, HR, out), BF16),
        g_p1=vmem((slots, HR, out), BF16),
        g_s1=vmem((slots, HR, mid), BF16),
        g_r1=vmem((slots, FR, mid), BF16),
        h_act1=vmem((1 if gather else 2, micros, FR, mid), BF16),
        h_mix1=vmem((2, micros, HR, mid), BF16),
        h_low1=vmem((2, micros, HR, out), BF16),
        h_act2=vmem((1 if gather else 2, micros, HR, mid), BF16),
        h_mix2=vmem((2, micros, HR, mid), BF16),
        h_image=vmem((2, micros, FR, inw), BF16),
        cuts=vmem((places, 2, 8, 128), F32),
        o_final=vmem((micros, HR, out // narrow), BF16),
        o_input=vmem((micros, FR, inw // narrow), BF16),
        o_norms=vmem((columns, 2, allch // wide), F32),
        o_rms=vmem((columns, 8, mid), F32),
    )
    stat_rows = (3, 2, 2, 2, 2, 2, 2, 2, 2, 2, 2, 2, 2, 1, 2)
    stat_widths = (mid, mid, out, mid, mid, out, out, mid, mid, out, mid, mid, out, out, mid)
    for step in range(STEPS):
        rows, width = stat_rows[step] * slots, stat_widths[step]
        if step in LOW_STEPS:
            scratch["stat%d" % step] = vmem((wide, 16, rows * width // 16), BF16)
        else:
            scratch["stat%d" % step] = vmem((wide, rows, width), F32)
    helper_local = dict(
        raw=vmem((micros, FULL * FULL, inw), BF16),
        pick=vmem((TAPS * HR, FR), BF16),
        h_picked=vmem((2, micros, HR, inw), BF16),
        t_base=vmem((TAPS * HR, HR), F32),
        t_row=vmem((TAPS * HR, HR), F32),
        t_col=vmem((TAPS * HR, HR), F32),
    )
    if gather:
        scratch["sp_act1"] = vmem((places, 2, micros, FR, 128), BF16)
        scratch["sp_act2"] = vmem((places, 2, micros, HR, 128), BF16)
    else:
        helper_local["h_cols"] = vmem((TAPS, 2, micros, HR, mid), BF16)
    for spec in products:
        name, taps, rows, width = spec.name, spec.taps, spec.rows, spec.width
        scratch["h_g_" + name] = vmem((2, micros, spec.cells, width), BF16)
        if spec.gathered:
            scratch["ga_" + name] = vmem((places, 2, micros, HR, width), BF16)
            helper_local["cols_" + name] = vmem((places * 2 * micros * HR, TAPS * 128), BF16)
        else:
            block = (taps, 2 * rows, width)
            if spec.halving:
                scratch["one_" + name] = vmem((2,) + block, BF16)
                scratch["two_" + name] = vmem(block, BF16)
                helper_local["p_" + name] = vmem((2, 2) + block, BF16)
            else:
                scratch["two_" + name] = vmem((places,) + block, BF16)
                helper_local["p_" + name] = vmem((places,) + block, BF16)
        last = (2, rows, width) if taps == 1 else (2, taps, rows, width)
        helper_local["last_" + name] = vmem(last, BF16)
        scratch["d_" + name] = vmem(last[1:], BF16)
    semaphores = dict(
        fetch=(16,),
        stat_send=(STEPS,),
        stat_recv=(STEPS,),
        chain_sends=(7 * columns * narrow + 5 * columns * columns + 2 * slots * narrow + 2 * narrow,),
        helper_sends=(7 * (places + 3) + 3 * places + 16,),
        h_recv=(5,),
        g_recv=(7,),
        y_recv=(7,),
        z_recv=(7,),
        o_recv=(4,),
        w_recv=(7,),
        one_recv=(7,),
        two_recv=(7,),
    )
    for name, shape in semaphores.items():
        scratch[name] = pltpu.SemaphoreType.DMA(shape)
    shared = ("h_", "o_", "sp", "ga", "cu", "on", "tw", "d_")
    chain_local = {name: scratch.pop(name) for name in tuple(scratch)
                   if name not in semaphores and name[:2] not in shared and name[:4] != "stat"}
    chain_local.update(
        raw=vmem((slots, FULL * FULL, inw), BF16),
        image=vmem((slots, FR, inw), BF16),
        picked=vmem((slots * HR, inw), BF16),
        pick=vmem((TAPS * HR, FR), BF16),
        tiles=vmem((slots, TAPS * HR, HR), BF16),
    )
    plan = SimpleNamespace(
        chain_names=tuple(chain_local), chain_local=tuple(chain_local.values()),
        helper_names=tuple(helper_local), helper_local=tuple(helper_local.values()),
        names=tuple(args) + tuple(outputs) + tuple(scratch),
        wide=wide, narrow=narrow, micros=micros, slots=slots,
        mid=mid, out=out, inw=inw, allch=allch,
        gather=gather, layers=tuple(zip(starts, widths)), products=products,
    )
    results = pl.pallas_call(
        functools.partial(kernel, plan),
        out_shape=tuple(jax.ShapeDtypeStruct(s, d) for s, d in outputs.values()),
        in_specs=[spec for _, spec in args.values()],
        out_specs=(in_vmem,) * (len(outputs) - 1) + (in_smem,),
        scratch_shapes=list(scratch.values()),
        compiler_params=pltpu.CompilerParams(
            collective_id=0, has_side_effects=True, vmem_limit_bytes=63 * 2**20 + 2**19
        ),
        name="bottleneck_pair",
    )(*[value for value, _ in args.values()])
    return hand_out(results)


def solution(mesh):
    return jax.shard_map(
        shards,
        mesh=mesh,
        in_specs=(
            P(None, WIDE, None, None),
            P(None, WIDE),
            P(None, WIDE, None),
            P(None, WIDE, None, None),
            P(), P(), P(), P(), P(), P(), P(), P(), P(),
        ),
        out_specs=(
            P(None, WIDE, None, NARROW),
            P(None, WIDE, None, NARROW),
            P(WIDE, NARROW),
            P(None, WIDE, NARROW),
            P(WIDE, NARROW),
            P(WIDE, NARROW),
            P(WIDE, NARROW),
            P(None, WIDE, NARROW),
            P(WIDE, NARROW),
            P((WIDE, NARROW)),
            P((WIDE, NARROW)),
            P(),
        ),
        check_vma=False,
    )
```

```python
import functools
import math
from types import SimpleNamespace

import jax
import jax.numpy as jnp
from jax import lax
from jax.experimental import pallas as pl
from jax.experimental.pallas import tpu as pltpu
from jax.sharding import PartitionSpec as P

MESH = pl.DeviceIdType.MESH
WIDE, NARROW = "wide", "narrow"
BF16 = jnp.bfloat16
F32 = jnp.float32
HALF = 7
FULL = 2 * HALF
EPSILON = 1e-05
C0 = math.sqrt(2.0 / math.pi)
C1 = C0 * 0.044715
HR = 64
FR = 208
TAPS = 9
STEPS = 15
LOW_STEPS = (6, 7, 8, 9, 10, 11, 13)
HALVING = ("p1",)


def dot(a, b):
    return jnp.dot(a, b, preferred_element_type=F32)


def dot_nt(a, b):
    return lax.dot_general(a, b, (((1,), (1,)), ((), ())), preferred_element_type=F32)


def dot_tn(a, b):
    return lax.dot_general(a, b, (((0,), (0,)), ((), ())), preferred_element_type=F32)


def spread(mask, width):
    return jnp.concatenate([mask] * (width // 128), axis=1)


def gelu(v):
    t = jnp.tanh(v * (C0 + C1 * (v * v)))
    h = 0.5 * v
    return h + h * t


def gelu_slope(v):
    v2 = v * v
    t = jnp.tanh(v * (C0 + C1 * v2))
    return 0.5 + 0.5 * t + (0.5 * v) * (1.0 - t * t) * (C0 + (3.0 * C1) * v2)


def column_sum(values):
    return jnp.sum(values, axis=0, keepdims=True)


def half_cell(p):
    i = lax.shift_right_logical(p * 9363, 16)
    return i, p - HALF * i


def full_cell(p):
    i = lax.shift_right_logical(p * 4682, 16)
    return i, p - FULL * i


def tap_of(r):
    t = lax.shift_right_logical(r, 6)
    ta = lax.shift_right_logical(t * 11, 5)
    return ta - 1, t - 3 * ta - 1


def one_zero(condition):
    return jnp.where(condition, 1.0, 0.0)


def strided_pick(rows, cells):
    a, b = tap_of(rows)
    p = lax.bitwise_and(rows, 63)
    i, j = half_cell(p)
    r, c = 2 * i + a, 2 * j + b
    inside = (p < HALF * HALF) & (r >= 0) & (r < FULL) & (c >= 0) & (c < FULL)
    return one_zero(inside & (cells == r * FULL + c)).astype(BF16)


def tile_pick(rows, cells, cut_row, cut_col):
    a, b = tap_of(rows)
    p = lax.bitwise_and(rows, 63)
    i, j = half_cell(p)
    r, c = i + a, j + b
    inside = (p < HALF * HALF) & (r >= 0) & (r < HALF) & (c >= 0) & (c < HALF)
    row_far = one_zero(r >= cut_row) - one_zero(i >= cut_row)
    col_far = one_zero(c >= cut_col) - one_zero(j >= cut_col)
    same = (row_far == 0.0) & (col_far == 0.0)
    return one_zero(inside & same & (cells == r * HALF + c)).astype(BF16)


class Group:
    def __init__(self, sems):
        self.sems = sems
        self.used = 0
        self.items = []

    def sem(self):
        self.used += 1
        return self.sems.at[self.used - 1]

    def remote(self, src, dst, recv_sem, device, when=None):
        copy = pltpu.make_async_remote_copy(
            src_ref=src, dst_ref=dst, send_sem=self.sem(), recv_sem=recv_sem,
            device_id=device, device_id_type=MESH,
        )
        if when is None:
            copy.start()
        else:
            pl.when(when)(copy.start)
        self.items.append((copy, when))

    def finish(self):
        for copy, when in self.items:
            if when is None:
                copy.wait_send()
            else:
                pl.when(when)(copy.wait_send)


def wait_bytes(ref, sem):
    pltpu.make_async_copy(ref, ref, sem).wait()


def kernel(plan, *refs):
    r = SimpleNamespace(**dict(zip(plan.names, refs)))
    r.stat = [getattr(r, "stat%d" % step) for step in range(STEPS)]
    wide, narrow, micros, slots = plan.wide, plan.narrow, plan.micros, plan.slots
    mid, out, inw, allch = plan.mid, plan.out, plan.inw, plan.allch
    places = wide // 2
    columns = narrow // 2
    layers = plan.layers
    w = lax.axis_index(WIDE)
    n = lax.axis_index(NARROW)
    x = n // 2
    core = n % 2
    first_micro = x * slots
    fetch = r.fetch
    parity = w % 2
    place = w // 2
    partner = w + 1 - 2 * parity
    own_act = 0 if plan.gather else parity

    def micro_of(s):
        return lax.rem(first_micro + s, micros)

    barrier = pltpu.get_barrier_semaphore()

    @pl.loop(1, wide)
    def _(d):
        pl.semaphore_signal(
            barrier, inc=1, device_id=(lax.rem(w + d, wide), n), device_id_type=MESH
        )

    for d in range(1, narrow):
        pl.semaphore_signal(
            barrier, inc=1, device_id=(w, lax.rem(n + d, narrow)), device_id_type=MESH
        )

        pl.semaphore_signal(
            barrier, inc=1, device_id=(partner, lax.rem(n + d, narrow)), device_id_type=MESH
        )

    def pass_barrier():
        pl.semaphore_wait(barrier, wide - 1 + 2 * (narrow - 1))

    def build_picks():
        rows = lax.broadcasted_iota(jnp.int32, (TAPS * HR, FR), 0)
        cells = lax.broadcasted_iota(jnp.int32, (TAPS * HR, FR), 1)
        r.pick[...] = strided_pick(rows, cells)

    def build_pick_back():
        rows = lax.broadcasted_iota(jnp.int32, (FR, TAPS * HR), 1)
        cells = lax.broadcasted_iota(jnp.int32, (FR, TAPS * HR), 0)
        r.pick_back[...] = strided_pick(rows, cells)

    def build_tiles(slot, micro):
        rows = lax.broadcasted_iota(jnp.int32, (TAPS * HR, HR), 0)
        cells = lax.broadcasted_iota(jnp.int32, (TAPS * HR, HR), 1)
        r.tiles[slot] = tile_pick(
            rows, cells, r.tile_cuts[0, 0, micro], r.tile_cuts[0, 1, micro]
        )

    def full_mask(micro):
        row, col = full_cell(lax.broadcasted_iota(jnp.int32, (FR, 128), 0))
        limit = 2 * r.image_sides[0, micro]
        return one_zero((row < limit) & (col < limit))

    def half_mask(micro):
        row, col = half_cell(lax.broadcasted_iota(jnp.int32, (HR, 128), 0))
        limit = r.image_sides[0, micro]
        return one_zero((row < limit) & (col < limit))

    def fetch_image(slot, micro):
        return pltpu.make_async_copy(r.inputs.at[micro, 0], r.raw.at[slot], fetch.at[slot])

    def mask_image(target, slot, micro):
        mask = full_mask(micro)
        raw = jnp.concatenate(
            [r.raw[slot].astype(F32), jnp.zeros((FR - FULL * FULL, inw), F32)], axis=0
        )
        target[...] = (raw * spread(mask, inw)).astype(BF16)

    def chain(*local):
        r.__dict__.update(zip(plan.chain_names, local))
        group = Group(r.chain_sends)
        weights = (
            (r.w_reduce1, r.k_reduce1), (r.w_spatial1, r.k_spatial1), (r.w_project1, r.k_project1),
            (r.w_expand1, r.k_expand1), (r.w_reduce2, r.k_reduce2), (r.w_spatial2, r.k_spatial2),
            (r.w_expand2, r.k_expand2),
        )

        def fetch_weight(index):
            return pltpu.make_async_copy(*weights[index], fetch.at[4 + index])

        fetch_image(0, micro_of(0)).start()
        fetch_weight(0).start()
        for s in range(1, slots):
            fetch_image(s, micro_of(s)).start()
        for index in range(1, 7):
            fetch_weight(index).start()

        def fetch_cotangent(s):
            return pltpu.make_async_copy(
                r.cotangent.at[micro_of(s), 0], r.cot_raw.at[s], fetch.at[11 + s]
            )

        for s in range(slots):
            fetch_cotangent(s).start()
            r.half[s] = half_mask(micro_of(s))
            r.full[s] = full_mask(micro_of(s))

        def send_stats(step):
            stat = r.stat[step]

            @pl.loop(0, wide)
            def _(d):
                p = lax.rem(wide - 1 - w + d, wide)

                @pl.when(p != w)
                def _():
                    pltpu.make_async_remote_copy(
                        src_ref=stat.at[w], dst_ref=stat.at[w],
                        send_sem=r.stat_send.at[step], recv_sem=r.stat_recv.at[step],
                        device_id=(p, n), device_id_type=MESH,
                    ).start()

        def wait_stats(step):
            stat = r.stat[step]
            wait_bytes(stat.at[pl.ds(0, wide - 1)], r.stat_recv.at[step])

        def total(step, row, begin=0, width=None):
            stat = r.stat[step]
            width = stat.shape[2] if width is None else width
            part = stat[0, row : row + 1, begin : begin + width]
            for j in range(1, wide):
                part = part + stat[j, row : row + 1, begin : begin + width]
            return part

        def put(step, row, value, begin=0):
            r.stat[step][w, row : row + 1, begin : begin + value.shape[1]] = value

        def put_pair(step, s, values, begin=0):
            put(step, 2 * s, column_sum(values), begin)
            put(step, 2 * s + 1, column_sum(values * values), begin)

        def put_low(row, rows, value):
            folds = 16 // rows
            part = value.shape[1] // folds
            for k in range(folds):
                at = row * folds + k
                r.stage[at : at + 1, 0:part] = value[:, k * part : (k + 1) * part]

        def send_low(step):
            width = r.stat[step].shape[2]
            r.stat[step][w] = r.stage[:, 0:width].astype(BF16)
            send_stats(step)

        def wait_low(step):
            wait_stats(step)
            width = r.stat[step].shape[2]
            part = r.stat[step][0].astype(F32)
            for j in range(1, wide):
                part = part + r.stat[step][j].astype(F32)
            r.sums[:, 0:width] = part

        def low_total(step, row, rows):
            folds = 16 // rows
            width = r.stat[step].shape[2]
            first = row * folds
            return jnp.concatenate(
                [r.sums[first + k : first + k + 1, 0:width] for k in range(folds)], axis=1
            )

        def inverse_count(s, layer):
            count = r.counts[s : s + 1, 0:1]
            return 1.0 / (count * (4.0 if layer == 0 else 1.0))

        def settle(s, layer, step, begin=0):
            start, width = layers[layer]
            inv_n = inverse_count(s, layer)
            mean = total(step, 2 * s, begin, width) * inv_n
            square = total(step, 2 * s + 1, begin, width) * inv_n
            inv = lax.rsqrt(square - mean * mean + EPSILON)
            scale = r.gains[:, start : start + width] * inv
            r.norms[2 * s : 2 * s + 1, start : start + width] = inv
            r.norms[2 * s + 1 : 2 * s + 2, start : start + width] = -mean * inv
            return scale, r.biases[:, start : start + width] - mean * scale

        def kept(s, layer):
            start, width = layers[layer]
            gain = r.gains[:, start : start + width]
            inv = r.norms[2 * s : 2 * s + 1, start : start + width]
            offset = r.norms[2 * s + 1 : 2 * s + 2, start : start + width]
            return inv, offset, gain * inv, r.biases[:, start : start + width] + gain * offset

        def normed(s, layer, z):
            inv, offset, _, _ = kept(s, layer)
            return z * inv + offset

        def activation(s, layer, z):
            _, _, scale, shift = kept(s, layer)
            return z * scale + shift

        def settle_back(s, layer, step, sum_u=None, sum_g=None):
            start, width = layers[layer]
            sum_u = low_total(step, 2 * s, 2 * slots) if sum_u is None else sum_u
            sum_g = low_total(step, 2 * s + 1, 2 * slots) if sum_g is None else sum_g
            live = jnp.where(first_micro + s < micros, 1.0, 0.0)
            for row, value in ((0, sum_g), (1, sum_u)):
                if s == 0:
                    r.norm_sums[row : row + 1, start : start + width] = value
                else:
                    r.norm_sums[row : row + 1, start : start + width] += live * value
            inv_n = inverse_count(s, layer)
            inv, offset, k0, _ = kept(s, layer)
            k2 = -k0 * (sum_g * inv_n)
            return k0, -k0 * (sum_u * inv_n) + k2 * offset, k2 * inv

        def live_row(s, row):
            if s == 0:
                return row
            return row * jnp.where(first_micro + s < micros, 1.0, 0.0)

        def fold_row(row):
            parts = [row[:, c : c + mid] for c in range(0, row.shape[1], mid)]
            return functools.reduce(lambda a, b: a + b, parts)

        def add_squares(s, index, values):
            row = live_row(s, fold_row(column_sum(values)))
            if s == 0:
                r.squares[index : index + 1, :] = row
            else:
                r.squares[index : index + 1, :] += row

        def share(src, dst, recv_sem):
            for c in range(columns):
                amount = min(slots, micros - c * slots)
                for h in range(columns if amount > 0 else 0):
                    group.remote(
                        src.at[0:amount], dst.at[c * slots : c * slots + amount], recv_sem,
                        (w, 2 * h), x == c,
                    )

        def share_grad(src, index):
            spec = plan.products[index]
            dst = getattr(r, "h_g_" + spec.name)
            for c in range(columns):
                amount = min(slots, micros - c * slots)
                order = sorted(range(narrow), key=lambda quarter: quarter // 2 == c)
                for quarter in order if amount > 0 else ():
                    h, v = quarter // 2, quarter % 2
                    group.remote(
                        src.at[0:amount, :, quarter * spec.width : (quarter + 1) * spec.width],
                        dst.at[parity, c * slots : c * slots + amount], r.g_recv.at[index],
                        (w - parity + v, 2 * h), x == c,
                    )

        def rows2(ref):
            value = ref[...]
            return value.reshape(value.shape[0] * value.shape[1], value.shape[2])

        def set_rows(ref, value):
            ref[...] = value.reshape(ref.shape)

        def rows_of(value, s, count=HR):
            return value[s * count : (s + 1) * count]

        def gather_tiles(s, value, select):
            picked = dot(select, value).astype(BF16)
            for t in range(TAPS):
                r.cols[s * HR : (s + 1) * HR, t * mid : (t + 1) * mid] = picked[
                    t * HR : (t + 1) * HR
                ]

        def half_wide(s, width):
            return spread(r.half[s], width)

        for s in range(slots):
            fetch_image(s, micro_of(s)).wait()
            mask_image(r.image.at[s], s, micro_of(s))
        fetch_weight(0).wait()
        for s in range(slots):
            z = dot(r.image[s], r.k_reduce1[...])
            r.z0[s] = z
            put_pair(0, s, z)
            side = r.image_sides[0, micro_of(s)]
            area = jnp.full((1, mid), side * side, jnp.int32).astype(F32)
            put(0, 2 * slots + s, area)
        build_picks()
        pass_barrier()
        send_stats(0)
        for s in range(slots):
            build_tiles(s, micro_of(s))
        centre = r.pick[4 * HR : 5 * HR, :]
        for s in range(slots):
            r.picked[s * HR : (s + 1) * HR, :] = dot(centre, r.image[s]).astype(BF16)
        fetch_weight(1).wait()
        wait_stats(0)
        for s in range(slots):
            r.counts[s : s + 1, :] = total(0, 2 * slots + s, 0, 128)

        for s in range(slots):
            scale, shift = settle(s, 0, 0)
            act = gelu(r.z0[s] * scale + shift) * spread(r.full[s], mid)
            act = act.astype(BF16)
            r.act1[s] = act
            gather_tiles(s, act, r.pick[...])
        z = dot(r.cols[...], r.k_spatial1[...])
        for s in range(slots):
            r.z1[s] = rows_of(z, s)
            put_pair(1, s, rows_of(z, s) * half_wide(s, mid))
        send_stats(1)
        share(r.act1, r.h_act1.at[own_act], r.h_recv.at[0])
        fetch_weight(2).wait()
        set_rows(r.z_short, dot(r.picked[...], r.k_project1[...]))
        for s in range(slots):
            put_pair(12, s, r.z_short[s])
        send_stats(12)
        for s in range(slots):
            r.slope0[s] = gelu_slope(activation(s, 0, r.z0[s])) * spread(r.full[s], mid)
        fetch_weight(3).wait()
        wait_stats(1)

        for s in range(slots):
            scale, shift = settle(s, 1, 1)
            mixed = gelu(r.z1[s] * scale + shift) * half_wide(s, mid)
            r.mix1[s] = mixed.astype(BF16)
        z = dot(rows2(r.mix1), r.k_expand1[...])
        for s in range(slots):
            r.z_branch[s] = rows_of(z, s)
            put_pair(2, s, rows_of(z, s))
        send_stats(2)
        share(r.mix1, r.h_mix1.at[parity], r.h_recv.at[1])
        for s in range(slots):
            r.slope1[s] = gelu_slope(activation(s, 1, r.z1[s])) * half_wide(s, mid)
        fetch_weight(4).wait()
        wait_stats(12)
        wait_stats(2)

        for s in range(slots):
            scale, shift = settle(s, 2, 2)
            scale_short, shift_short = settle(s, 3, 12)
            joined = (r.z_branch[s] * scale + shift) + (
                r.z_short[s] * scale_short + shift_short
            )
            r.slope2[s] = joined
            block = gelu(joined) * half_wide(s, out)
            r.low1[s] = block.astype(BF16)
        z = dot(rows2(r.low1), r.k_reduce2[...])
        for s in range(slots):
            r.z3[s] = rows_of(z, s)
            put_pair(3, s, rows_of(z, s))
        send_stats(3)
        share(r.low1, r.h_low1.at[parity], r.h_recv.at[2])
        for s in range(slots):
            mask = half_wide(s, out)
            branch = activation(s, 2, r.z_branch[s])
            joined = r.slope2[s]
            add_squares(s, 0, branch * branch * mask)
            block = gelu(joined) * mask
            add_squares(s, 1, block * block)
            r.slope2[s] = gelu_slope(joined) * mask
        fetch_weight(5).wait()
        wait_stats(3)

        for s in range(slots):
            scale, shift = settle(s, 4, 3)
            act = gelu(r.z3[s] * scale + shift) * half_wide(s, mid)
            act = act.astype(BF16)
            r.act2[s] = act
            gather_tiles(s, act, r.tiles[s])
        z = dot(r.cols[...], r.k_spatial2[...])
        for s in range(slots):
            r.z4[s] = rows_of(z, s)
            put_pair(4, s, rows_of(z, s) * half_wide(s, mid))
        send_stats(4)
        share(r.act2, r.h_act2.at[own_act], r.h_recv.at[3])
        for s in range(slots):
            r.slope3[s] = gelu_slope(activation(s, 4, r.z3[s])) * half_wide(s, mid)
        fetch_weight(6).wait()
        wait_stats(4)

        for s in range(slots):
            scale, shift = settle(s, 5, 4)
            mixed = gelu(r.z4[s] * scale + shift) * half_wide(s, mid)
            r.mix2[s] = mixed.astype(BF16)
        z = dot(rows2(r.mix2), r.k_expand2[...])
        for s in range(slots):
            r.z5[s] = rows_of(z, s)
            put_pair(5, s, rows_of(z, s))
        send_stats(5)
        share(r.mix2, r.h_mix2.at[parity], r.h_recv.at[4])
        for s in range(slots):
            r.slope4[s] = gelu_slope(activation(s, 5, r.z4[s])) * half_wide(s, mid)
            fetch_cotangent(s).wait()
        wait_stats(5)

        for s in range(slots):
            scale, shift = settle(s, 6, 5)
            joined = (r.z5[s] * scale + shift) + r.low1[s].astype(F32)
            cot = jnp.concatenate(
                [r.cot_raw[s].astype(F32), jnp.zeros((HR - HALF * HALF, out), F32)], axis=0
            )
            u = gelu_slope(joined) * cot * half_wide(s, out)
            r.u_out[s] = u
            put_low(2 * s, 2 * slots, column_sum(u))
            put_low(2 * s + 1, 2 * slots, column_sum(u * normed(s, 6, r.z5[s])))
        send_low(6)
        for s in range(slots):
            mask = half_wide(s, out)
            branch = activation(s, 6, r.z5[s])
            add_squares(s, 2, branch * branch * mask)
            block = gelu(branch + r.low1[s].astype(F32)) * mask
            add_squares(s, 3, block * block)
            r.final[s] = block.astype(BF16)
        part = out // narrow
        for s in range(slots):
            for target in range(narrow):
                src = r.final.at[s, :, target * part : (target + 1) * part]
                dst = r.o_final.at[first_micro + s]
                group.remote(
                    src, dst, r.o_recv.at[0], (w, target),
                    (first_micro + s < micros) & (n != target),
                )
        r.stat[14][w] = r.squares[...]
        send_stats(14)
        wait_low(6)

        for s in range(slots):
            k0, k1, k2 = settle_back(s, 6, 6)
            grad = (k0 * r.u_out[s] + k1 + k2 * r.z5[s]) * half_wide(s, out)
            r.g_e2[s] = grad.astype(BF16)
        back = dot_nt(rows2(r.g_e2), r.k_expand2[...]).astype(BF16).astype(F32)
        for s in range(slots):
            u = rows_of(back, s) * r.slope4[s]
            r.u_mid[s] = u
            put_low(2 * s, 2 * slots, column_sum(u))
            put_low(2 * s + 1, 2 * slots, column_sum(u * normed(s, 5, r.z4[s])))
        send_low(7)
        share_grad(r.g_e2, 0)
        wait_low(7)
        wait_stats(14)
        for index in range(4):
            r.rms_part[index : index + 1, :] = total(14, index)
        count = r.counts[0:1, :]
        for s in range(1, slots):
            count = count + live_row(s, r.counts[s : s + 1, :])
        r.rms_part[4:5, :] = spread(count, mid)

        for s in range(slots):
            k0, k1, k2 = settle_back(s, 5, 7)
            grad = (k0 * r.u_mid[s] + k1 + k2 * r.z4[s]) * half_wide(s, mid)
            r.g_s2[s] = grad.astype(BF16)
            gather_tiles(s, r.g_s2[s], r.tiles[s])
        back = None
        for t in range(TAPS):
            back_tap = dot_nt(
                r.cols[:, t * mid : (t + 1) * mid],
                r.k_spatial2[(8 - t) * mid : (9 - t) * mid, :],
            )
            back = back_tap if back is None else back + back_tap
        back = back.astype(BF16).astype(F32)
        for s in range(slots):
            u = rows_of(back, s) * r.slope3[s]
            r.u_mid[s] = u
            put_low(2 * s, 2 * slots, column_sum(u))
            put_low(2 * s + 1, 2 * slots, column_sum(u * normed(s, 4, r.z3[s])))
        send_low(8)
        share_grad(r.g_s2, 1)
        wait_low(8)

        for s in range(slots):
            k0, k1, k2 = settle_back(s, 4, 8)
            grad = (k0 * r.u_mid[s] + k1 + k2 * r.z3[s]) * half_wide(s, mid)
            r.g_r2[s] = grad.astype(BF16)
        back = dot_nt(rows2(r.g_r2), r.k_reduce2[...])
        for s in range(slots):
            u = (rows_of(back, s) + r.u_out[s].astype(BF16).astype(F32)) * r.slope2[s]
            r.u_out[s] = u
            put_low(2 * s, 2 * slots, column_sum(u))
            put_low(2 * s + 1, 2 * slots, column_sum(u * normed(s, 2, r.z_branch[s])))
        send_low(9)
        for s in range(slots):
            put_low(s, slots, column_sum(r.u_out[s] * normed(s, 3, r.z_short[s])))
        send_low(13)
        share_grad(r.g_r2, 2)
        wait_low(9)

        for s in range(slots):
            k0, k1, k2 = settle_back(s, 2, 9)
            grad = (k0 * r.u_out[s] + k1 + k2 * r.z_branch[s]) * half_wide(s, out)
            r.g_e1[s] = grad.astype(BF16)
        back = dot_nt(rows2(r.g_e1), r.k_expand1[...]).astype(BF16).astype(F32)
        for s in range(slots):
            u = rows_of(back, s) * r.slope1[s]
            r.u_mid[s] = u
            put_low(2 * s, 2 * slots, column_sum(u))
            put_low(2 * s + 1, 2 * slots, column_sum(u * normed(s, 1, r.z1[s])))
        send_low(10)
        sums_u = [low_total(9, 2 * s, 2 * slots) for s in range(slots)]
        wait_low(13)
        for s in range(slots):
            k0, k1, k2 = settle_back(s, 3, 13, sums_u[s], low_total(13, s, slots))
            grad = (k0 * r.u_out[s] + k1 + k2 * r.z_short[s]) * half_wide(s, out)
            r.g_p1[s] = grad.astype(BF16)
        share_grad(r.g_e1, 3)
        share_grad(r.g_p1, 4)
        build_pick_back()
        r.picked[...] = dot_nt(rows2(r.g_p1), r.k_project1[...]).astype(
            BF16
        )
        wait_low(10)

        for s in range(slots):
            k0, k1, k2 = settle_back(s, 1, 10)
            grad = (k0 * r.u_mid[s] + k1 + k2 * r.z1[s]) * half_wide(s, mid)
            r.g_s1[s] = grad.astype(BF16)
        g_rows = rows2(r.g_s1)
        for t in range(TAPS):
            r.cols[:, t * mid : (t + 1) * mid] = dot_nt(
                g_rows, r.k_spatial1[t * mid : (t + 1) * mid, :]
            ).astype(BF16)
        for s in range(slots):
            back = jnp.concatenate(
                [r.cols[s * HR : (s + 1) * HR, t * mid : (t + 1) * mid] for t in range(TAPS)],
                axis=0,
            )
            u = dot(r.pick_back[...], back) * r.slope0[s]
            r.slope0[s] = u
            put_low(2 * s, 2 * slots, column_sum(u))
            put_low(2 * s + 1, 2 * slots, column_sum(u * normed(s, 0, r.z0[s])))
        send_low(11)
        share_grad(r.g_s1, 5)
        wait_low(11)

        for s in range(slots):
            k0, k1, k2 = settle_back(s, 0, 11)
            grad = (k0 * r.slope0[s] + k1 + k2 * r.z0[s]) * spread(r.full[s], mid)
            r.g_r1[s] = grad.astype(BF16)
        share_grad(r.g_r1, 6)
        section = allch // wide
        own = pl.ds(pl.multiple_of(w * section, 128), section)
        for target in range(narrow):
            group.remote(
                r.norm_sums.at[:, own], r.o_norms.at[x], r.o_recv.at[2], (w, target),
                n != target,
            )
            group.remote(
                r.rms_part, r.o_rms.at[x], r.o_recv.at[3], (w, target), n != target
            )
        r.o_norms[x] = r.norm_sums[:, own]
        r.o_rms[x] = r.rms_part[...]
        for s in range(slots):
            grad = dot_nt(r.g_r1[s], r.k_reduce1[...])
            grad = grad + dot(
                r.pick_back[:, 4 * HR : 5 * HR], r.picked[s * HR : (s + 1) * HR, :]
            )
            r.image[s] = grad.astype(BF16)
        part = inw // narrow
        for s in range(slots):
            for target in range(narrow):
                group.remote(
                    r.image.at[s, :, target * part : (target + 1) * part],
                    r.o_input.at[first_micro + s], r.o_recv.at[1], (w, target),
                    (first_micro + s < micros) & (n != target),
                )
        for s in range(slots):
            for target in range(narrow):

                @pl.when((n == target) & (first_micro + s < micros))
                def _(s=s, target=target):
                    wide_part = out // narrow
                    r.o_final[first_micro + s] = r.final[
                        s, :, target * wide_part : (target + 1) * wide_part
                    ]
                    r.o_input[first_micro + s] = r.image[
                        s, :, target * part : (target + 1) * part
                    ]

        for c in range(columns):
            amount = min(slots, micros - c * slots)
            others = micros - max(amount, 0)

            @pl.when(x == c)
            def _(others=others):
                wait_bytes(r.o_final.at[0:others], r.o_recv.at[0])
                wait_bytes(r.o_input.at[0:others], r.o_recv.at[1])

        wait_bytes(r.o_norms.at[0 : columns - 1], r.o_recv.at[2])
        wait_bytes(r.o_rms.at[0 : columns - 1], r.o_recv.at[3])
        wait_products()
        group.finish()
        for step in range(STEPS):
            wait_bytes(r.stat[step].at[pl.ds(0, wide - 1)], r.stat_send.at[step])

    def wait_products():
        for index, spec in enumerate(plan.products):
            landing = getattr(r, "d_" + spec.name)
            wait_bytes(landing, r.w_recv.at[index])
            getattr(r, "out_" + spec.name)[...] = landing[...].astype(F32)

    def helper(*local):
        r.__dict__.update(zip(plan.helper_names, local))
        group = Group(r.helper_sends)
        low, high = place % 2, place // 2

        def relay(ref, sem):
            group.remote(ref.at[parity], ref.at[parity], r.y_recv.at[sem], (partner, n))

        def arrived(ref, sem):
            wait_bytes(ref.at[0], r.y_recv.at[sem])

        def scatter(src, dst, sem):
            for q in range(places):
                part = src.at[:, :, q * 128 : (q + 1) * 128]
                group.remote(
                    part, dst.at[place, parity], r.z_recv.at[sem], (2 * q + parity, n), place != q
                )

                @pl.when(place == q)
                def _(q=q):
                    dst[q, parity] = src[:, :, q * 128 : (q + 1) * 128]

        def forward(ref, sem):
            if places > 1:
                wait_bytes(ref.at[0 : places - 1, 0], r.z_recv.at[sem])
            group.remote(
                ref.at[:, parity], ref.at[:, parity], r.y_recv.at[sem], (partner, n)
            )

        def forwarded(ref, sem):
            wait_bytes(ref.at[:, 0], r.y_recv.at[sem])

        def tile_base():
            rows = lax.broadcasted_iota(jnp.int32, (TAPS * HR, HR), 0)
            cells = lax.broadcasted_iota(jnp.int32, (TAPS * HR, HR), 1)
            a, b = tap_of(rows)
            p = lax.bitwise_and(rows, 63)
            i, j = half_cell(p)
            ti, tj = i + a, j + b
            inside = (p < HALF * HALF) & (ti >= 0) & (ti < HALF) & (tj >= 0) & (tj < HALF)
            r.t_base[...] = one_zero(inside & (cells == ti * HALF + tj))
            r.t_row[...] = jnp.where(a != 0, jnp.maximum(i, ti), -1).astype(F32)
            r.t_col[...] = jnp.where(b != 0, jnp.maximum(j, tj), -1).astype(F32)

        def tiles_at(q, v, m):
            keep = (r.t_row[...] != r.cuts[q, v, 2 * m : 2 * m + 1, 0:HR]) & (
                r.t_col[...] != r.cuts[q, v, 2 * m + 1 : 2 * m + 2, 0:HR]
            )
            return jnp.where(keep, r.t_base[...], 0.0).astype(BF16)

        def strided_columns(cols, source):
            @pl.loop(0, places)
            def _(q):
                for v in range(2):
                    grids = jnp.concatenate([source[q, v, m] for m in range(micros)], axis=1)
                    picked = dot(r.pick[...], grids).astype(BF16)
                    for m in range(micros):
                        row = pl.multiple_of(((q * 2 + v) * micros + m) * HR, HR)
                        for t in range(TAPS):
                            cols[pl.ds(row, HR), t * 128 : (t + 1) * 128] = picked[
                                t * HR : (t + 1) * HR, m * 128 : (m + 1) * 128
                            ]

        def tile_columns(cols, source):
            @pl.loop(0, places)
            def _(q):
                for v in range(2):
                    for m in range(micros):
                        row = pl.multiple_of(((q * 2 + v) * micros + m) * HR, HR)
                        picked = dot(tiles_at(q, v, m), source[q, v, m]).astype(BF16)
                        for t in range(TAPS):
                            cols[pl.ds(row, HR), t * 128 : (t + 1) * 128] = picked[
                                t * HR : (t + 1) * HR
                            ]

        def pair_columns(name, source):
            for v in range(2):
                for m in range(micros):
                    select = r.pick[...] if name == "s1" else tiles_at(place, v, m)
                    picked = dot(select, source[v, m]).astype(BF16)
                    for t in range(TAPS):
                        r.h_cols[t, v, m] = picked[t * HR : (t + 1) * HR]

        def flat(value):
            return value.reshape(math.prod(value.shape[:-1]), value.shape[-1])

        def store_blocks(product, tap, begin, value, deep, halving):
            step = min(deep, value.shape[0])
            for b in range(0, value.shape[0], step):
                row = begin + b
                at = pl.ds(row % deep, step)
                block = row // deep
                if halving:
                    product[block // 2, block % 2, tap, at, :] = value[b : b + step]
                else:
                    product[block, tap, at, :] = value[b : b + step]

        def multiply(spec):
            grad = flat(getattr(r, "h_g_" + spec.name)[...])
            product = getattr(r, "p_" + spec.name)
            deep = spec.depth // places
            chunk = min(256, spec.depth)
            if spec.taps == 1:
                left = getattr(r, spec.left)
                for begin in range(0, spec.depth, chunk):
                    value = dot_tn(flat(left[..., begin : begin + chunk]), grad).astype(BF16)
                    store_blocks(product, 0, begin, value, deep, spec.halving)
            else:
                pair_columns(spec.name, getattr(r, spec.left))

                @pl.loop(0, TAPS)
                def _(t):
                    for begin in range(0, spec.depth, chunk):
                        value = dot_tn(
                            flat(r.h_cols[t, :, :, :, begin : begin + chunk]), grad
                        ).astype(BF16)
                        store_blocks(product, t, begin, value, deep, spec.halving)

        def start(index):
            spec = plan.products[index]
            grad = getattr(r, "h_g_" + spec.name)
            wait_bytes(grad, r.g_recv.at[index])
            if spec.gathered:
                source, target = grad, getattr(r, "ga_" + spec.name)
            else:
                multiply(spec)
                source, target = getattr(r, "p_" + spec.name), getattr(r, "two_" + spec.name)
            if spec.halving:
                group.remote(
                    source.at[:, 1 - low], getattr(r, "one_" + spec.name),
                    r.one_recv.at[index], (2 * (place + 1 - 2 * low) + parity, n),
                )
                return
            for q in range(places):
                group.remote(
                    source if spec.gathered else source.at[q], target.at[place],
                    r.two_recv.at[index], (2 * q + parity, n), place != q,
                )
            target[place] = source[...] if spec.gathered else source[place]

        def middle(index):
            spec = plan.products[index]
            if not spec.halving:
                return
            source, one = getattr(r, "p_" + spec.name), getattr(r, "one_" + spec.name)
            wait_bytes(one, r.one_recv.at[index])
            far = source[1 - high, low].astype(F32) + one[1 - high].astype(F32)
            source[1 - high, low] = far.astype(BF16)
            group.remote(
                source.at[1 - high, low], getattr(r, "two_" + spec.name), r.two_recv.at[index],
                (2 * (place + 2 - 4 * high) + parity, n),
            )

        def finish(index):
            spec = plan.products[index]
            rows = spec.rows
            last = getattr(r, "last_" + spec.name)
            target = getattr(r, ("ga_" if spec.gathered else "two_") + spec.name)
            if spec.halving:
                wait_bytes(target, r.two_recv.at[index])
            elif places > 1:
                wait_bytes(target.at[0 : places - 1], r.two_recv.at[index])
            result = getattr(r, "out_" + spec.name)
            landing = getattr(r, "d_" + spec.name)

            def keep(half, part, at=Ellipsis):
                last[(half,) if at is Ellipsis else (half, at)] = part.astype(BF16)
                if half == 0:

                    @pl.when(parity == 0)
                    def _():
                        result[at] = part

            if spec.gathered:
                cols = getattr(r, "cols_" + spec.name)
                value = dot_tn(flat(target[...]), cols[...])
                for t in range(TAPS):
                    tap = value[:, t * 128 : (t + 1) * 128].T
                    for half in range(2):
                        keep(half, tap[half * rows : (half + 1) * rows], t)
            else:
                if spec.halving:
                    value = getattr(r, "p_" + spec.name)[high, low].astype(F32)
                    value = value + getattr(r, "one_" + spec.name)[high].astype(F32)
                    value = value + target[...].astype(F32)
                else:
                    value = target[0].astype(F32)
                    for q in range(1, places):
                        value = value + target[q].astype(F32)
                for half in range(2):
                    part = value[:, half * rows : (half + 1) * rows]
                    keep(half, part if spec.taps > 1 else part[0])

            sem = r.w_recv.at[index]
            group.remote(last.at[1], landing, sem, (partner, n), parity == 0)
            group.remote(last.at[0], landing, sem, (partner, n + 1), parity == 1)
            group.remote(last.at[1], landing, sem, (w, n + 1), parity == 1)

        for m in range(micros):
            fetch_image(m, m).start()
        build_picks()
        tile_base()
        for m in range(micros):
            for k in range(2):
                cut = jnp.full((1, 128), r.tile_cuts[0, k, m], jnp.int32).astype(F32)
                r.cuts[place, parity, 2 * m + k : 2 * m + k + 1, :] = cut
        for m in range(micros):
            fetch_image(m, m).wait()
            mask_image(r.h_image.at[parity, m], m, m)
        pass_barrier()
        relay(r.h_image, 0)
        if plan.gather:
            for q in range(places):
                group.remote(
                    r.cuts.at[place, parity], r.cuts.at[place, parity], r.z_recv.at[1],
                    (2 * q + parity, n), place != q,
                )
        else:
            relay(r.cuts.at[place], 1)
        wait_bytes(r.h_act1.at[0], r.h_recv.at[0])
        if plan.gather:
            scatter(r.h_act1.at[0], r.sp_act1, 2)
            forward(r.cuts, 1)
        else:
            relay(r.h_act1, 2)
        wait_bytes(r.h_mix1.at[0], r.h_recv.at[1])
        relay(r.h_mix1, 3)
        if plan.gather:
            forward(r.sp_act1, 2)
        wait_bytes(r.h_low1.at[0], r.h_recv.at[2])
        relay(r.h_low1, 4)
        if plan.gather:
            forwarded(r.sp_act1, 2)
            strided_columns(r.cols_s1, r.sp_act1)
        arrived(r.h_image, 0)
        centre = r.pick[4 * HR : 5 * HR, :]
        for v in range(2):
            for m in range(micros):
                r.h_picked[v, m] = dot(centre, r.h_image[v, m]).astype(BF16)
        wait_bytes(r.h_act2.at[0], r.h_recv.at[3])
        if plan.gather:
            scatter(r.h_act2.at[0], r.sp_act2, 5)
        else:
            relay(r.h_act2, 5)
        wait_bytes(r.h_mix2.at[0], r.h_recv.at[4])
        relay(r.h_mix2, 6)
        if plan.gather:
            forward(r.sp_act2, 5)
            forwarded(r.cuts, 1)
            forwarded(r.sp_act2, 5)
            tile_columns(r.cols_s2, r.sp_act2)
        else:
            arrived(r.cuts.at[0], 1)
            arrived(r.h_act1, 2)
            arrived(r.h_act2, 5)
        arrived(r.h_mix1, 3)
        arrived(r.h_low1, 4)
        arrived(r.h_mix2, 6)

        start(0)
        start(1)
        start(2)
        start(4)
        start(3)
        middle(4)
        start(5)
        finish(0)
        finish(1)
        finish(2)
        start(6)
        finish(3)
        finish(4)
        finish(5)
        finish(6)

        wait_bytes(r.o_final, r.o_recv.at[0])
        wait_bytes(r.o_input, r.o_recv.at[1])
        wait_bytes(r.o_norms, r.o_recv.at[2])
        wait_bytes(r.o_rms, r.o_recv.at[3])
        pl.when(parity == 1)(wait_products)
        group.finish()

    @pl.when(core == 1)
    def _():
        pl.run_scoped(chain, *plan.chain_local)

    @pl.when(core == 0)
    def _():
        pl.run_scoped(helper, *plan.helper_local)

    for m in range(micros):
        r.out_block[m, 0] = r.o_final[m, 0 : HALF * HALF, :]
        r.out_input[m, 0] = r.o_input[m, 0 : FULL * FULL, :]
    norms = r.o_norms[0]
    sums = r.o_rms[0]
    for c in range(1, columns):
        norms = norms + r.o_norms[c]
        sums = sums + r.o_rms[c]
    share_width = allch // (wide * narrow)
    for target in range(narrow):

        @pl.when(n == target)
        def _(target=target):
            piece = norms[:, target * share_width : (target + 1) * share_width]
            r.out_gains[...] = piece[0]
            r.out_biases[...] = piece[1]

    square = jnp.sum(sums[0:4], axis=1, keepdims=True)
    rms = jnp.sqrt(square / (sums[4:5, 0:1] * out))
    for index in range(4):
        r.out_rms[index] = rms[index, 0]


def hand_out(results):
    count = len(results)

    def copies(*refs):
        for i in range(count - 1):
            refs[count + i][...] = refs[i][...]
        for index in range(4):
            refs[2 * count - 1][index] = refs[count - 1][index]

    in_vmem = pl.BlockSpec(memory_space=pltpu.VMEM)
    in_smem = pl.BlockSpec(memory_space=pltpu.SMEM)
    places = (in_vmem,) * (count - 1) + (in_smem,)
    return pl.pallas_call(
        copies,
        out_shape=tuple(jax.ShapeDtypeStruct(v.shape, v.dtype) for v in results),
        in_specs=places,
        out_specs=places,
        name="hand_out",
    )(*results)


def shards(
    inputs, image_sides, tile_cuts, cotangent, w_reduce1, w_spatial1, w_expand1, w_project1,
    w_reduce2, w_spatial2, w_expand2, norm_gains, norm_biases,
):
    wide = lax.axis_size(WIDE)
    narrow = lax.axis_size(NARROW)
    columns = narrow // 2
    micros = inputs.shape[0]
    slots = -(-micros // columns)
    inw, mid = w_reduce1.shape
    out = w_expand1.shape[1]
    allch = norm_gains.shape[0]
    places = wide // 2
    gather = mid // places == 128
    starts = (0, mid, 2 * mid, 2 * mid + out, 2 * mid + 2 * out, 3 * mid + 2 * out,
              4 * mid + 2 * out)
    widths = (mid, mid, out, out, mid, mid, out)

    def product(name, taps, depth, width, left, rows):
        return SimpleNamespace(
            name=name, taps=taps, depth=depth, width=width // narrow, rows=depth // wide,
            left=left, cells=rows, gathered=gather and taps > 1,
            halving=places == 4 and name in HALVING,
        )

    products = (
        product("e2", 1, mid, out, "h_mix2", HR),
        product("s2", TAPS, mid, mid, "h_act2", HR),
        product("r2", 1, out, mid, "h_low1", HR),
        product("e1", 1, mid, out, "h_mix1", HR),
        product("p1", 1, inw, out, "h_picked", HR),
        product("s1", TAPS, mid, mid, "h_act1", HR),
        product("r1", 1, inw, mid, "h_image", FR),
    )
    vmem = pltpu.VMEM
    hbm = pl.BlockSpec(memory_space=pl.ANY)
    in_vmem = pl.BlockSpec(memory_space=pltpu.VMEM)
    in_smem = pl.BlockSpec(memory_space=pltpu.SMEM)

    args = dict(
        inputs=(inputs, hbm),
        image_sides=(image_sides.T, in_smem),
        tile_cuts=(tile_cuts.transpose(1, 2, 0), in_smem),
        cotangent=(cotangent, hbm),
        w_reduce1=(w_reduce1, hbm),
        w_spatial1=(w_spatial1.reshape(TAPS * mid, mid), hbm),
        w_expand1=(w_expand1, hbm),
        w_project1=(w_project1, hbm),
        w_reduce2=(w_reduce2, hbm),
        w_spatial2=(w_spatial2.reshape(TAPS * mid, mid), hbm),
        w_expand2=(w_expand2, hbm),
        gains=(norm_gains.reshape(1, allch), in_vmem),
        biases=(norm_biases.reshape(1, allch), in_vmem),
    )
    share = allch // (wide * narrow)
    outputs = dict(
        out_block=((micros, 1, HALF * HALF, out // narrow), BF16),
        out_input=((micros, 1, FULL * FULL, inw // narrow), BF16),
    )
    for spec in (products[6], products[5], products[3], products[4], products[2], products[1],
                 products[0]):
        shape = (spec.rows, spec.width)
        if spec.taps > 1:
            shape = (spec.taps,) + shape
        outputs["out_" + spec.name] = (shape, F32)
    outputs["out_gains"] = ((share,), F32)
    outputs["out_biases"] = ((share,), F32)
    outputs["out_rms"] = ((4,), F32)

    scratch = dict(
        pick_back=vmem((FR, TAPS * HR), BF16),
        k_reduce1=vmem(w_reduce1.shape, BF16),
        k_spatial1=vmem((TAPS * mid, mid), BF16),
        k_expand1=vmem(w_expand1.shape, BF16),
        k_project1=vmem(w_project1.shape, BF16),
        k_reduce2=vmem(w_reduce2.shape, BF16),
        k_spatial2=vmem((TAPS * mid, mid), BF16),
        k_expand2=vmem(w_expand2.shape, BF16),
        cot_raw=vmem((slots, HALF * HALF, out), BF16),
        half=vmem((slots, HR, 128), F32),
        full=vmem((slots, FR, 128), F32),
        counts=vmem((slots, 128), F32),
        norms=vmem((2 * slots, allch), F32),
        norm_sums=vmem((2, allch), F32),
        squares=vmem((4, mid), F32),
        stage=vmem((16, out // 4), F32),
        sums=vmem((16, out // 4), F32),
        rms_part=vmem((8, mid), F32),
        z0=vmem((slots, FR, mid), F32),
        slope0=vmem((slots, FR, mid), F32),
        act1=vmem((slots, FR, mid), BF16),
        cols=vmem((slots * HR, TAPS * mid), BF16),
        z1=vmem((slots, HR, mid), F32),
        slope1=vmem((slots, HR, mid), F32),
        mix1=vmem((slots, HR, mid), BF16),
        z_branch=vmem((slots, HR, out), F32),
        z_short=vmem((slots, HR, out), F32),
        slope2=vmem((slots, HR, out), F32),
        low1=vmem((slots, HR, out), BF16),
        z3=vmem((slots, HR, mid), F32),
        slope3=vmem((slots, HR, mid), F32),
        act2=vmem((slots, HR, mid), BF16),
        z4=vmem((slots, HR, mid), F32),
        slope4=vmem((slots, HR, mid), F32),
        mix2=vmem((slots, HR, mid), BF16),
        z5=vmem((slots, HR, out), F32),
        u_out=vmem((slots, HR, out), F32),
        u_mid=vmem((slots, HR, mid), F32),
        final=vmem((slots, HR, out), BF16),
        g_e2=vmem((slots, HR, out), BF16),
        g_s2=vmem((slots, HR, mid), BF16),
        g_r2=vmem((slots, HR, mid), BF16),
        g_e1=vmem((slots, HR, out), BF16),
        g_p1=vmem((slots, HR, out), BF16),
        g_s1=vmem((slots, HR, mid), BF16),
        g_r1=vmem((slots, FR, mid), BF16),
        h_act1=vmem((1 if gather else 2, micros, FR, mid), BF16),
        h_mix1=vmem((2, micros, HR, mid), BF16),
        h_low1=vmem((2, micros, HR, out), BF16),
        h_act2=vmem((1 if gather else 2, micros, HR, mid), BF16),
        h_mix2=vmem((2, micros, HR, mid), BF16),
        h_image=vmem((2, micros, FR, inw), BF16),
        cuts=vmem((places, 2, 8, 128), F32),
        o_final=vmem((micros, HR, out // narrow), BF16),
        o_input=vmem((micros, FR, inw // narrow), BF16),
        o_norms=vmem((columns, 2, allch // wide), F32),
        o_rms=vmem((columns, 8, mid), F32),
    )
    stat_rows = (3, 2, 2, 2, 2, 2, 2, 2, 2, 2, 2, 2, 2, 1, 2)
    stat_widths = (mid, mid, out, mid, mid, out, out, mid, mid, out, mid, mid, out, out, mid)
    for step in range(STEPS):
        rows, width = stat_rows[step] * slots, stat_widths[step]
        if step in LOW_STEPS:
            scratch["stat%d" % step] = vmem((wide, 16, rows * width // 16), BF16)
        else:
            scratch["stat%d" % step] = vmem((wide, rows, width), F32)
    helper_local = dict(
        raw=vmem((micros, FULL * FULL, inw), BF16),
        pick=vmem((TAPS * HR, FR), BF16),
        h_picked=vmem((2, micros, HR, inw), BF16),
        t_base=vmem((TAPS * HR, HR), F32),
        t_row=vmem((TAPS * HR, HR), F32),
        t_col=vmem((TAPS * HR, HR), F32),
    )
    if gather:
        scratch["sp_act1"] = vmem((places, 2, micros, FR, 128), BF16)
        scratch["sp_act2"] = vmem((places, 2, micros, HR, 128), BF16)
    else:
        helper_local["h_cols"] = vmem((TAPS, 2, micros, HR, mid), BF16)
    for spec in products:
        name, taps, rows, width = spec.name, spec.taps, spec.rows, spec.width
        scratch["h_g_" + name] = vmem((2, micros, spec.cells, width), BF16)
        if spec.gathered:
            scratch["ga_" + name] = vmem((places, 2, micros, HR, width), BF16)
            helper_local["cols_" + name] = vmem((places * 2 * micros * HR, TAPS * 128), BF16)
        else:
            block = (taps, 2 * rows, width)
            if spec.halving:
                scratch["one_" + name] = vmem((2,) + block, BF16)
                scratch["two_" + name] = vmem(block, BF16)
                helper_local["p_" + name] = vmem((2, 2) + block, BF16)
            else:
                scratch["two_" + name] = vmem((places,) + block, BF16)
                helper_local["p_" + name] = vmem((places,) + block, BF16)
        last = (2, rows, width) if taps == 1 else (2, taps, rows, width)
        helper_local["last_" + name] = vmem(last, BF16)
        scratch["d_" + name] = vmem(last[1:], BF16)
    semaphores = dict(
        fetch=(16,),
        stat_send=(STEPS,),
        stat_recv=(STEPS,),
        chain_sends=(7 * columns * narrow + 5 * columns * columns + 2 * slots * narrow + 2 * narrow,),
        helper_sends=(7 * (places + 3) + 3 * places + 16,),
        h_recv=(5,),
        g_recv=(7,),
        y_recv=(7,),
        z_recv=(7,),
        o_recv=(4,),
        w_recv=(7,),
        one_recv=(7,),
        two_recv=(7,),
    )
    for name, shape in semaphores.items():
        scratch[name] = pltpu.SemaphoreType.DMA(shape)
    shared = ("h_", "o_", "sp", "ga", "cu", "on", "tw", "d_")
    chain_local = {name: scratch.pop(name) for name in tuple(scratch)
                   if name not in semaphores and name[:2] not in shared and name[:4] != "stat"}
    chain_local.update(
        raw=vmem((slots, FULL * FULL, inw), BF16),
        image=vmem((slots, FR, inw), BF16),
        picked=vmem((slots * HR, inw), BF16),
        pick=vmem((TAPS * HR, FR), BF16),
        tiles=vmem((slots, TAPS * HR, HR), BF16),
    )
    plan = SimpleNamespace(
        chain_names=tuple(chain_local), chain_local=tuple(chain_local.values()),
        helper_names=tuple(helper_local), helper_local=tuple(helper_local.values()),
        names=tuple(args) + tuple(outputs) + tuple(scratch),
        wide=wide, narrow=narrow, micros=micros, slots=slots,
        mid=mid, out=out, inw=inw, allch=allch,
        gather=gather, layers=tuple(zip(starts, widths)), products=products,
    )
    results = pl.pallas_call(
        functools.partial(kernel, plan),
        out_shape=tuple(jax.ShapeDtypeStruct(s, d) for s, d in outputs.values()),
        in_specs=[spec for _, spec in args.values()],
        out_specs=(in_vmem,) * (len(outputs) - 1) + (in_smem,),
        scratch_shapes=list(scratch.values()),
        compiler_params=pltpu.CompilerParams(
            collective_id=0, has_side_effects=True, vmem_limit_bytes=63 * 2**20 + 2**19
        ),
        name="bottleneck_pair",
    )(*[value for value, _ in args.values()])
    return hand_out(results)


def solution(mesh):
    return jax.shard_map(
        shards,
        mesh=mesh,
        in_specs=(
            P(None, WIDE, None, None),
            P(None, WIDE),
            P(None, WIDE, None),
            P(None, WIDE, None, None),
            P(), P(), P(), P(), P(), P(), P(), P(), P(),
        ),
        out_specs=(
            P(None, WIDE, None, NARROW),
            P(None, WIDE, None, NARROW),
            P(WIDE, NARROW),
            P(None, WIDE, NARROW),
            P(WIDE, NARROW),
            P(WIDE, NARROW),
            P(WIDE, NARROW),
            P(None, WIDE, NARROW),
            P(WIDE, NARROW),
            P((WIDE, NARROW)),
            P((WIDE, NARROW)),
            P(),
        ),
        check_vma=False,
    )
```
